128 devices in a mesh: slab: 8 (over x, core), patch: 16 (over z, y).
Axes of the slice: x: 4, y: 4, z: 4, core: 2. Of those that a mesh axis runs over, the one named last changes fastest.
Arguments:
- coarse: bfloat16 [12, 1024, 4096], P(None, 'slab', 'patch'), may hold values from -6 to 6
- latent: float32 [12, 1024, 4096], P(None, 'slab', 'patch'), may hold values from -6 to 6
- noise_level: float32 [1], replicated, may hold values from 0.3 to 3
- reg_first: bfloat16 [9, 128, 12], replicated, may hold values from -0.625 to 0.625
- reg_second: bfloat16 [9, 12, 128], replicated, may hold values from -0.1875 to 0.1875
- den_first: bfloat16 [9, 128, 24], replicated, may hold values from -0.4375 to 0.4375
- den_middle: bfloat16 [128, 128], replicated, may hold values from -0.5 to 0.5
- den_pool: bfloat16 [128, 128], replicated, may hold values from -2 to 2
- den_last: bfloat16 [9, 12, 128], replicated, may hold values from -0.1875 to 0.1875
- anchors: int32 [8, 16, 2], P('slab'), may hold values from 0 to 3872, as said below
- patch_count: int32 [8], P('slab'), may hold values from 1 to 16, 96 in all
- patch_weight: int32 [224, 224], replicated, may hold values from 1 to 4
Outputs:
- next_state: float32 [12, 1024, 4096], P(None, 'slab', 'patch')
- estimate: float32 [12, 1024, 4096], P(None, 'slab', 'patch')
The draws below stay inside these ranges and needn't reach their ends.
Inputs may be any that keep to these rules, and one draw needn't show every extreme that they name: anchors[s, k] is the top row and left column of patch k of slab s; the row lies between s * 128 - 224 // 2 and s * 128 + 128 - 224 // 2, within 0 to 800; the column lies within 0 to 3872; patch 0 of every slab stands at column 0 and patch 1 at column 3872. Slab s denoises the entries 0 to patch_count[s] - 1 of its table.
All inputs are finite; a program needn't handle non-finite values. No bound on the sum of `patch_count` on one device may be relied on, other than what follows from the above.
Results may differ from the reference program's by a relative error of at most 0.0028.
Values may be sent and summed in bfloat16 or wider, within the bound.
A program may use at most 192 MiB of HBM per device.

```python
import math
import jax
import jax.numpy as jnp
import numpy as np
from jax import lax

ROWS_DEV = 128
PATCH = 224
CHANNELS = 12
INPUTS = 12
REG_WIDTH = 128
DEN_WIDTH = 128
SLABS = 8
PER_SLAB = 16
ROWS = 1024
COLS = 4096
ALL_PATCHES = 96


def draw_anchors(key, part):
    key = jax.random.fold_in(key, 11)
    first_key, second_key = jax.random.split(key)
    slab = jnp.arange(SLABS, dtype=jnp.int32)[:, None]
    offsets = jax.random.randint(first_key, (SLABS, PER_SLAB), -(PATCH // 2), ROWS_DEV - PATCH // 2 + 1)
    top_rows = jnp.clip(slab * ROWS_DEV + offsets, 0, ROWS - PATCH)
    columns = jax.random.randint(second_key, (SLABS, PER_SLAB), 0, COLS - PATCH + 1)
    columns = columns.at[:, 0].set(0).at[:, 1].set(COLS - PATCH)
    return jnp.stack([top_rows, columns], -1).astype(jnp.int32)


def place_ends(entries, own_key, low, high):
    longest = entries.shape.index(max(entries.shape))
    spots = []
    for shift in (0, 1):
        where = [jax.random.randint(jax.random.fold_in(own_key, axis), (), 0, length) for axis, length in enumerate(entries.shape)]
        where[longest] = (where[longest] + shift) % entries.shape[longest]
        spots.append(tuple(where))
    return entries.at[spots[0]].set(low).at[spots[1]].set(high)


def steps_of(key, extent, shards, least, top_value):
    level, own = 1.0, jax.random.fold_in(key, 6)
    for dim, parts in shards:
        steps = jnp.exp(jax.random.uniform(jax.random.fold_in(own, dim), (parts,), jnp.float32, least / len(shards), top_value / len(shards)))
        level = level * jnp.repeat(steps, extent[dim] // parts).reshape([-1 if axis == dim else 1 for axis in range(len(extent))])
    return level


def split_up(amount, total, bound, lean):
    portions = [(1 << 20) // math.isqrt(grade ** lean) + 1 for grade in range(2, amount + 1)]
    spare, given = total - bound - (amount - 1), [1] * (amount - 1)
    while spare > 0:
        free = [i for i in range(amount - 1) if given[i] < bound]
        mass, left = sum([portions[i] for i in free]), spare
        for i in free:
            more = min(bound - given[i], max(1, left * portions[i] // mass), spare)
            given[i] = given[i] + more
            spare = spare - more
    return np.array([bound] + given)


def uneven_parts(rng, amount, total, bound, skew):
    if amount == 2:
        one = jax.random.randint(rng, (), max(1, total - bound), min(bound, total - 1) + 1)
        return jnp.stack([one, total - one])
    lengths = jnp.asarray(split_up(amount, total, bound, skew), jnp.int32)
    twos = (amount - 1) // 2
    giver, taker = lengths[1:1 + 2 * twos:2], lengths[2:2 + 2 * twos:2]
    slack = jnp.minimum(giver - 1, bound - taker)
    shifted = jax.random.randint(jax.random.fold_in(rng, 1), (twos,), 0, 1 << 20) % (slack + 1)
    lengths = lengths.at[1:1 + 2 * twos:2].set(giver - shifted).at[2:2 + 2 * twos:2].set(taker + shifted)
    return lengths[jax.random.permutation(jax.random.fold_in(rng, 2), amount)]


def bell_draw(own_key, dims, width, limit, pieces=(), held_as=jnp.bfloat16):
    factor_of = steps_of(own_key, dims, pieces, -0.22, 0.18) if pieces else 1.0
    result = jax.random.normal(own_key, dims, jnp.float32) * width * factor_of
    return jnp.minimum(jnp.maximum(result, -limit), limit).astype(held_as)


def setup_inputs(seed: int = 0) -> dict:
    key_of = jax.random.split(jax.random.key(seed), 13)
    coarse = bell_draw(key_of[0], (INPUTS, ROWS, COLS), 1.0, 6.0, ((1, 8), (2, 16)))
    latent = bell_draw(key_of[1], (CHANNELS, ROWS, COLS), 1.0, 6.0, ((1, 8), (2, 16)), jnp.float32)
    noise_level = jnp.clip(jnp.exp(jax.random.uniform(key_of[2], (1,), jnp.float32, math.log(0.3), math.log(3.0))), 0.3, 3.0)
    reg_first = bell_draw(key_of[3], (9, REG_WIDTH, INPUTS), (9 * INPUTS) ** -0.5, 0.625)
    reg_second = bell_draw(key_of[4], (9, CHANNELS, REG_WIDTH), (9 * REG_WIDTH) ** -0.5, 0.1875)
    den_first = bell_draw(key_of[5], (9, DEN_WIDTH, 2 * CHANNELS), (18 * CHANNELS) ** -0.5, 0.4375)
    den_middle = bell_draw(key_of[6], (DEN_WIDTH, DEN_WIDTH), DEN_WIDTH ** -0.5, 0.5)
    den_pool = bell_draw(key_of[7], (DEN_WIDTH, DEN_WIDTH), (DEN_WIDTH // 16) ** -0.5, 2.0)
    den_last = bell_draw(key_of[8], (9, CHANNELS, DEN_WIDTH), (9 * DEN_WIDTH) ** -0.5, 0.1875)
    anchors = draw_anchors(jax.random.fold_in(key_of[12], 71), 0)
    patch_count = uneven_parts(key_of[10], SLABS, ALL_PATCHES, PER_SLAB, 2).astype(jnp.int32)
    patch_weight = place_ends(jax.random.randint(key_of[11], (PATCH, PATCH), 1, 5), jax.random.fold_in(key_of[11], 1), 1, 4).astype(jnp.int32)
    return {"coarse": coarse, "latent": latent, "noise_level": noise_level, "reg_first": reg_first, "reg_second": reg_second, "den_first": den_first, "den_middle": den_middle, "den_pool": den_pool, "den_last": den_last, "anchors": anchors, "patch_count": patch_count, "patch_weight": patch_weight}


sigma_data = 0.5
step_ratio = 0.6

def conv_valid(padded, weight, height, breadth):
    channels = padded.shape[0]
    total = None
    for shift_r in range(3):
        for shift_c in range(3):
            piece = padded[:, shift_r:shift_r + height, shift_c:shift_c + breadth].reshape(channels, height * breadth)
            term = jnp.dot(weight[3 * shift_r + shift_c], piece, preferred_element_type=jnp.float32)
            total = term if total is None else total + term
    return total.reshape(weight.shape[1], height, breadth)

def pad_one(field):
    return jnp.pad(field, ((0, 0), (1, 1), (1, 1)))

def denoise(piece, first, middle, pool, last):
    size = piece.shape[1]
    hidden = jax.nn.silu(conv_valid(pad_one(piece), first, size, size)).astype(jnp.bfloat16)
    pooled = lax.optimization_barrier(jnp.sum(hidden.astype(jnp.float32), axis=(1, 2))) / (size * size)
    lift = jnp.dot(pool.astype(jnp.float32), pooled, precision=lax.Precision.HIGHEST)
    inner = jnp.dot(middle, hidden.reshape(hidden.shape[0], size * size), preferred_element_type=jnp.float32)
    inner = jax.nn.silu(inner + lift[:, None]).astype(jnp.bfloat16).reshape(hidden.shape[0], size, size)
    return conv_valid(pad_one(inner), last, size, size)

def precondition(noise_level):
    level = noise_level[0]
    spread = level * level + sigma_data * sigma_data
    return (1.0 / jnp.sqrt(spread), sigma_data * sigma_data / spread, level * sigma_data / jnp.sqrt(spread))

def regression(coarse, reg_first, reg_second):
    inputs, height, breadth = coarse.shape
    framed = jnp.pad(coarse, ((0, 0), (2, 2), (2, 2)))
    col_valid = jnp.arange(breadth + 2, dtype=jnp.int32)
    col_valid = (col_valid >= 1) & (col_valid <= breadth)

    def block(index):
        start = (index * ROWS_DEV).astype(jnp.int32)
        rows = lax.dynamic_slice(framed, (jnp.int32(0), start, jnp.int32(0)), (inputs, ROWS_DEV + 4, breadth + 4))
        hidden = jax.nn.silu(conv_valid(rows, reg_first, ROWS_DEV + 2, breadth + 2))
        global_row = start - 1 + jnp.arange(ROWS_DEV + 2, dtype=jnp.int32)
        row_valid = (global_row >= 0) & (global_row < height)
        inside = row_valid[:, None] & col_valid[None, :]
        hidden = jnp.where(inside[None], hidden, 0.0).astype(jnp.bfloat16)
        return conv_valid(hidden, reg_second, ROWS_DEV, breadth)
    blocks = lax.map(block, jnp.arange(SLABS, dtype=jnp.int32))
    return jnp.transpose(blocks, (1, 0, 2, 3)).reshape(blocks.shape[1], height, breadth)

def reference(coarse, latent, noise_level, reg_first, reg_second, den_first, den_middle, den_pool, den_last, anchors, patch_count, patch_weight):
    height, breadth = (latent.shape[1], latent.shape[2])
    channels = latent.shape[0]
    mean = regression(coarse, reg_first, reg_second)
    scale_in, skip, scale_out = precondition(noise_level)
    condition = jnp.concatenate([(scale_in * latent).astype(jnp.bfloat16), mean.astype(jnp.bfloat16)], 0)
    weight = patch_weight.astype(jnp.float32)
    per_slab = anchors.shape[1]

    def visit(index, totals):
        slab = index // per_slab
        slot = index % per_slab
        row = anchors[slab, slot, 0]
        column = anchors[slab, slot, 1]

        def include(current):
            start = (jnp.int32(0), row, column)
            piece = lax.dynamic_slice(condition, start, (condition.shape[0], PATCH, PATCH))
            output = denoise(piece, den_first, den_middle, den_pool, den_last)
            term = jnp.concatenate([output * weight, weight[None]], 0)
            old = lax.dynamic_slice(current, start, term.shape)
            return lax.dynamic_update_slice(current, old + term, start)

        def leave(current):
            return current
        return lax.cond(slot < patch_count[slab], include, leave, totals)
    totals = lax.fori_loop(0, anchors.shape[0] * per_slab, visit, jnp.zeros((channels + 1, height, breadth), jnp.float32))
    blended = totals[:channels] / (1.0 + totals[channels])
    denoised = skip * latent + scale_out * blended
    next_state = latent + (step_ratio - 1.0) * (latent - denoised)
    return (next_state, mean + denoised)
```

```python
import functools

import jax
import jax.numpy as jnp
from jax import lax
from jax.experimental import pallas as pl
from jax.experimental.pallas import tpu as pltpu
from jax.sharding import PartitionSpec as P

sigma_data = 0.5
step_ratio = 0.6

HALO = 4
STRIDE = 272
GROUP = 8
CHUNK = GROUP * STRIDE
PAD = 384
FRONT = 544
NEG = -1e30
VMEM = 60 * 1024 * 1024
f32, bf16 = jnp.float32, jnp.bfloat16


def silu_half(t):
    return t + t * jnp.tanh(t)


def tap_offsets():
    return [(a - 1) * STRIDE + (b - 1) for a in range(3) for b in range(3)]


def regress_kernel(
    rows, patch, tile_r, tile_c,
    meta, order, tab_r, tab_c,
    coarse, latent, rowi, coli, r0v, c0v, w1, w2, w3, wring,
    first_out, mean_out, part_out, ring_out, strips_out,
    hidden, cond_a, cond_b, cond_c, colmask, sbuf, sem,
):
    chunks = rows // GROUP
    offs = tap_offsets()
    row_lo, row_hi, col_lo, col_hi, number = (meta[0], meta[1], meta[2], meta[3], meta[4])
    hidden[:, :PAD] = jnp.zeros((128, PAD), bf16)
    hidden[:, PAD + chunks * CHUNK :] = jnp.zeros((128, PAD), bf16)
    for ref in (cond_a, cond_b):
        ref[:, :PAD] = jnp.zeros((ref.shape[0], PAD), ref.dtype)
        ref[:, PAD + chunks * CHUNK :] = jnp.zeros((ref.shape[0], PAD), ref.dtype)
    cond_c[:FRONT, :] = jnp.zeros((FRONT, 128), f32)
    cond_c[FRONT + chunks * CHUNK :, :] = jnp.zeros((FRONT, 128), f32)

    @pl.loop(0, chunks)
    def _(k):
        base = pl.multiple_of(k * CHUNK, 128)
        wide = coarse[:, pl.ds(base, CHUNK + 2 * PAD)]
        stack = jnp.concatenate([wide[:, PAD + o : PAD + o + CHUNK] for o in offs], 0)
        t = jnp.dot(w1[...], stack, preferred_element_type=f32)
        row = rowi[...] + k * GROUP
        col = coli[...]
        inside = (row >= row_lo) & (row < row_hi) & (col >= col_lo) & (col < col_hi)
        keep = jnp.where(inside, 1.0, 0.0)[:1]
        hidden[:, pl.ds(base + PAD, CHUNK)] = (silu_half(t) * keep).astype(bf16)

    @pl.loop(0, chunks)
    def _(k):
        base = pl.multiple_of(k * CHUNK, 128)
        y = jnp.dot(w2[...], hidden[:, pl.ds(base, CHUNK + 2 * PAD)], preferred_element_type=f32)
        mean = None
        for t, o in enumerate(offs):
            term = y[16 * t : 16 * t + 16, PAD + o : PAD + o + CHUNK]
            mean = term if mean is None else mean + term
        mean_out[:, pl.ds(base, CHUNK)] = mean
        lat = latent[:, pl.ds(base + PAD, CHUNK)].astype(f32)
        mid = lat[8:] + mean[:8]
        cond_a[:, pl.ds(base + PAD, CHUNK)] = jnp.concatenate([lat[:8], mid], 0).astype(bf16)
        cond_b[:, pl.ds(base + PAD, CHUNK)] = mean[8:]
        full = jnp.concatenate([lat[:8], mid, mean[8:], jnp.zeros((104, CHUNK), f32)], 0)
        for j in range(CHUNK // 128):
            cond_c[pl.ds(base + FRONT + 128 * j, 128), :] = full[:, 128 * j : 128 * j + 128].T

    jcol = lax.broadcasted_iota(jnp.int32, (STRIDE, 128), 0)
    c0b = c0v[...]
    in_cols = (
        (jcol > c0b) & (jcol < c0b + (patch - 1)) & (jcol >= HALO) & (jcol < HALO + tile_c)
    )
    colmask[...] = jnp.where(in_cols, 1.0, 0.0).astype(bf16)
    part_out[...] = jnp.zeros_like(part_out)

    @pl.loop(0, chunks)
    def _(k):
        base = pl.multiple_of(k * CHUNK, 128)
        wa = cond_a[:, pl.ds(base, CHUNK + 2 * PAD)]
        wb = cond_b[:, pl.ds(base, CHUNK + 2 * PAD)]
        parts = [wa[:, PAD + o : PAD + o + CHUNK] for o in offs]
        for a in range(3):
            b8 = [wb[:, PAD + o : PAD + o + CHUNK] for o in offs[3 * a : 3 * a + 3]]
            parts.append(jnp.concatenate([b8[0], b8[1]], 0).astype(bf16))
            parts.append(jnp.concatenate([b8[2], b8[2]], 0).astype(bf16))
        stack = jnp.concatenate(parts, 0)
        t = jnp.dot(w3[...], stack, preferred_element_type=f32)
        first = silu_half(t).astype(bf16)
        first_out[:, pl.ds(base, CHUNK)] = first
        r0b = r0v[...]
        cm = colmask[...]
        masks = []
        for i in range(GROUP):
            row = k * GROUP + i
            keep = (
                (r0b < row) & (row < r0b + (patch - 1)) & (row >= HALO) & (row < HALO + tile_r)
            )
            masks.append(cm * jnp.where(keep, 1.0, 0.0).astype(bf16))
        part_out[...] += jnp.dot(first, jnp.concatenate(masks, 0), preferred_element_type=f32)

    ring_out[...] = jnp.zeros_like(ring_out)

    def strip(start, count, stride, taps, valid_of):
        total = None
        for a, b in taps:
            where = start + (a - 1) * STRIDE + (b - 1)
            if stride == 1:
                cells = cond_c[pl.ds(where, count), :]
            else:
                cells = cond_c[pl.ds(where, count, stride=stride), :]
            cells = jnp.where(valid_of(a, b), cells, 0.0).astype(bf16)
            term = jnp.dot(cells, wring[3 * a + b], preferred_element_type=f32)
            total = term if total is None else total + term
        got = silu_half(total)
        if count % 16:
            got = jnp.concatenate([got, jnp.zeros((16 - count % 16, 128), f32)], 0)
        return got.astype(bf16)

    @pl.loop(0, number)
    def _(n):
        q = order[n]
        r0, c0 = tab_r[q], tab_c[q]
        r1, c1 = r0 + patch - 1, c0 + patch - 1
        j = lax.broadcasted_iota(jnp.int32, (STRIDE, 128), 0)
        i = lax.broadcasted_iota(jnp.int32, (rows, 128), 0)

        def add(value, weight):
            got = jnp.sum(value.astype(f32) * jnp.where(weight, 1.0, 0.0), 0, keepdims=True)
            ring_out[pl.ds(q, 1), :] += got

        for s, (r, height) in enumerate(((r0, (1, 2)), (r1, (0, 1)))):

            @pl.when((r >= HALO - 1) & (r <= HALO + tile_r))
            def _(s=s, r=r, height=height):
                value = strip(
                    FRONT + r * STRIDE, STRIDE, 1,
                    [(a, b) for a in height for b in range(3)],
                    lambda a, b: (j + (b - 1) >= c0) & (j + (b - 1) <= c1),
                )
                sbuf[s, :, :] = value
                own = (r >= HALO) & (r < HALO + tile_r)
                add(value, own & (j >= c0) & (j <= c1) & (j >= HALO) & (j < HALO + tile_c))

        for s, (c, breadth) in enumerate(((c0, (1, 2)), (c1, (0, 1)))):

            @pl.when((c >= HALO - 1) & (c <= HALO + tile_c))
            def _(s=s, c=c, breadth=breadth):
                value = strip(
                    FRONT + c, rows, STRIDE,
                    [(a, b) for a in range(3) for b in breadth],
                    lambda a, b: (i + (a - 1) >= r0) & (i + (a - 1) <= r1),
                )
                sbuf[2 + s, : value.shape[0], :] = value
                own = (c >= HALO) & (c < HALO + tile_c)
                add(value[:rows], own & (i > r0) & (i < r1) & (i >= HALO) & (i < HALO + tile_r))

        copy = pltpu.make_async_copy(sbuf, strips_out.at[n], sem)
        copy.start()
        copy.wait()


def patch_kernel(
    rows, patch, tile_r, tile_c,
    meta, order, tab_r, tab_c,
    first, strips, lift, weight, coli, ones, w4, w5,
    out,
    m, acc, sbuf, keep_row, keep_col, wcol, sem,
):
    chunks = rows // GROUP
    offs = tap_offsets()
    number = meta[4]
    wide = CHUNK + 2 * PAD
    tiles = wide // 128
    m[:FRONT, :] = jnp.zeros((FRONT, 128), f32)
    m[FRONT + chunks * CHUNK :, :] = jnp.zeros((FRONT, 128), f32)

    @pl.loop(0, chunks)
    def _(k):
        base = pl.multiple_of(k * CHUNK, 128)
        x = first[:, pl.ds(base, CHUNK)]
        y = lax.dot_general(x, w4[...], (((0,), (0,)), ((), ())), preferred_element_type=f32)
        m[pl.ds(base + FRONT, CHUNK), :] = y

    acc[...] = jnp.zeros_like(acc)

    @pl.loop(0, number)
    def _(n):
        q = order[n]
        r0, c0 = tab_r[q], tab_c[q]
        r1, c1 = r0 + patch - 1, c0 + patch - 1
        copy = pltpu.make_async_copy(strips.at[n], sbuf, sem)
        copy.start()
        copy.wait()
        half_lift = lift[pl.ds(q, 1), :]
        j = lax.broadcasted_iota(jnp.int32, (STRIDE, 128), 0)
        i = lax.broadcasted_iota(jnp.int32, (rows, 128), 0)

        def row_ok(r):
            return (r >= HALO - 1) & (r <= HALO + tile_r)

        def col_ok(c):
            return (c >= HALO - 1) & (c <= HALO + tile_c)

        def row_at(r):
            return pl.ds(FRONT + r * STRIDE, STRIDE)

        def col_at(c):
            return pl.ds(FRONT + c, rows, stride=STRIDE)

        cols = ((0, c0 - 1, None), (1, c0, 2), (2, c1, 3), (3, c1 + 1, None))
        rws = ((0, r0 - 1, None), (1, r0, 0), (2, r1, 1), (3, r1 + 1, None))
        for s, c, source in cols:

            @pl.when(col_ok(c))
            def _(s=s, c=c, source=source):
                keep_col[s, :, :] = m[col_at(c), :]
                if source is None:
                    m[col_at(c), :] = jnp.full((rows, 128), NEG, f32)
                else:
                    cells = sbuf[source, : -(-rows // 16) * 16, :]
                    got = jnp.dot(cells, w4[...], preferred_element_type=f32)[:rows]
                    m[col_at(c), :] = jnp.where((i >= r0) & (i <= r1), got, NEG)

        for s, r, source in rws:

            @pl.when(row_ok(r))
            def _(s=s, r=r, source=source):
                keep_row[s, :, :] = m[row_at(r), :]
                if source is None:
                    m[row_at(r), :] = jnp.full((STRIDE, 128), NEG, f32)
                else:
                    got = jnp.dot(sbuf[source], w4[...], preferred_element_type=f32)
                    m[row_at(r), :] = jnp.where((j >= c0) & (j <= c1), got, NEG)

        col = coli[...]
        wcol[...] = jnp.where((col >= c0) & (col <= c1), 1.0, 0.0)
        shift = r0 * STRIDE + c0

        @pl.loop(jnp.maximum(r0, HALO - 1) // GROUP, jnp.minimum(r1, HALO + tile_r) // GROUP + 1)
        def _(k):
            base = pl.multiple_of(k * CHUNK, 128)
            t = m[pl.ds(base + FRONT, CHUNK), :] + half_lift
            inner = silu_half(t).astype(bf16)
            y = lax.dot_general(
                w5[...], inner, (((1,), (1,)), ((), ())), preferred_element_type=f32
            )
            total = None
            for t, o in enumerate(offs):
                term = y[16 * t : 16 * t + 16]
                lead = PAD - o
                term = jnp.concatenate(
                    [jnp.zeros((16, lead), f32), term, jnp.zeros((16, wide - lead - CHUNK), f32)], 1
                )
                total = term if total is None else total + term
            lane = base - PAD - shift + WFRONT
            rem = lane % 128
            start = lane // 128
            blocks = weight[pl.ds(start, tiles + 1), :, :].reshape((tiles + 1) * 8, 128)
            rolled = pltpu.roll(blocks, (128 - rem) % 128, 1).reshape(tiles + 1, 8, 128)
            at = lax.broadcasted_iota(jnp.int32, (8, 128), 1)
            w8 = jnp.concatenate(
                [jnp.where(at < 128 - rem, rolled[x], rolled[x + 1]) for x in range(tiles)], 1
            )
            w8 = w8 * wcol[...]
            w16 = jnp.concatenate([w8, w8], 0)
            acc[:, pl.ds(base, wide)] += (total + ones[...]) * w16

        for s, r, source in rws[::-1]:

            @pl.when(row_ok(r))
            def _(s=s, r=r):
                m[row_at(r), :] = keep_row[s, :, :]

        for s, c, source in cols[::-1]:

            @pl.when(col_ok(c))
            def _(s=s, c=c):
                m[col_at(c), :] = keep_col[s, :, :]

    @pl.loop(0, chunks)
    def _(k):
        base = pl.multiple_of(k * CHUNK, 128)
        got = acc[:, pl.ds(base + PAD, CHUNK)]
        out[:, pl.ds(base, CHUNK)] = got / (1.0 + got[12:13])


WFRONT = 4096


def passed(block, axis, step):
    count = lax.axis_size(axis)
    route = [(i, i + step) for i in range(count) if 0 <= i + step < count]
    return lax.ppermute(block, axis, route)


def with_halo(cells, axis, dim, width):
    head = lax.slice_in_dim(cells, 0, width, axis=dim)
    tail = lax.slice_in_dim(cells, cells.shape[dim] - width, cells.shape[dim], axis=dim)
    return jnp.concatenate([passed(tail, axis, 1), cells, passed(head, axis, -1)], axis=dim)


def precondition(noise_level):
    level = noise_level[0]
    spread = level * level + sigma_data * sigma_data
    return (
        1.0 / jnp.sqrt(spread),
        sigma_data * sigma_data / spread,
        level * sigma_data / jnp.sqrt(spread),
    )


def body(
    coarse, latent, noise_level, reg_first, reg_second, den_first, den_middle, den_pool, den_last,
    anchors, patch_count, patch_weight,
):
    channels, tile_r, tile_c = latent.shape
    inputs = coarse.shape[0]
    patch = patch_weight.shape[0]
    rows = tile_r + 2 * HALO
    size = rows * STRIDE
    slab = lax.axis_index("slab")
    column = lax.axis_index("patch")
    scale_in, skip, scale_out = precondition(noise_level)

    both = jnp.concatenate([coarse, (scale_in * latent).astype(bf16)], 0)
    both = with_halo(with_halo(both, "slab", 1, HALO), "patch", 2, HALO)
    both = jnp.pad(both, ((0, 0), (0, 0), (0, STRIDE - both.shape[2])))
    both = both.reshape(inputs + channels, size)
    coarse_flat = jnp.pad(both[:inputs], ((0, 16 - inputs), (PAD, PAD)))
    latent_flat = jnp.pad(both[inputs:], ((0, 16 - channels), (PAD, PAD)))

    table = jnp.concatenate([anchors[0], jnp.broadcast_to(patch_count[:, None], (1, 2))], 0)
    tables = jnp.stack([passed(table, "slab", 1), table, passed(table, "slab", -1)], 0)
    per_slab = anchors.shape[1]
    live = jnp.arange(per_slab)[None, :] < tables[:, per_slab, :1]
    tab_r = tables[:, :per_slab, 0] - slab * tile_r + HALO
    tab_c = tables[:, :per_slab, 1] - column * tile_c + HALO
    live = live & (tab_r < HALO + tile_r) & (tab_r + patch > HALO)
    live = (live & (tab_c < HALO + tile_c) & (tab_c + patch > HALO)).reshape(-1)
    far = 1 << 20
    entries = 3 * per_slab
    tab_r = jnp.where(live, tab_r.reshape(-1), far)
    tab_c = jnp.where(live, tab_c.reshape(-1), far)
    place = jnp.cumsum(live.astype(jnp.int32)) - 1
    number = jnp.sum(live.astype(jnp.int32))
    labels = jnp.arange(entries, dtype=jnp.int32)
    hit = live[None, :] & (place[None, :] == labels[:, None])
    order = jnp.sum(jnp.where(hit, labels[None, :], 0), 1)
    top = HALO - slab * tile_r
    left = HALO - column * tile_c
    meta = jnp.stack(
        [
            top, top + lax.axis_size("slab") * tile_r,
            left, left + lax.axis_size("patch") * tile_c, number,
        ]
    ).astype(jnp.int32)

    w1 = 0.5 * jnp.pad(jnp.transpose(reg_first, (1, 0, 2)), ((0, 0), (0, 0), (0, 16 - inputs)))
    w1 = w1.reshape(128, 144)
    w2 = jnp.pad(reg_second, ((0, 0), (4, 0), (0, 0))).reshape(144, 128)
    den = 0.5 * den_first
    main = jnp.transpose(den[:, :, :16], (1, 0, 2)).reshape(128, 144)
    rest = den[:, :, 16:]
    zero = jnp.zeros_like(rest[0])
    side = []
    for a in range(3):
        side += [rest[3 * a], rest[3 * a + 1], rest[3 * a + 2], zero]
    w3 = jnp.concatenate([main] + side, 1)
    wring = jnp.pad(jnp.transpose(den, (0, 2, 1)), ((0, 0), (0, 128 - 2 * channels), (0, 0)))
    w4 = (0.5 * den_middle).T
    w5 = jnp.pad(den_last, ((0, 0), (0, 4), (0, 0))).reshape(144, 128)

    flat = jnp.arange(CHUNK, dtype=jnp.int32)
    rowi = jnp.broadcast_to(flat // STRIDE, (8, CHUNK))
    coli = jnp.broadcast_to(flat % STRIDE, (8, CHUNK))
    lanes_r = jnp.pad(tab_r, (0, 128 - entries), constant_values=far)[None]
    lanes_c = jnp.pad(tab_c, (0, 128 - entries), constant_values=far)[None]

    smem = pl.BlockSpec(memory_space=pltpu.SMEM)
    vmem = pl.BlockSpec(memory_space=pltpu.VMEM)
    anyw = pl.BlockSpec(memory_space=pl.ANY)
    fixed = (rows, patch, tile_r, tile_c)
    params = pltpu.CompilerParams(vmem_limit_bytes=VMEM)
    first, mean, part, ring, strips = pl.pallas_call(
        functools.partial(regress_kernel, *fixed),
        in_specs=[smem] * 4 + [vmem] * 10,
        out_specs=[vmem, vmem, vmem, vmem, anyw],
        out_shape=[
            jax.ShapeDtypeStruct((128, size), bf16),
            jax.ShapeDtypeStruct((16, size), f32),
            jax.ShapeDtypeStruct((128, 128), f32),
            jax.ShapeDtypeStruct((entries, 128), f32),
            jax.ShapeDtypeStruct((entries, 4, STRIDE, 128), bf16),
        ],
        scratch_shapes=[
            pltpu.VMEM((128, size + 2 * PAD), bf16),
            pltpu.VMEM((16, size + 2 * PAD), bf16),
            pltpu.VMEM((8, size + 2 * PAD), f32),
            pltpu.VMEM((size + 2 * FRONT, 128), f32),
            pltpu.VMEM((STRIDE, 128), bf16),
            pltpu.VMEM((4, STRIDE, 128), bf16),
            pltpu.SemaphoreType.DMA,
        ],
        compiler_params=params,
        name="regress",
    )(
        meta, order, tab_r, tab_c,
        coarse_flat, latent_flat, rowi, coli, lanes_r, lanes_c, w1, w2, w3, wring,
    )

    sums = ring + part[:, :entries].T
    sums = sums + passed(sums, "patch", 1) + passed(sums, "patch", -1)
    sums = sums.reshape(3, per_slab, 128)
    owned = sums[1] + passed(sums[2], "slab", 1) + passed(sums[0], "slab", -1)
    sums = jnp.stack([passed(owned, "slab", 1), owned, passed(owned, "slab", -1)], 0)
    pooled = sums.reshape(entries, 128) / (patch * patch)
    lift = 0.5 * jnp.dot(pooled, den_pool.astype(f32).T, precision=lax.Precision.HIGHEST)

    weight = jnp.pad(patch_weight.astype(f32), ((0, 0), (0, STRIDE - patch))).reshape(-1)
    weight = jnp.pad(weight, (WFRONT, 4096 + 128))
    weight = jnp.broadcast_to(weight.reshape(-1, 1, 128), (weight.shape[0] // 128, 8, 128))
    wide = CHUNK + 2 * PAD
    spot = jnp.arange(wide, dtype=jnp.int32)
    coli_wide = jnp.broadcast_to((spot - PAD + 2 * STRIDE) % STRIDE, (8, wide))
    ones = jnp.where(
        (jnp.arange(16)[:, None] >= 12) & (spot[None] >= PAD) & (spot[None] < PAD + CHUNK), 1.0, 0.0
    )
    blended = pl.pallas_call(
        functools.partial(patch_kernel, *fixed),
        in_specs=[smem] * 4 + [vmem, anyw] + [vmem] * 6,
        out_specs=vmem,
        out_shape=jax.ShapeDtypeStruct((16, size), f32),
        scratch_shapes=[
            pltpu.VMEM((size + 2 * FRONT, 128), f32),
            pltpu.VMEM((16, size + 2 * PAD), f32),
            pltpu.VMEM((4, STRIDE, 128), bf16),
            pltpu.VMEM((4, STRIDE, 128), f32),
            pltpu.VMEM((4, rows, 128), f32),
            pltpu.VMEM((8, wide), f32),
            pltpu.SemaphoreType.DMA,
        ],
        compiler_params=params,
        name="patches",
    )(
        meta, order, tab_r, tab_c,
        first, strips, lift, weight, coli_wide, ones, w4, w5,
    )

    def tile_of(flat):
        return flat.reshape(-1, rows, STRIDE)[:, HALO : HALO + tile_r, HALO : HALO + tile_c]

    blended = tile_of(blended[:channels])
    mean = tile_of(mean[4:])
    denoised = skip * latent + scale_out * blended
    next_state = latent + (step_ratio - 1.0) * (latent - denoised)
    return (next_state, mean + denoised)


def solution(mesh):
    return jax.shard_map(
        body,
        mesh=mesh,
        in_specs=(
            P(None, "slab", "patch"), P(None, "slab", "patch"),
            P(), P(), P(), P(), P(), P(), P(),
            P("slab", None, None), P("slab"), P(),
        ),
        out_specs=(P(None, "slab", "patch"), P(None, "slab", "patch")),
        check_vma=False,
    )
```

```python
import functools

import jax
import jax.numpy as jnp
from jax import lax
from jax.experimental import pallas as pl
from jax.experimental.pallas import tpu as pltpu
from jax.sharding import PartitionSpec as P

sigma_data = 0.5
step_ratio = 0.6

HALO = 4
STRIDE = 272
PLANES = 8
PAD = 384
FRONT = 544
STEP = 256
TILE = 512
COLUMN = 24
NEG = -1e30
VMEM = 60 * 1024 * 1024
f32, bf16 = jnp.float32, jnp.bfloat16


def lanes_of(rows):
    return -(-(rows // PLANES * STRIDE) // STEP) * STEP


def silu_half(t):
    return t + t * jnp.tanh(t)


def shifted(ref, base, step, depth):
    at = base + PAD
    edge = STRIDE // 128 * 128
    rest = STRIDE - edge
    mid = ref[:, pl.ds(at - 128, step + 256)]
    low = ref[(PLANES - 1) * depth :, pl.ds(at - edge - 128, step + 256)]
    high = ref[:depth, pl.ds(at + edge - 128, step + 256)]
    out = []
    for b in range(3):
        m = mid[:, 127 + b : 127 + b + step]
        rows = [low[:, 127 + b - rest : 127 + b - rest + step]]
        rows += [m[depth * i : depth * i + depth] for i in range(PLANES)]
        rows += [high[:, 127 + b + rest : 127 + b + rest + step]]
        out.append(rows)
    return out


def overlapped(parts):
    got = [parts[0][:96]]
    for a, b in zip(parts, parts[1:]):
        got.append(a[96:] + b[:96])
    return got + [parts[-1][96:]]


def combined(ref, base, step):
    at = base + PAD
    edge = STRIDE // 128 * 128
    rest = STRIDE - edge

    def columns(plane, start, move):
        total = None
        for b in range(3):
            row = (plane + 1) * 48 + b * 16
            block = ref[row : row + 16, pl.ds(start - 128, step + 256)]
            term = block[:, 127 + b + move : 127 + b + move + step]
            total = term if total is None else total + term
        return total

    planes = [columns(i, at, 0) for i in range(PLANES)]
    planes[-1] += columns(-1, at + edge, rest)
    planes[0] += columns(PLANES, at - edge, -rest)
    return planes


def regress_kernel(
    rows, patch, tile_r, tile_c,
    meta, order, tab_r, tab_c,
    coarse, latent, rowi, coli, r0v, c0v, w1, w2, w3, wrow, wcol,
    first_out, mean_out, part_out, ring_out, strips_out,
    sums, cond_a, cond_b, cond_c, sbuf, sem,
):
    size = lanes_of(rows)
    steps = size // STEP
    cells = size + 2 * FRONT
    groups = rows // PLANES
    row_lo, row_hi, col_lo, col_hi, number = (meta[0], meta[1], meta[2], meta[3], meta[4])
    for ref in (sums, cond_a, cond_b):
        ref[:, :PAD] = jnp.zeros((ref.shape[0], PAD), ref.dtype)
        ref[:, PAD + size :] = jnp.zeros((ref.shape[0], PAD), ref.dtype)
    cond_c[:FRONT, :] = jnp.zeros((FRONT, 128), f32)
    cond_c[FRONT + size : 2 * FRONT + size, :] = jnp.zeros((FRONT, 128), f32)
    cond_c[cells : cells + FRONT, :] = jnp.zeros((FRONT, 128), f32)
    cond_c[cells + FRONT + size :, :] = jnp.zeros((cond_c.shape[0] - cells - FRONT - size, 128), f32)

    @pl.loop(0, steps, unroll=4)
    def _(k):
        base = pl.multiple_of(k * STEP, 128)
        x = shifted(coarse, base, STEP, 16)
        row = rowi[:, pl.ds(base, STEP)]
        col = coli[:, pl.ds(base, STEP)]
        inside = (row >= row_lo) & (row < row_hi) & (col >= col_lo) & (col < col_hi)
        keep = jnp.where(inside, 1.0, 0.0)
        parts = []
        for pair in range(PLANES // 2):
            stack = jnp.concatenate(
                [x[b][2 * pair + r] for r in range(4) for b in range(3)], 0
            )
            h = silu_half(jnp.dot(w1[...], stack, preferred_element_type=f32))
            h = jnp.concatenate(
                [
                    h[:128] * keep[2 * pair : 2 * pair + 1],
                    h[128:] * keep[2 * pair + 1 : 2 * pair + 2],
                ],
                0,
            ).astype(bf16)
            parts.append(jnp.dot(w2[...], h, preferred_element_type=f32))
        sums[:, pl.ds(base + PAD, STEP)] = jnp.concatenate(overlapped(parts), 0)

    @pl.loop(0, steps, unroll=4)
    def _(k):
        base = pl.multiple_of(k * STEP, 128)
        means = combined(sums, base, STEP)
        lat = latent[:, pl.ds(base + PAD, STEP)].astype(f32)
        zero = jnp.zeros((8, STEP), f32)
        main, side, full = [], [], []
        for i, mean in enumerate(means):
            head = lat[16 * i : 16 * i + 8]
            mid = lat[16 * i + 8 : 16 * i + 16] + mean[:8]
            main += [head, mid]
            side.append(mean[8:])
            full += [head, mid, mean[8:], zero]
        mean_out[:, pl.ds(base, STEP)] = jnp.concatenate(means, 0)
        cond_a[:, pl.ds(base + PAD, STEP)] = jnp.concatenate(main, 0).astype(bf16)
        cond_b[:, pl.ds(base + PAD, STEP)] = jnp.concatenate(side, 0)
        for h in range(2):
            block = jnp.concatenate(full[16 * h : 16 * h + 16], 0)
            for j in range(STEP // 128):
                cond_c[pl.ds(base + h * cells + FRONT + 128 * j, 128), :] = block[
                    :, 128 * j : 128 * j + 128
                ].T

    part_out[...] = jnp.zeros_like(part_out)

    @pl.loop(0, steps, unroll=4)
    def _(k):
        base = pl.multiple_of(k * STEP, 128)
        xa = shifted(cond_a, base, STEP, 16)
        xb = shifted(cond_b, base, STEP, 8)
        left = [
            jnp.concatenate([xb[0][i], xb[1][i]], 0).astype(bf16) for i in range(PLANES + 2)
        ]
        right = [
            jnp.concatenate([xb[2][i], xb[2][min(i + 1, PLANES + 1)]], 0).astype(bf16)
            for i in range(PLANES + 2)
        ]
        group = base // STRIDE
        lane = lax.broadcasted_iota(jnp.int32, (STEP, 128), 0)
        split = (group + 1) * STRIDE - base
        later = lane >= split
        col = lane + base - group * STRIDE - jnp.where(later, STRIDE, 0)
        c0b, r0b = c0v[...], r0v[...]
        wanted = (
            (col > c0b) & (col < c0b + (patch - 1)) & (col >= HALO) & (col < HALO + tile_c)
        )
        now = jnp.where(wanted & (lane < split), 1.0, 0.0).astype(bf16)
        late = jnp.where(wanted & later, 1.0, 0.0).astype(bf16)

        def row_keep(row):
            keep = (
                (r0b < row) & (row < r0b + (patch - 1)) & (row >= HALO) & (row < HALO + tile_r)
            )
            return jnp.where(keep, 1.0, 0.0).astype(bf16)

        masks, firsts = [], []
        for i in range(PLANES):
            stack = jnp.concatenate(
                [xa[b][i + a] for a in range(3) for b in range(3)]
                + [left[i], left[i + 1], left[i + 2], right[i], right[i + 2]],
                0,
            )
            first = silu_half(jnp.dot(w3[...], stack, preferred_element_type=f32)).astype(bf16)
            first_out[128 * i : 128 * i + 128, pl.ds(base, STEP)] = first
            firsts.append(first)
            row = group * PLANES + i
            masks.append(now * row_keep(row) + late * row_keep(row + PLANES))
        part_out[...] += jnp.dot(
            jnp.concatenate(firsts, 1), jnp.concatenate(masks, 0), preferred_element_type=f32
        )

    ring_out[...] = jnp.zeros_like(ring_out)
    j = lax.broadcasted_iota(jnp.int32, (STRIDE, 128), 0)
    g = lax.broadcasted_iota(jnp.int32, (COLUMN, 128), 0)
    i = jnp.concatenate([g * PLANES + p for p in range(PLANES)], 0)
    live = jnp.concatenate([g < groups for p in range(PLANES)], 0)

    @pl.loop(0, number)
    def _(n):
        q = order[n]
        r0, c0 = tab_r[q], tab_c[q]
        r1, c1 = r0 + patch - 1, c0 + patch - 1

        def add(value, weight):
            got = jnp.sum(jnp.where(weight, value.astype(f32), 0.0), 0, keepdims=True)
            ring_out[pl.ds(q, 1), :] += got

        for s, (r, height) in enumerate(((r0, (1, 2)), (r1, (0, 1)))):

            @pl.when((r >= HALO - 1) & (r <= HALO + tile_r))
            def _(s=s, r=r, height=height):
                total = None
                for a in height:
                    at = r + a - 1
                    plane = at % PLANES
                    start = plane // 4 * cells + FRONT + at // PLANES * STRIDE
                    for b in range(3):
                        x = cond_c[pl.ds(start + b - 1, STRIDE), :]
                        x = jnp.where((j + (b - 1) >= c0) & (j + (b - 1) <= c1), x, 0.0)
                        term = jnp.dot(
                            x.astype(bf16), wrow[plane % 4, 3 * a + b], preferred_element_type=f32
                        )
                        total = term if total is None else total + term
                value = silu_half(total).astype(bf16)
                sbuf[STRIDE * s : STRIDE * s + STRIDE, :] = value
                own = (r >= HALO) & (r < HALO + tile_r)
                add(value, own & (j >= c0) & (j <= c1) & (j >= HALO) & (j < HALO + tile_c))

        for s, (c, breadth) in enumerate(((c0, (1, 2)), (c1, (0, 1)))):

            @pl.when((c >= HALO - 1) & (c <= HALO + tile_c))
            def _(s=s, c=c, breadth=breadth):
                total = None
                for b in breadth:

                    def at(h, g_move, b=b):
                        start = h * cells + FRONT + c + b - 1 + g_move * STRIDE
                        return cond_c[pl.ds(start, COLUMN, stride=STRIDE), :]

                    halves = [at(0, 0), at(1, 0)]
                    planes = [at(1, -1)[:, 96:]]
                    planes += [
                        halves[p // 4][:, p % 4 * 32 : p % 4 * 32 + 32] for p in range(PLANES)
                    ]
                    planes += [at(0, 1)[:, :32]]
                    for a in range(3):
                        x = jnp.concatenate(planes[a : a + PLANES], 0)
                        inside = (i + (a - 1) >= r0) & (i + (a - 1) <= r1)
                        x = jnp.where(inside[:, :32], x, 0.0).astype(bf16)
                        term = jnp.dot(x, wcol[3 * a + b], preferred_element_type=f32)
                        total = term if total is None else total + term
                value = silu_half(total).astype(bf16)
                lo = 2 * STRIDE + PLANES * COLUMN * s
                sbuf[lo : lo + PLANES * COLUMN, :] = value
                own = (c >= HALO) & (c < HALO + tile_c) & live
                add(value, own & (i > r0) & (i < r1) & (i >= HALO) & (i < HALO + tile_r))

        copy = pltpu.make_async_copy(sbuf, strips_out.at[n], sem)
        copy.start()
        copy.wait()


def patch_kernel(
    rows, patch, tile_r, tile_c,
    meta, order, tab_r, tab_c,
    first, strips, lift, weight, w4, w5,
    out,
    m, acc, sbuf, keep_row, keep_col, wbuf, sem,
):
    size = lanes_of(rows)
    steps = size // STEP
    groups = rows // PLANES
    number = meta[4]
    high = 2 * STRIDE
    tall = PLANES * COLUMN

    def fetch(n):
        return pltpu.make_async_copy(strips.at[n], sbuf.at[n % 2], sem.at[n % 2])

    @pl.when(number > 0)
    def _():
        fetch(0).start()

    @pl.loop(0, steps, unroll=2)
    def _(k):
        base = pl.multiple_of(k * STEP, 128)
        for i in range(PLANES):
            x = first[128 * i : 128 * i + 128, pl.ds(base, STEP)]
            y = lax.dot_general(x, w4[...], (((0,), (0,)), ((), ())), preferred_element_type=f32)
            m[pl.ds(base + i * size, STEP), :] = y

    acc[...] = jnp.zeros_like(acc)
    m[PLANES * size :, :] = jnp.zeros((TILE, 128), f32)
    j = lax.broadcasted_iota(jnp.int32, (STRIDE, 128), 0)
    g = lax.broadcasted_iota(jnp.int32, (COLUMN, 128), 0)
    lane = lax.broadcasted_iota(jnp.int32, (8, TILE), 1)
    ones = jnp.where(lax.broadcasted_iota(jnp.int32, (16, TILE), 0) >= 12, 1.0, 0.0)

    @pl.loop(0, number)
    def _(n):
        q = order[n]
        r0, c0 = tab_r[q], tab_c[q]
        r1, c1 = r0 + patch - 1, c0 + patch - 1
        slot = n % 2
        fetch(n).wait()

        @pl.when(n + 1 < number)
        def _():
            fetch(n + 1).start()

        half_lift = lift[pl.ds(q, 1), :]

        def row_ok(r):
            return (r >= HALO - 1) & (r <= HALO + tile_r)

        def col_ok(c):
            return (c >= HALO - 1) & (c <= HALO + tile_c)

        def row_at(r):
            return pl.ds(pl.multiple_of(r % PLANES * size + r // PLANES * STRIDE, 8), STRIDE)

        def col_at(c, i):
            return pl.ds(c + i * size, groups, stride=STRIDE)

        cols = ((0, c0 - 1, None), (1, c0, 0), (2, c1, 1), (3, c1 + 1, None))
        rws = ((0, r0 - 1, None), (1, r0, 0), (2, r1, 1), (3, r1 + 1, None))
        for s, c, source in cols:

            @pl.when(col_ok(c))
            def _(s=s, c=c, source=source):
                if source is not None:
                    strip = sbuf[slot, high + tall * source : high + tall * source + tall, :]
                    got = jnp.dot(strip, w4[...], preferred_element_type=f32)
                for i in range(PLANES):
                    keep_col[s, i, :groups, :] = m[col_at(c, i), :]
                    if source is None:
                        new = jnp.full((groups, 128), NEG, f32)
                    else:
                        row = g * PLANES + i
                        new = got[COLUMN * i : COLUMN * i + COLUMN]
                        new = jnp.where((row >= r0) & (row <= r1), new, NEG)[:groups]
                    m[col_at(c, i), :] = new

        for s, r, source in rws:

            @pl.when(row_ok(r))
            def _(s=s, r=r, source=source):
                keep_row[s, :, :] = m[row_at(r), :]
                if source is None:
                    m[row_at(r), :] = jnp.full((STRIDE, 128), NEG, f32)
                else:
                    strip = sbuf[slot, STRIDE * source : STRIDE * source + STRIDE, :]
                    got = jnp.dot(strip, w4[...], preferred_element_type=f32)
                    m[row_at(r), :] = jnp.where((j >= c0) & (j <= c1), got, NEG)

        top = r0 // PLANES
        phase = r0 - top * PLANES
        move = top * STRIDE + c0
        shifts = (move, move + STRIDE, jnp.where(phase == 0, move - STRIDE, move))
        clo, chi = jnp.maximum(c0, HALO - 1), jnp.minimum(c1, HALO + tile_c)
        glo = jnp.maximum(r0, HALO - 1) // PLANES
        ghi = jnp.minimum(r1, HALO + tile_r) // PLANES

        @pl.loop((glo * STRIDE + clo) // TILE, (ghi * STRIDE + chi) // TILE + 1)
        def _(k):
            base = pl.multiple_of(k * TILE, 128)
            col_start = base % STRIDE
            col = lane + col_start
            for _ in range((TILE + STRIDE - 2) // STRIDE):
                col = jnp.where(col >= STRIDE, col - STRIDE, col)
            for b in range(3):
                inside = (col - (b - 1) >= c0) & (col - (b - 1) <= c1)
                for v, shift in enumerate(shifts):
                    source = base - shift - (b - 1) + WFRONT
                    rem = source % 128
                    count = TILE // 128
                    blocks = weight[pl.ds(source // 128, count + 1), :, :]
                    blocks = blocks.reshape(8 * count + 8, 128)
                    rolled = pltpu.roll(blocks, (128 - rem) % 128, 1)
                    here = lane[:, :128] < 128 - rem
                    got = jnp.concatenate(
                        [
                            jnp.where(here, rolled[8 * x : 8 * x + 8], rolled[8 * x + 8 : 8 * x + 16])
                            for x in range(count)
                        ],
                        1,
                    )
                    wbuf[8 * (3 * v + b) : 8 * (3 * v + b) + 8, :] = jnp.where(inside, got, 0.0)
            pairs = []
            for pair in range(PLANES // 2):
                halves = []
                for i in (2 * pair, 2 * pair + 1):
                    t = m[pl.ds(base + i * size, TILE), :] + half_lift
                    halves.append(silu_half(t).astype(bf16))
                pairs.append(jnp.concatenate(halves, 1))
            y = lax.dot_general(
                w5[...], jnp.concatenate(pairs, 0), (((1,), (1,)), ((), ())),
                preferred_element_type=f32,
            )
            parts = overlapped([y[:, TILE * x : TILE * x + TILE] for x in range(PLANES // 2)])
            for i in range(-1, PLANES + 1):
                block = parts[(i + 1) // 2][(i + 1) % 2 * 48 : (i + 1) % 2 * 48 + 48]
                if i < 0:
                    version = 1
                elif i == PLANES:
                    version = 2
                else:
                    version = jnp.where(phase <= i, 0, 1)
                line = (i - phase) % PLANES
                for b in range(3):
                    term = block[16 * b : 16 * b + 16]
                    if b == 1 and 0 <= i < PLANES:
                        term = term + ones
                    w = wbuf[pl.ds(8 * (3 * version + b) + line, 1), :]
                    row = 48 * (i + 1) + 16 * b
                    acc[row : row + 16, pl.ds(base + PAD, TILE)] += term * w

        for s, r, source in rws[::-1]:

            @pl.when(row_ok(r))
            def _(s=s, r=r):
                m[row_at(r), :] = keep_row[s, :, :]

        for s, c, source in cols[::-1]:

            @pl.when(col_ok(c))
            def _(s=s, c=c):
                for i in range(PLANES):
                    m[col_at(c, i), :] = keep_col[s, i, :groups, :]

    @pl.loop(0, steps)
    def _(k):
        base = pl.multiple_of(k * STEP, 128)
        planes = combined(acc, base, STEP)
        out[:, pl.ds(base, STEP)] = jnp.concatenate([p / (1.0 + p[12:13]) for p in planes], 0)


WFRONT = 2048


def passed(block, axis, step):
    count = lax.axis_size(axis)
    route = [(i, i + step) for i in range(count) if 0 <= i + step < count]
    return lax.ppermute(block, axis, route)


def with_halo(cells, axis, dim, width):
    head = lax.slice_in_dim(cells, 0, width, axis=dim)
    tail = lax.slice_in_dim(cells, cells.shape[dim] - width, cells.shape[dim], axis=dim)
    return jnp.concatenate([passed(tail, axis, 1), cells, passed(head, axis, -1)], axis=dim)


def precondition(noise_level):
    level = noise_level[0]
    spread = level * level + sigma_data * sigma_data
    return (
        1.0 / jnp.sqrt(spread),
        sigma_data * sigma_data / spread,
        level * sigma_data / jnp.sqrt(spread),
    )


def specs():
    return (
        pl.BlockSpec(memory_space=pltpu.SMEM),
        pl.BlockSpec(memory_space=pltpu.VMEM),
        pl.BlockSpec(memory_space=pl.ANY),
    )


def run_regress(fixed, entries, *args):
    size = lanes_of(fixed[0])
    smem, vmem, anyw = specs()
    cells = size + 2 * FRONT
    return pl.pallas_call(
        functools.partial(regress_kernel, *fixed),
        in_specs=[smem] * 4 + [vmem] * 11,
        out_specs=[vmem, vmem, vmem, vmem, anyw],
        out_shape=[
            jax.ShapeDtypeStruct((PLANES * 128, size), bf16),
            jax.ShapeDtypeStruct((PLANES * 16, size), f32),
            jax.ShapeDtypeStruct((128, 128), f32),
            jax.ShapeDtypeStruct((entries, 128), f32),
            jax.ShapeDtypeStruct((entries, 2 * (STRIDE + PLANES * COLUMN), 128), bf16),
        ],
        scratch_shapes=[
            pltpu.VMEM((48 * (PLANES + 2), size + 2 * PAD), f32),
            pltpu.VMEM((16 * PLANES, size + 2 * PAD), bf16),
            pltpu.VMEM((8 * PLANES, size + 2 * PAD), f32),
            pltpu.VMEM((2 * cells + COLUMN * STRIDE - size + STRIDE, 128), f32),
            pltpu.VMEM((2 * (STRIDE + PLANES * COLUMN), 128), bf16),
            pltpu.SemaphoreType.DMA,
        ],
        compiler_params=pltpu.CompilerParams(vmem_limit_bytes=VMEM),
        name="regress",
    )(*args)


def run_patches(fixed, *args):
    rows = fixed[0]
    size = lanes_of(rows)
    smem, vmem, anyw = specs()
    return pl.pallas_call(
        functools.partial(patch_kernel, *fixed),
        in_specs=[smem] * 4 + [vmem, anyw] + [vmem] * 4,
        out_specs=vmem,
        out_shape=jax.ShapeDtypeStruct((PLANES * 16, size), f32),
        scratch_shapes=[
            pltpu.VMEM((PLANES * size + TILE, 128), f32),
            pltpu.VMEM((48 * (PLANES + 2), size + 2 * PAD), f32),
            pltpu.VMEM((2, 2 * (STRIDE + PLANES * COLUMN), 128), bf16),
            pltpu.VMEM((4, STRIDE, 128), f32),
            pltpu.VMEM((4, PLANES, COLUMN, 128), f32),
            pltpu.VMEM((72, TILE), f32),
            pltpu.SemaphoreType.DMA((2,)),
        ],
        compiler_params=pltpu.CompilerParams(vmem_limit_bytes=VMEM),
        name="patches",
    )(*args)


NEAR = [(di, dj) for di in range(-2, 3) for dj in range(-1, 2) if (di, dj) != (0, 0)]
MESH = pl.DeviceIdType.MESH


def neighbours(near, shape):
    me = (lax.axis_index("slab"), lax.axis_index("patch"))
    out = []
    for offset in near:
        at = tuple(a + d for a, d in zip(me, offset))
        there = (at[0] >= 0) & (at[0] < shape[0]) & (at[1] >= 0) & (at[1] < shape[1])
        out.append((there, at))
    return out


def greet(around):
    barrier = pltpu.get_barrier_semaphore()
    for there, at in around:

        @pl.when(there)
        def _(at=at):
            pl.semaphore_signal(barrier, inc=1, device_id=at, device_id_type=MESH)

    peers = jnp.int32(0)
    for there, at in around:
        peers = peers + there.astype(jnp.int32)
    pl.semaphore_wait(barrier, peers)


def pool_kernel(shape, per_slab, cells, part, ring, pool, lift, mine, got, send, recv):
    around = neighbours(NEAR, shape)
    greet(around)
    mine[...] = ring[...] + part[...].T[: 3 * per_slab]
    copies = []
    for x, (there, at) in enumerate(around):
        copy = pltpu.make_async_remote_copy(
            src_ref=mine, dst_ref=got.at[len(NEAR) - 1 - x],
            send_sem=send.at[x], recv_sem=recv.at[len(NEAR) - 1 - x],
            device_id=at, device_id_type=MESH,
        )
        copies.append(copy)

        @pl.when(there)
        def _(copy=copy):
            copy.start()

    lift[...] = mine[...]
    for x, (there, at) in enumerate(around):
        di = NEAR[x][0]

        @pl.when(there)
        def _(x=x, di=di):
            copies[len(NEAR) - 1 - x].wait_recv()
            for d in range(3):
                e = d - di
                if 0 <= e < 3:
                    lift[per_slab * d : per_slab * d + per_slab, :] += got[
                        x, per_slab * e : per_slab * e + per_slab, :
                    ]

    for x, (there, at) in enumerate(around):

        @pl.when(there)
        def _(x=x):
            copies[x].wait_send()

    lift[...] = 0.5 * lax.dot_general(
        lift[...] / cells, pool[...], (((1,), (1,)), ((), ())),
        precision=lax.Precision.HIGHEST, preferred_element_type=f32,
    )


def run_pool(shape, per_slab, cells, *args):
    vmem = specs()[1]
    entries = 3 * per_slab
    return pl.pallas_call(
        functools.partial(pool_kernel, shape, per_slab, cells),
        in_specs=[vmem] * 3,
        out_specs=vmem,
        out_shape=jax.ShapeDtypeStruct((entries, 128), f32),
        scratch_shapes=[
            pltpu.VMEM((entries, 128), f32),
            pltpu.VMEM((len(NEAR), entries, 128), f32),
            pltpu.SemaphoreType.DMA((len(NEAR),)),
            pltpu.SemaphoreType.DMA((len(NEAR),)),
        ],
        compiler_params=pltpu.CompilerParams(collective_id=1, has_side_effects=True),
        name="pool",
    )(*args)


def body(
    coarse, latent, noise_level, reg_first, reg_second, den_first, den_middle, den_pool, den_last,
    anchors, patch_count, patch_weight,
):
    channels, tile_r, tile_c = latent.shape
    inputs = coarse.shape[0]
    patch = patch_weight.shape[0]
    rows = tile_r + 2 * HALO
    size = lanes_of(rows)
    groups = rows // PLANES
    used = groups * STRIDE
    slab = lax.axis_index("slab")
    column = lax.axis_index("patch")
    scale_in, skip, scale_out = precondition(noise_level)

    both = jnp.concatenate([coarse, (scale_in * latent).astype(bf16)], 0)
    both = with_halo(with_halo(both, "slab", 1, HALO), "patch", 2, HALO)
    both = jnp.pad(both, ((0, 0), (0, 0), (0, STRIDE - both.shape[2])))
    both = both.reshape(inputs + channels, groups, PLANES, STRIDE).transpose(2, 0, 1, 3)
    both = both.reshape(PLANES, inputs + channels, used)

    def planes_of(part):
        part = jnp.pad(part, ((0, 0), (0, 16 - part.shape[1]), (PAD, PAD + size - used)))
        return part.reshape(PLANES * 16, size + 2 * PAD)

    coarse_flat = planes_of(both[:, :inputs])
    latent_flat = planes_of(both[:, inputs:])

    table = jnp.concatenate([anchors[0], jnp.broadcast_to(patch_count[:, None], (1, 2))], 0)
    tables = jnp.stack([passed(table, "slab", 1), table, passed(table, "slab", -1)], 0)
    per_slab = anchors.shape[1]
    live = jnp.arange(per_slab)[None, :] < tables[:, per_slab, :1]
    tab_r = tables[:, :per_slab, 0] - slab * tile_r + HALO
    tab_c = tables[:, :per_slab, 1] - column * tile_c + HALO
    live = live & (tab_r < HALO + tile_r) & (tab_r + patch > HALO)
    live = (live & (tab_c < HALO + tile_c) & (tab_c + patch > HALO)).reshape(-1)
    far = 1 << 20
    entries = 3 * per_slab
    tab_r = jnp.where(live, tab_r.reshape(-1), far)
    tab_c = jnp.where(live, tab_c.reshape(-1), far)
    place = jnp.cumsum(live.astype(jnp.int32)) - 1
    number = jnp.sum(live.astype(jnp.int32))
    labels = jnp.arange(entries, dtype=jnp.int32)
    hit = live[None, :] & (place[None, :] == labels[:, None])
    order = jnp.sum(jnp.where(hit, labels[None, :], 0), 1)
    top = HALO - slab * tile_r
    left = HALO - column * tile_c
    meta = jnp.stack(
        [
            top, top + lax.axis_size("slab") * tile_r,
            left, left + lax.axis_size("patch") * tile_c, number,
        ]
    ).astype(jnp.int32)

    def gather_pair(weight):
        taps = jnp.pad(jnp.transpose(weight, (1, 0, 2)), ((0, 0), (0, 0), (0, 16 - weight.shape[2])))
        taps = taps.reshape(128, 144)
        return jnp.concatenate(
            [jnp.pad(taps, ((0, 0), (0, 48))), jnp.pad(taps, ((0, 0), (48, 0)))], 0
        )

    def spread_pair(weight, front):
        taps = jnp.pad(weight, ((0, 0), (front, 16 - front - weight.shape[1]), (0, 0)))
        taps = taps.reshape(3, 48, 128)[::-1].reshape(144, 128)
        return jnp.concatenate(
            [jnp.pad(taps, ((0, 48), (0, 0))), jnp.pad(taps, ((48, 0), (0, 0)))], 1
        )

    w1 = gather_pair(0.5 * reg_first)
    w2 = spread_pair(reg_second, 4)
    den = 0.5 * den_first
    main = jnp.transpose(den[:, :, :16], (1, 0, 2)).reshape(128, 144)
    rest = den[:, :, 16:]
    side = [rest[t] for t in (0, 1, 3, 4, 6, 7, 2, 5, 8)] + [jnp.zeros_like(rest[0])]
    w3 = jnp.concatenate([main] + side, 1)
    wcol = jnp.pad(jnp.transpose(den, (0, 2, 1)), ((0, 0), (0, 32 - 2 * channels), (0, 0)))
    wrow = jnp.stack([jnp.pad(wcol, ((0, 0), (32 * u, 96 - 32 * u), (0, 0))) for u in range(4)], 0)
    w4 = (0.5 * den_middle).T
    w5 = spread_pair(den_last, 0)

    flat = jnp.arange(size, dtype=jnp.int32)
    rowi = PLANES * (flat // STRIDE)[None] + jnp.arange(PLANES, dtype=jnp.int32)[:, None]
    coli = jnp.broadcast_to(flat % STRIDE, (PLANES, size))
    lanes_r = jnp.pad(tab_r, (0, 128 - entries), constant_values=far)[None]
    lanes_c = jnp.pad(tab_c, (0, 128 - entries), constant_values=far)[None]

    fixed = (rows, patch, tile_r, tile_c)
    first, mean, part, ring, strips = run_regress(
        fixed, entries,
        meta, order, tab_r, tab_c,
        coarse_flat, latent_flat, rowi, coli, lanes_r, lanes_c, w1, w2, w3, wrow, wcol,
    )

    shape = (lax.axis_size("slab"), lax.axis_size("patch"))
    lift = run_pool(shape, per_slab, patch * patch, part, ring, den_pool.astype(f32))

    weight = jnp.pad(patch_weight.astype(f32), ((0, 0), (0, STRIDE - patch)))
    weight = weight.reshape(patch // PLANES, PLANES, STRIDE).transpose(1, 0, 2)
    weight = weight.reshape(PLANES, patch // PLANES * STRIDE)
    end = -weight.shape[1] % 128
    weight = jnp.pad(weight, ((0, 0), (WFRONT, end + WFRONT)))
    weight = weight.reshape(PLANES, -1, 128).transpose(1, 0, 2)
    blended = run_patches(
        fixed, meta, order, tab_r, tab_c, first, strips, lift, weight, w4, w5
    )

    def tile_of(flat):
        planes = flat.reshape(PLANES, 16, size)[:, :, :used].reshape(PLANES, 16, groups, STRIDE)
        whole = planes.transpose(1, 2, 0, 3).reshape(16, rows, STRIDE)
        return whole[:, HALO : HALO + tile_r, HALO : HALO + tile_c]

    blended = tile_of(blended)[:channels]
    mean = tile_of(mean)[4:]
    denoised = skip * latent + scale_out * blended
    next_state = latent + (step_ratio - 1.0) * (latent - denoised)
    return (next_state, mean + denoised)


def solution(mesh):
    return jax.shard_map(
        body,
        mesh=mesh,
        in_specs=(
            P(None, "slab", "patch"), P(None, "slab", "patch"),
            P(), P(), P(), P(), P(), P(), P(),
            P("slab", None, None), P("slab"), P(),
        ),
        out_specs=(P(None, "slab", "patch"), P(None, "slab", "patch")),
        check_vma=False,
    )
```

```python
import functools

import jax
import jax.numpy as jnp
import numpy as np
from jax import lax
from jax.experimental import pallas as pl
from jax.experimental.pallas import tpu as pltpu
from jax.sharding import PartitionSpec as P

sigma_data = 0.5
step_ratio = 0.6

HALO = 4
TOP = 8
STRIDE = 264
STRIP = 272
PLANES = 8
PAD = 384
FRONT = 528
STEP = 256
TILE = 512
COLUMN = 24
NEG = -1e30
VMEM = 60 * 1024 * 1024
f32, bf16 = jnp.float32, jnp.bfloat16


def lanes_of(rows):
    return -(-(rows // PLANES * STRIDE) // STEP) * STEP


def silu_half(t):
    return t + t * jnp.tanh(t)


def shifted(ref, base, step, depth):
    at = base + PAD
    edge = STRIDE // 128 * 128
    rest = STRIDE - edge
    mid = ref[:, pl.ds(at - 128, step + 256)]
    low = ref[(PLANES - 1) * depth :, pl.ds(at - edge - 128, step + 256)]
    high = ref[:depth, pl.ds(at + edge - 128, step + 256)]
    out = []
    for b in range(3):
        m = mid[:, 127 + b : 127 + b + step]
        rows = [low[:, 127 + b - rest : 127 + b - rest + step]]
        rows += [m[depth * i : depth * i + depth] for i in range(PLANES)]
        rows += [high[:, 127 + b + rest : 127 + b + rest + step]]
        out.append(rows)
    return out


def overlapped(parts):
    got = [parts[0][:96]]
    for a, b in zip(parts, parts[1:]):
        got.append(a[96:] + b[:96])
    return got + [parts[-1][96:]]


def combined(ref, base, step):
    at = base + PAD
    edge = STRIDE // 128 * 128
    rest = STRIDE - edge

    def columns(plane, start, move):
        total = None
        for b in range(3):
            row = (plane + 1) * 48 + b * 16
            block = ref[row : row + 16, pl.ds(start - 128, step + 256)]
            term = block[:, 127 + b + move : 127 + b + move + step]
            total = term if total is None else total + term
        return total

    planes = [columns(i, at, 0) for i in range(PLANES)]
    planes[-1] += columns(-1, at + edge, rest)
    planes[0] += columns(PLANES, at - edge, -rest)
    return planes


def gather_pair(raw, out):
    zero = jnp.zeros((128, 16 - raw.shape[2]), bf16)
    parts = []
    for t in range(9):
        parts += [raw[t] * 0.5, zero]
    gap = jnp.zeros((128, 48), bf16)
    out[:128, :] = jnp.concatenate(parts + [gap], 1)
    out[128:, :] = jnp.concatenate([gap] + parts, 1)


def spread_pair(raw, out, front):
    zeros = [jnp.zeros((n, 128), f32) for n in (front, 16 - front - raw.shape[1]) if n]
    parts = []
    for a in (2, 1, 0):
        for b in range(3):
            taps = raw[3 * a + b].astype(f32)
            parts += [zeros[0], taps] if front else [taps, zeros[0]]
    gap = jnp.zeros((48, 128), f32)
    out[:, :128] = jnp.concatenate(parts + [gap], 0).astype(bf16)
    out[:, 128:] = jnp.concatenate([gap] + parts, 0).astype(bf16)


def regress_kernel(
    rows, patch, tile_r, tile_c,
    meta, tabs, coarse, latent, rowi, coli, tabs_v, raw1, raw2, raw3,
    first_out, mean_out, part_out, ring_out, strips_out, order,
    w1, w2, w3, sums, cond_a, cond_b, cond_c, sbuf, sem,
):
    size = lanes_of(rows)
    steps = size // STEP
    cells = size + 2 * FRONT
    groups = rows // PLANES
    row_lo, row_hi, col_lo, col_hi = meta[0], meta[1], meta[2], meta[3]
    gather_pair(raw1, w1)
    spread_pair(raw2, w2, 4)
    zero8 = jnp.zeros((128, 8), bf16)
    w3[...] = 0.5 * jnp.concatenate(
        [raw3[t][:, :16] for t in range(9)]
        + [raw3[t][:, 16:] for t in (0, 1, 3, 4, 6, 7, 2, 5, 8)] + [zero8], 1
    )

    def enlist(q, n):
        live = tabs[0, q] < FAR

        @pl.when(live)
        def _():
            order[n] = q

        return n + live.astype(jnp.int32)

    entries = ring_out.shape[0]
    number = lax.fori_loop(0, entries, enlist, jnp.int32(0))
    order[entries] = number
    for ref in (sums, cond_a, cond_b):
        ref[:, :PAD] = jnp.zeros((ref.shape[0], PAD), ref.dtype)
        ref[:, PAD + size :] = jnp.zeros((ref.shape[0], PAD), ref.dtype)
    cond_c[:FRONT, :] = jnp.zeros((FRONT, 128), f32)
    cond_c[FRONT + size : 2 * FRONT + size, :] = jnp.zeros((FRONT, 128), f32)
    cond_c[cells : cells + FRONT, :] = jnp.zeros((FRONT, 128), f32)
    cond_c[cells + FRONT + size :, :] = jnp.zeros((cond_c.shape[0] - cells - FRONT - size, 128), f32)

    @pl.loop(0, steps, unroll=4)
    def _(k):
        base = pl.multiple_of(k * STEP, 128)
        x = shifted(coarse, base, STEP, 16)
        row = rowi[:, pl.ds(base, STEP)]
        col = coli[:, pl.ds(base, STEP)]
        inside = (row >= row_lo) & (row < row_hi) & (col >= col_lo) & (col < col_hi)
        keep = jnp.where(inside, 1.0, 0.0)
        parts = []
        for pair in range(PLANES // 2):
            stack = jnp.concatenate(
                [x[b][2 * pair + r] for r in range(4) for b in range(3)], 0
            )
            h = silu_half(jnp.dot(w1[...], stack, preferred_element_type=f32))
            h = jnp.concatenate(
                [
                    h[:128] * keep[2 * pair : 2 * pair + 1],
                    h[128:] * keep[2 * pair + 1 : 2 * pair + 2],
                ],
                0,
            ).astype(bf16)
            parts.append(jnp.dot(w2[...], h, preferred_element_type=f32))
        sums[:, pl.ds(base + PAD, STEP)] = jnp.concatenate(overlapped(parts), 0)

    @pl.loop(0, steps, unroll=4)
    def _(k):
        base = pl.multiple_of(k * STEP, 128)
        means = combined(sums, base, STEP)
        lat = latent[:, pl.ds(base + PAD, STEP)].astype(f32)
        zero = jnp.zeros((8, STEP), f32)
        main, side, full = [], [], []
        for i, mean in enumerate(means):
            head = lat[16 * i : 16 * i + 8]
            mid = lat[16 * i + 8 : 16 * i + 16] + mean[:8]
            main += [head, mid]
            side.append(mean[8:])
            full += [head, mid, mean[8:], zero]
        mean_out[:, pl.ds(base, STEP)] = jnp.concatenate(means, 0)
        cond_a[:, pl.ds(base + PAD, STEP)] = jnp.concatenate(main, 0).astype(bf16)
        cond_b[:, pl.ds(base + PAD, STEP)] = jnp.concatenate(side, 0)
        for h in range(2):
            block = jnp.concatenate(full[16 * h : 16 * h + 16], 0)
            for j in range(STEP // 128):
                cond_c[pl.ds(base + h * cells + FRONT + 128 * j, 128), :] = block[
                    :, 128 * j : 128 * j + 128
                ].T

    part_out[...] = jnp.zeros_like(part_out)

    @pl.loop(0, steps, unroll=4)
    def _(k):
        base = pl.multiple_of(k * STEP, 128)
        xa = shifted(cond_a, base, STEP, 16)
        xb = shifted(cond_b, base, STEP, 8)
        left = [
            jnp.concatenate([xb[0][i], xb[1][i]], 0).astype(bf16) for i in range(PLANES + 2)
        ]
        right = [
            jnp.concatenate([xb[2][i], xb[2][min(i + 1, PLANES + 1)]], 0).astype(bf16)
            for i in range(PLANES + 2)
        ]
        group = base // STRIDE
        lane = lax.broadcasted_iota(jnp.int32, (STEP, 128), 0)
        split = (group + 1) * STRIDE - base
        later = lane >= split
        col = lane + base - group * STRIDE - jnp.where(later, STRIDE, 0)
        r0b, c0b = tabs_v[:1], tabs_v[1:2]
        wanted = (
            (col > c0b) & (col < c0b + (patch - 1)) & (col >= HALO) & (col < HALO + tile_c)
        )
        now = jnp.where(wanted & (lane < split), 1.0, 0.0).astype(bf16)
        late = jnp.where(wanted & later, 1.0, 0.0).astype(bf16)

        def row_keep(row):
            keep = (
                (r0b < row) & (row < r0b + (patch - 1)) & (row >= TOP) & (row < TOP + tile_r)
            )
            return jnp.where(keep, 1.0, 0.0).astype(bf16)

        masks, firsts = [], []
        for i in range(PLANES):
            stack = jnp.concatenate(
                [xa[b][i + a] for a in range(3) for b in range(3)]
                + [left[i], left[i + 1], left[i + 2], right[i], right[i + 2]],
                0,
            )
            first = silu_half(jnp.dot(w3[...], stack, preferred_element_type=f32)).astype(bf16)
            first_out[128 * i : 128 * i + 128, pl.ds(base, STEP)] = first
            firsts.append(first)
            row = group * PLANES + i
            masks.append(now * row_keep(row) + late * row_keep(row + PLANES))
        part_out[...] += jnp.dot(
            jnp.concatenate(firsts, 1), jnp.concatenate(masks, 0), preferred_element_type=f32
        )

    ring_out[...] = jnp.zeros_like(ring_out)
    j = lax.broadcasted_iota(jnp.int32, (STRIDE, 128), 0)
    g = lax.broadcasted_iota(jnp.int32, (COLUMN, 128), 0)
    i = jnp.concatenate([g * PLANES + p for p in range(PLANES)], 0)
    live = jnp.concatenate([g < groups for p in range(PLANES)], 0)

    @pl.loop(0, number)
    def _(n):
        q = order[n]
        r0, c0 = tabs[0, q], tabs[1, q]
        r1, c1 = r0 + patch - 1, c0 + patch - 1

        def add(value, weight):
            got = jnp.sum(jnp.where(weight, value.astype(f32), 0.0), 0, keepdims=True)
            ring_out[pl.ds(q, 1), :] += got

        for s, (r, height) in enumerate(((r0, (1, 2)), (r1, (0, 1)))):

            @pl.when((r >= TOP - 1) & (r <= TOP + tile_r))
            def _(s=s, r=r, height=height):
                total = None
                for a in height:
                    at = r + a - 1
                    plane = at % PLANES
                    start = plane // 4 * cells + FRONT + at // PLANES * STRIDE
                    for b in range(3):
                        x = cond_c[pl.ds(start + b - 1, STRIDE), :]
                        x = jnp.where((j + (b - 1) >= c0) & (j + (b - 1) <= c1), x, 0.0)
                        x = pltpu.roll(x, (128 - plane % 4 * 32) % 128, 1)[:, :24].astype(bf16)
                        term = lax.dot_general(
                            x, raw3[3 * a + b], (((1,), (1,)), ((), ())), preferred_element_type=f32
                        )
                        total = term if total is None else total + term
                value = silu_half(0.5 * total)
                tail = jnp.zeros((STRIP - STRIDE, 128), f32)
                sbuf[STRIP * s : STRIP * s + STRIP, :] = jnp.concatenate([value, tail], 0).astype(bf16)
                value = value.astype(bf16)
                own = (r >= TOP) & (r < TOP + tile_r)
                add(value, own & (j >= c0) & (j <= c1) & (j >= HALO) & (j < HALO + tile_c))

        for s, (c, breadth) in enumerate(((c0, (1, 2)), (c1, (0, 1)))):

            @pl.when((c >= HALO - 1) & (c <= HALO + tile_c))
            def _(s=s, c=c, breadth=breadth):
                total = None
                for b in breadth:

                    def at(h, g_move, b=b):
                        start = h * cells + FRONT + c + b - 1 + g_move * STRIDE
                        return cond_c[pl.ds(start, COLUMN, stride=STRIDE), :]

                    halves = [at(0, 0), at(1, 0)]
                    planes = [at(1, -1)[:, 96:]]
                    planes += [
                        halves[p // 4][:, p % 4 * 32 : p % 4 * 32 + 32] for p in range(PLANES)
                    ]
                    planes += [at(0, 1)[:, :32]]
                    for a in range(3):
                        x = jnp.concatenate(planes[a : a + PLANES], 0)
                        inside = (i + (a - 1) >= r0) & (i + (a - 1) <= r1)
                        x = jnp.where(inside[:, :32], x, 0.0)[:, :24].astype(bf16)
                        term = lax.dot_general(
                            x, raw3[3 * a + b], (((1,), (1,)), ((), ())), preferred_element_type=f32
                        )
                        total = term if total is None else total + term
                value = silu_half(0.5 * total).astype(bf16)
                lo = 2 * STRIP + PLANES * COLUMN * s
                sbuf[lo : lo + PLANES * COLUMN, :] = value
                own = (c >= HALO) & (c < HALO + tile_c) & live
                add(value, own & (i > r0) & (i < r1) & (i >= TOP) & (i < TOP + tile_r))

        copy = pltpu.make_async_copy(sbuf, strips_out.at[n], sem)
        copy.start()
        copy.wait()


def patch_kernel(
    rows, patch, tile_r, tile_c,
    order, tabs, noise, first, strips, lift, weight, mean, latent, middle, raw5,
    next_out, est_out,
    w5, m, acc, sbuf, keep_row, keep_col, wbuf, sem,
):
    size = lanes_of(rows)
    steps = size // STEP
    groups = rows // PLANES
    number = order[lift.shape[0]]
    spread_pair(raw5, w5, 0)

    def mixed(x, dim):
        return 0.5 * lax.dot_general(
            x, middle[...], (((dim,), (1,)), ((), ())), preferred_element_type=f32
        )
    high = 2 * STRIP
    tall = PLANES * COLUMN

    def fetch(n):
        return pltpu.make_async_copy(strips.at[n], sbuf.at[n % 2], sem.at[n % 2])

    @pl.when(number > 0)
    def _():
        fetch(0).start()

    @pl.loop(0, steps, unroll=2)
    def _(k):
        base = pl.multiple_of(k * STEP, 128)
        for i in range(PLANES):
            x = first[128 * i : 128 * i + 128, pl.ds(base, STEP)]
            m[pl.ds(base + i * size, STEP), :] = mixed(x, 0)

    acc[...] = jnp.zeros_like(acc)
    m[PLANES * size :, :] = jnp.zeros((TILE, 128), f32)
    j = lax.broadcasted_iota(jnp.int32, (STRIDE, 128), 0)
    g = lax.broadcasted_iota(jnp.int32, (COLUMN, 128), 0)
    lane = lax.broadcasted_iota(jnp.int32, (8, TILE), 1)
    ones = jnp.where(lax.broadcasted_iota(jnp.int32, (16, TILE), 0) >= 12, 1.0, 0.0)

    @pl.loop(0, number)
    def _(n):
        q = order[n]
        r0, c0 = tabs[0, q], tabs[1, q]
        r1, c1 = r0 + patch - 1, c0 + patch - 1
        slot = n % 2
        fetch(n).wait()

        @pl.when(n + 1 < number)
        def _():
            fetch(n + 1).start()

        half_lift = lift[pl.ds(q, 1), :]

        def row_ok(r):
            return (r >= TOP - 1) & (r <= TOP + tile_r)

        def col_ok(c):
            return (c >= HALO - 1) & (c <= HALO + tile_c)

        def row_at(r):
            return pl.ds(pl.multiple_of(r % PLANES * size + r // PLANES * STRIDE, 8), STRIDE)

        def col_at(c, i):
            return pl.ds(c + i * size, groups, stride=STRIDE)

        cols = ((0, c0 - 1, None), (1, c0, 0), (2, c1, 1), (3, c1 + 1, None))
        rws = ((0, r0 - 1, None), (1, r0, 0), (2, r1, 1), (3, r1 + 1, None))
        for s, c, source in cols:

            @pl.when(col_ok(c))
            def _(s=s, c=c, source=source):
                if source is not None:
                    strip = sbuf[slot, high + tall * source : high + tall * source + tall, :]
                    got = mixed(strip, 1)
                for i in range(PLANES):
                    keep_col[s, i, :groups, :] = m[col_at(c, i), :]
                    if source is None:
                        new = jnp.full((groups, 128), NEG, f32)
                    else:
                        row = g * PLANES + i
                        new = got[COLUMN * i : COLUMN * i + COLUMN]
                        new = jnp.where((row >= r0) & (row <= r1), new, NEG)[:groups]
                    m[col_at(c, i), :] = new

        for s, r, source in rws:

            @pl.when(row_ok(r))
            def _(s=s, r=r, source=source):
                keep_row[s, :, :] = m[row_at(r), :]
                if source is None:
                    m[row_at(r), :] = jnp.full((STRIDE, 128), NEG, f32)
                else:
                    strip = sbuf[slot, STRIP * source : STRIP * source + STRIP, :]
                    got = mixed(strip, 1)[:STRIDE]
                    m[row_at(r), :] = jnp.where((j >= c0) & (j <= c1), got, NEG)

        top = r0 // PLANES
        phase = r0 - top * PLANES
        move = top * STRIDE + c0
        shifts = (move, move + STRIDE, jnp.where(phase == 0, move - STRIDE, move))
        clo, chi = jnp.maximum(c0, HALO - 1), jnp.minimum(c1, HALO + tile_c)
        glo = jnp.maximum(r0, TOP - 1) // PLANES
        ghi = jnp.minimum(r1, TOP + tile_r) // PLANES

        @pl.loop((glo * STRIDE + clo) // TILE, (ghi * STRIDE + chi) // TILE + 1)
        def _(k):
            base = pl.multiple_of(k * TILE, 128)
            col_start = base % STRIDE
            col = lane + col_start
            for _ in range((TILE + STRIDE - 2) // STRIDE):
                col = jnp.where(col >= STRIDE, col - STRIDE, col)
            for b in range(3):
                inside = (col - (b - 1) >= c0) & (col - (b - 1) <= c1)
                for v, shift in enumerate(shifts):
                    source = base - shift - (b - 1) + WFRONT
                    rem = source % 128
                    count = TILE // 128
                    blocks = weight[pl.ds(source // 128, count + 1), :, :]
                    blocks = blocks.reshape(8 * count + 8, 128)
                    rolled = pltpu.roll(blocks, (128 - rem) % 128, 1)
                    here = lane[:, :128] < 128 - rem
                    got = jnp.concatenate(
                        [
                            jnp.where(here, rolled[8 * x : 8 * x + 8], rolled[8 * x + 8 : 8 * x + 16])
                            for x in range(count)
                        ],
                        1,
                    )
                    wbuf[8 * (3 * v + b) : 8 * (3 * v + b) + 8, :] = jnp.where(inside, got, 0.0)
            pairs = []
            for pair in range(PLANES // 2):
                halves = []
                for i in (2 * pair, 2 * pair + 1):
                    t = m[pl.ds(base + i * size, TILE), :] + half_lift
                    halves.append(silu_half(t).astype(bf16))
                pairs.append(jnp.concatenate(halves, 1))
            y = lax.dot_general(
                w5[...], jnp.concatenate(pairs, 0), (((1,), (1,)), ((), ())),
                preferred_element_type=f32,
            )
            parts = overlapped([y[:, TILE * x : TILE * x + TILE] for x in range(PLANES // 2)])
            for i in range(-1, PLANES + 1):
                block = parts[(i + 1) // 2][(i + 1) % 2 * 48 : (i + 1) % 2 * 48 + 48]
                if i < 0:
                    version = 1
                elif i == PLANES:
                    version = 2
                else:
                    version = jnp.where(phase <= i, 0, 1)
                line = (i - phase) % PLANES
                for b in range(3):
                    term = block[16 * b : 16 * b + 16]
                    if b == 1 and 0 <= i < PLANES:
                        term = term + ones
                    w = wbuf[pl.ds(8 * (3 * version + b) + line, 1), :]
                    row = 48 * (i + 1) + 16 * b
                    acc[row : row + 16, pl.ds(base + PAD, TILE)] += term * w

        for s, r, source in rws[::-1]:

            @pl.when(row_ok(r))
            def _(s=s, r=r):
                m[row_at(r), :] = keep_row[s, :, :]

        for s, c, source in cols[::-1]:

            @pl.when(col_ok(c))
            def _(s=s, c=c):
                for i in range(PLANES):
                    m[col_at(c, i), :] = keep_col[s, i, :groups, :]

    for k in range(tile_r // PLANES):
        start = (k + TOP // PLANES) * STRIDE + HALO
        whole = start // 128 * 128
        off = start - whole
        span = -(-(off + tile_c) // 128) * 128
        planes = combined(acc, whole, span)
        got = jnp.stack([p / (1.0 + p[12:13]) for p in planes], 0)[:, :, off : off + tile_c]
        got = jnp.swapaxes(got, 0, 1)[:12]
        base = mean[:, whole : whole + span].reshape(PLANES, 16, span)[:, :, off : off + tile_c]
        base = jnp.swapaxes(base, 0, 1)[4:]
        rows_at = slice(PLANES * k, PLANES * k + PLANES)
        scale_in, skip, scale_out = precondition(noise)
        lat = latent[:, rows_at, :]
        denoised = skip * lat + scale_out * got
        next_out[:, rows_at, :] = lat + (step_ratio - 1.0) * (lat - denoised)
        est_out[:, rows_at, :] = base + denoised


FAR = 1 << 20
WFRONT = 2048


def precondition(noise):
    level = jnp.full((1, 1, 1), noise[0], f32)
    spread = level * level + sigma_data * sigma_data
    root = jnp.sqrt(spread)
    return 1.0 / root, sigma_data * sigma_data / spread, level * sigma_data / root


def specs():
    return (
        pl.BlockSpec(memory_space=pltpu.SMEM),
        pl.BlockSpec(memory_space=pltpu.VMEM),
        pl.BlockSpec(memory_space=pl.ANY),
    )


def run_regress(fixed, entries, *args):
    size = lanes_of(fixed[0])
    smem, vmem, anyw = specs()
    cells = size + 2 * FRONT
    return pl.pallas_call(
        functools.partial(regress_kernel, *fixed),
        in_specs=[smem] * 2 + [vmem] * 8,
        out_specs=[vmem, vmem, vmem, vmem, anyw, smem],
        out_shape=[
            jax.ShapeDtypeStruct((PLANES * 128, size), bf16),
            jax.ShapeDtypeStruct((PLANES * 16, size), f32),
            jax.ShapeDtypeStruct((128, 128), f32),
            jax.ShapeDtypeStruct((entries, 128), f32),
            jax.ShapeDtypeStruct((entries, 2 * (STRIP + PLANES * COLUMN), 128), bf16),
            jax.ShapeDtypeStruct((entries + 1,), jnp.int32),
        ],
        scratch_shapes=[
            pltpu.VMEM((256, 192), bf16),
            pltpu.VMEM((192, 256), bf16),
            pltpu.VMEM((128, 224), bf16),
            pltpu.VMEM((48 * (PLANES + 2), size + 2 * PAD), f32),
            pltpu.VMEM((16 * PLANES, size + 2 * PAD), bf16),
            pltpu.VMEM((8 * PLANES, size + 2 * PAD), f32),
            pltpu.VMEM((2 * cells + COLUMN * STRIDE - size + STRIDE, 128), f32),
            pltpu.VMEM((2 * (STRIP + PLANES * COLUMN), 128), bf16),
            pltpu.SemaphoreType.DMA,
        ],
        compiler_params=pltpu.CompilerParams(vmem_limit_bytes=VMEM),
        name="regress",
    )(*args)


def run_patches(fixed, *args):
    rows = fixed[0]
    size = lanes_of(rows)
    smem, vmem, anyw = specs()
    return pl.pallas_call(
        functools.partial(patch_kernel, *fixed),
        in_specs=[smem] * 3 + [vmem, anyw] + [vmem] * 6,
        out_specs=[vmem] * 2,
        out_shape=[jax.ShapeDtypeStruct((12, fixed[2], fixed[3]), f32)] * 2,
        scratch_shapes=[
            pltpu.VMEM((192, 256), bf16),
            pltpu.VMEM((PLANES * size + TILE, 128), f32),
            pltpu.VMEM((48 * (PLANES + 2), size + 2 * PAD), f32),
            pltpu.VMEM((2, 2 * (STRIP + PLANES * COLUMN), 128), bf16),
            pltpu.VMEM((4, STRIDE, 128), f32),
            pltpu.VMEM((4, PLANES, COLUMN, 128), f32),
            pltpu.VMEM((72, TILE), f32),
            pltpu.SemaphoreType.DMA((2,)),
        ],
        compiler_params=pltpu.CompilerParams(vmem_limit_bytes=VMEM),
        name="patches",
    )(*args)


NEAR = [(di, dj) for di in range(-2, 3) for dj in range(-1, 2) if (di, dj) != (0, 0)]
MESH = pl.DeviceIdType.MESH


def neighbours(near, shape):
    me = (lax.axis_index("slab"), lax.axis_index("patch"))
    out = []
    for offset in near:
        at = tuple(a + d for a, d in zip(me, offset))
        there = (at[0] >= 0) & (at[0] < shape[0]) & (at[1] >= 0) & (at[1] < shape[1])
        out.append((there, at))
    return out


def greet(around):
    barrier = pltpu.get_barrier_semaphore()
    for there, at in around:

        @pl.when(there)
        def _(at=at):
            pl.semaphore_signal(barrier, inc=1, device_id=at, device_id_type=MESH)

    peers = jnp.int32(0)
    for there, at in around:
        peers = peers + there.astype(jnp.int32)
    pl.semaphore_wait(barrier, peers)


def pool_kernel(shape, per_slab, cells, part, ring, pool, lift, mine, got, send, recv):
    around = neighbours(NEAR, shape)
    greet(around)
    mine[...] = ring[...] + part[...].T[: 3 * per_slab]
    copies = []
    for x, (there, at) in enumerate(around):
        copy = pltpu.make_async_remote_copy(
            src_ref=mine, dst_ref=got.at[len(NEAR) - 1 - x],
            send_sem=send.at[x], recv_sem=recv.at[len(NEAR) - 1 - x],
            device_id=at, device_id_type=MESH,
        )
        copies.append(copy)

        @pl.when(there)
        def _(copy=copy):
            copy.start()

    lift[...] = mine[...]
    for x, (there, at) in enumerate(around):
        di = NEAR[x][0]

        @pl.when(there)
        def _(x=x, di=di):
            copies[len(NEAR) - 1 - x].wait_recv()
            for d in range(3):
                e = d - di
                if 0 <= e < 3:
                    lift[per_slab * d : per_slab * d + per_slab, :] += got[
                        x, per_slab * e : per_slab * e + per_slab, :
                    ]

    for x, (there, at) in enumerate(around):

        @pl.when(there)
        def _(x=x):
            copies[x].wait_send()

    lift[...] = 0.5 * lax.dot_general(
        lift[...] / cells, pool[...].astype(f32), (((1,), (1,)), ((), ())),
        precision=lax.Precision.HIGHEST, preferred_element_type=f32,
    )


SIDES = [(-1, 0), (1, 0), (0, -1), (0, 1), (-1, -1), (-1, 1), (1, -1), (1, 1)]


def frame_kernel(
    shape, per_slab, patch,
    noise, coarse, latent, table, move, ends, back,
    coarse_out, latent_out, tabs_out,
    both, framed, edge_rows, edge_cols, corners, strip, tables, send, recv,
):
    channels, tile_r, tile_c = latent.shape
    around = neighbours(SIDES, shape)
    there = [a[0] for a in around]
    scale_in = precondition(noise)[0]
    both[:channels, :, :] = coarse[...]
    both[channels:, :, :] = (scale_in * latent[...]).astype(bf16)
    greet(around)

    def last(d):
        return slice(0, 16) if d < 0 else slice(tile_r - 16, tile_r)

    def side(d):
        return slice(0, 128) if d < 0 else slice(tile_c - 128, tile_c)

    opposite = [SIDES.index((-a, -b)) for a, b in SIDES]
    copies = []

    def copy(x, source, target, slot):
        here = opposite[x]
        return pltpu.make_async_remote_copy(
            src_ref=source, dst_ref=target, send_sem=send.at[slot, x], recv_sem=recv.at[slot, here],
            device_id=around[x][1], device_id_type=MESH,
        )

    def begin(x, one):
        copies.append((x, one))

        @pl.when(there[x])
        def _():
            one.start()

    for x in (0, 1):
        begin(x, copy(x, both.at[:, last(SIDES[x][0]), :], edge_rows.at[opposite[x]], 0))
        begin(x, copy(x, table, tables.at[opposite[x]], 1))
    for x in range(4, 8):
        di, dj = SIDES[x]
        begin(x, copy(x, both.at[:, last(di), side(dj)], corners.at[opposite[x] - 4], 0))
    flat = both[...].reshape(2 * channels * tile_r, tile_c)
    strip[...] = lax.dot_general(
        ends[...], flat, (((1,), (1,)), ((), ())), preferred_element_type=f32
    )
    for x in (2, 3):
        begin(x, copy(x, strip, edge_cols.at[opposite[x] - 2], 0))

    @pl.loop(0, 2 * channels)
    def _(c):
        x = jnp.dot(both[c], move[...], preferred_element_type=f32)
        framed[c + c // channels * (16 - channels), TOP : TOP + tile_r, :] = x

    for x in range(8):

        @pl.when(jnp.logical_not(there[x]))
        def _(x=x):
            if x < 2:
                edge_rows[x] = jnp.zeros(edge_rows.shape[1:], bf16)
                tables[x] = jnp.zeros(tables.shape[1:], jnp.int32)
            elif x < 4:
                edge_cols[x - 2] = jnp.zeros(edge_cols.shape[1:], f32)
            else:
                corners[x - 4] = jnp.zeros(corners.shape[1:], bf16)

    for x, one in copies:

        @pl.when(there[x])
        def _(one=one):
            one.wait_send()

    for x, one in copies:

        @pl.when(there[opposite[x]])
        def _(one=one):
            one.wait_recv()

    for c in range(2 * channels):
        at = c + c // channels * (16 - channels)
        cols = jnp.concatenate(
            [edge_cols[x][:, tile_r * c : tile_r * c + tile_r] for x in range(2)], 0
        ).astype(bf16)
        framed[at, TOP : TOP + tile_r, :] += lax.dot_general(
            cols, back[256:272, :], (((0,), (0,)), ((), ())), preferred_element_type=f32
        )
        for x, rows_at in ((0, slice(0, TOP)), (1, slice(TOP + tile_r, 2 * TOP + tile_r))):
            x4 = 4 + 2 * x
            got = jnp.dot(edge_rows[x, c], move[...], preferred_element_type=f32)
            got += jnp.dot(corners[x4 - 4, c], back[:128, :], preferred_element_type=f32)
            got += jnp.dot(corners[x4 - 3, c], back[128:256, :], preferred_element_type=f32)
            framed[at, rows_at, :] = got[16 - TOP :] if x == 0 else got[:TOP]
    zero = jnp.zeros((16 - channels, tile_r + 2 * TOP, STRIDE), f32)
    framed[channels:16] = zero
    framed[16 + channels :] = zero
    groups = (tile_r + 2 * TOP) // PLANES
    parts = []
    for g in range(groups):
        block = framed[:, PLANES * g : PLANES * g + PLANES, :]
        parts.append(jnp.swapaxes(block, 0, 1))
    rest = coarse_out.shape[1] - PAD - groups * STRIDE
    for i in range(PLANES):
        row = jnp.concatenate(
            [jnp.zeros((32, PAD), f32)] + [p[i] for p in parts] + [jnp.zeros((32, rest), f32)], 1
        ).astype(bf16)
        coarse_out[16 * i : 16 * i + 16, :] = row[:16]
        latent_out[16 * i : 16 * i + 16, :] = row[16:]

    lane = lax.broadcasted_iota(jnp.int32, (8, 128), 1)
    got = jnp.where(lane < per_slab, tables[0], jnp.where(lane < 2 * per_slab, table[...], tables[1]))
    row0 = got[:1] - (lax.axis_index("slab") * tile_r - TOP)
    col0 = got[1:2] - (lax.axis_index("patch") * tile_c - HALO)
    live = (got[3:4] < got[2:3]) & (lane[:1] < 3 * per_slab)
    live = live & (row0 < TOP + tile_r) & (row0 + patch > TOP)
    live = live & (col0 < HALO + tile_c) & (col0 + patch > HALO)
    tabs_out[...] = jnp.concatenate(
        [jnp.where(live, row0, FAR), jnp.where(live, col0, FAR), lane[:6]], 0
    )


def run_frame(shape, per_slab, patch, tile, *args):
    channels, tile_r, tile_c = tile
    smem, vmem, anyw = specs()
    lanes = lanes_of(tile_r + 2 * TOP) + 2 * PAD
    return pl.pallas_call(
        functools.partial(frame_kernel, shape, per_slab, patch),
        in_specs=[smem] + [vmem] * 6,
        out_specs=[vmem] * 3,
        out_shape=[
            jax.ShapeDtypeStruct((PLANES * 16, lanes), bf16),
            jax.ShapeDtypeStruct((PLANES * 16, lanes), bf16),
            jax.ShapeDtypeStruct((8, 128), jnp.int32),
        ],
        scratch_shapes=[
            pltpu.VMEM((2 * channels, tile_r, tile_c), bf16),
            pltpu.VMEM((32, tile_r + 2 * TOP, STRIDE), f32),
            pltpu.VMEM((2, 2 * channels, 16, tile_c), bf16),
            pltpu.VMEM((2, 8, 2 * channels * tile_r), f32),
            pltpu.VMEM((4, 2 * channels, 16, 128), bf16),
            pltpu.VMEM((8, 2 * channels * tile_r), f32),
            pltpu.VMEM((2, 8, 128), jnp.int32),
            pltpu.SemaphoreType.DMA((2, 8)),
            pltpu.SemaphoreType.DMA((2, 8)),
        ],
        compiler_params=pltpu.CompilerParams(
            collective_id=2, has_side_effects=True, vmem_limit_bytes=VMEM
        ),
        name="frame",
    )(*args)


def run_pool(shape, per_slab, cells, *args):
    vmem = specs()[1]
    entries = 3 * per_slab
    return pl.pallas_call(
        functools.partial(pool_kernel, shape, per_slab, cells),
        in_specs=[vmem] * 3,
        out_specs=vmem,
        out_shape=jax.ShapeDtypeStruct((entries, 128), f32),
        scratch_shapes=[
            pltpu.VMEM((entries, 128), f32),
            pltpu.VMEM((len(NEAR), entries, 128), f32),
            pltpu.SemaphoreType.DMA((len(NEAR),)),
            pltpu.SemaphoreType.DMA((len(NEAR),)),
        ],
        compiler_params=pltpu.CompilerParams(collective_id=1, has_side_effects=True),
        name="pool",
    )(*args)


def frame_constants(tile_c):
    move = np.zeros((tile_c, STRIDE), np.float32)
    move[np.arange(tile_c), HALO + np.arange(tile_c)] = 1
    ends = np.zeros((8, tile_c), np.float32)
    back = np.zeros((272, STRIDE), np.float32)
    for x in range(HALO):
        ends[x, x] = 1
        ends[HALO + x, tile_c - HALO + x] = 1
        back[128 - HALO + x, x] = 1
        back[128 + x, HALO + tile_c + x] = 1
        back[256 + HALO + x, x] = 1
        back[264 + x, HALO + tile_c + x] = 1
    return tuple(jnp.asarray(a, bf16) for a in (move, ends, back))


def body(
    coarse, latent, noise_level, reg_first, reg_second, den_first, den_middle, den_pool, den_last,
    anchors, patch_count, patch_weight,
):
    tile_r, tile_c = latent.shape[1:]
    patch = patch_weight.shape[0]
    rows = tile_r + 2 * TOP
    size = lanes_of(rows)
    slab = lax.axis_index("slab")
    column = lax.axis_index("patch")
    shape = (lax.axis_size("slab"), lax.axis_size("patch"))
    per_slab = anchors.shape[1]

    labels = np.arange(per_slab, dtype=np.int32)
    table = jnp.stack(
        [anchors[0, :, 0], anchors[0, :, 1], jnp.broadcast_to(patch_count, (per_slab,)), labels], 0
    )
    table = jnp.pad(jnp.tile(table, (1, 3)), ((0, 4), (0, 128 - 3 * per_slab)))
    coarse_flat, latent_flat, tabs = run_frame(
        shape, per_slab, patch, latent.shape,
        noise_level, coarse, latent, table, *frame_constants(tile_c),
    )

    top = TOP - slab * tile_r
    left = HALO - column * tile_c
    meta = jnp.stack([top, top + shape[0] * tile_r, left, left + shape[1] * tile_c])
    flat = np.arange(size, dtype=np.int32)
    rowi = PLANES * (flat // STRIDE)[None] + np.arange(PLANES, dtype=np.int32)[:, None]
    coli = np.broadcast_to(flat % STRIDE, (PLANES, size))
    fixed = (rows, patch, tile_r, tile_c)
    first, mean, part, ring, strips, order = run_regress(
        fixed, 3 * per_slab,
        meta.astype(jnp.int32), tabs, coarse_flat, latent_flat,
        jnp.asarray(rowi, jnp.int32), jnp.asarray(coli, jnp.int32),
        tabs, reg_first, reg_second, den_first,
    )

    lift = run_pool(shape, per_slab, patch * patch, part, ring, den_pool)

    weight = jnp.pad(patch_weight.astype(f32), ((0, 0), (0, STRIDE - patch)))
    weight = weight.reshape(patch // PLANES, PLANES, STRIDE).transpose(1, 0, 2)
    weight = weight.reshape(PLANES, patch // PLANES * STRIDE)
    end = -weight.shape[1] % 128
    weight = jnp.pad(weight, ((0, 0), (WFRONT, end + WFRONT)))
    weight = weight.reshape(PLANES, -1, 128).transpose(1, 0, 2)
    next_state, estimate = run_patches(
        fixed,
        order, tabs, noise_level, first, strips, lift, weight, mean, latent, den_middle, den_last,
    )
    return (next_state, estimate)


def solution(mesh):
    return jax.shard_map(
        body,
        mesh=mesh,
        in_specs=(
            P(None, "slab", "patch"), P(None, "slab", "patch"),
            P(), P(), P(), P(), P(), P(), P(),
            P("slab", None, None), P("slab"), P(),
        ),
        out_specs=(P(None, "slab", "patch"), P(None, "slab", "patch")),
        check_vma=False,
    )
```

```python
import functools

import jax
import jax.numpy as jnp
import numpy as np
from jax import lax
from jax.experimental import pallas as pl
from jax.experimental.pallas import tpu as pltpu
from jax.sharding import PartitionSpec as P

sigma_data = 0.5
step_ratio = 0.6

HALO = 4
TOP = 8
STRIDE = 264
STRIP = 272
PLANES = 8
PAD = 384
FRONT = 528
LAG = 3
STEP = 256
TILE = 512
COLUMN = 24
NEG = -1e30
VMEM = 60 * 1024 * 1024
f32, bf16 = jnp.float32, jnp.bfloat16


def lanes_of(rows):
    return -(-(rows // PLANES * STRIDE) // STEP) * STEP


def silu_half(t):
    return t + t * jnp.tanh(t)


def shifted(ref, base, step, depth):
    at = base + PAD
    edge = STRIDE // 128 * 128
    rest = STRIDE - edge
    mid = ref[:, pl.ds(at - 128, step + 256)]
    low = ref[(PLANES - 1) * depth :, pl.ds(at - edge - 128, step + 256)]
    high = ref[:depth, pl.ds(at + edge - 128, step + 256)]
    out = []
    for b in range(3):
        m = mid[:, 127 + b : 127 + b + step]
        rows = [low[:, 127 + b - rest : 127 + b - rest + step]]
        rows += [m[depth * i : depth * i + depth] for i in range(PLANES)]
        rows += [high[:, 127 + b + rest : 127 + b + rest + step]]
        out.append(rows)
    return out


def overlapped(parts):
    got = [parts[0][:96]]
    for a, b in zip(parts, parts[1:]):
        got.append(a[96:] + b[:96])
    return got + [parts[-1][96:]]


def combined(ref, base, step):
    at = base + PAD
    edge = STRIDE // 128 * 128
    rest = STRIDE - edge

    def columns(plane, start, move):
        total = None
        for b in range(3):
            row = (plane + 1) * 48 + b * 16
            block = ref[row : row + 16, pl.ds(start - 128, step + 256)]
            term = block[:, 127 + b + move : 127 + b + move + step]
            total = term if total is None else total + term
        return total

    planes = [columns(i, at, 0) for i in range(PLANES)]
    planes[-1] += columns(-1, at + edge, rest)
    planes[0] += columns(PLANES, at - edge, -rest)
    return planes


def taps_of(raw, lo, hi, count):
    parts = []
    for t in range(9):
        parts.append(0.5 * raw[t].astype(f32)[lo:hi])
        if hi - lo < count:
            parts.append(jnp.zeros((count - hi + lo, 128), f32))
    return parts


def gather_pair(raw, out):
    gap = [jnp.zeros((48, 128), f32)]
    parts = taps_of(raw, 0, raw.shape[1], 16)
    out[:128, :] = jnp.concatenate(parts + gap, 0).T.astype(bf16)
    out[128:, :] = jnp.concatenate(gap + parts, 0).T.astype(bf16)


def spread_pair(raw, out, front):
    zeros = [jnp.zeros((n, 128), f32) for n in (front, 16 - front - raw.shape[1]) if n]
    parts = []
    for a in (2, 1, 0):
        for b in range(3):
            taps = raw[3 * a + b].astype(f32)
            parts += [zeros[0], taps] if front else [taps, zeros[0]]
    gap = jnp.zeros((48, 128), f32)
    out[:, :128] = jnp.concatenate(parts + [gap], 0).astype(bf16)
    out[:, 128:] = jnp.concatenate([gap] + parts, 0).astype(bf16)


def regress_kernel(
    rows, patch, tile_r, tile_c,
    meta, tabs, coarse, latent, tabs_v, raw1, raw2, raw3,
    first_out, mean_out, part_out, ring_out, strips_out, order,
    w1, w2, w3, sums, cond_a, cond_b, cond_c, sbuf, sem,
):
    size = lanes_of(rows)
    steps = size // STEP
    cells = size + 2 * FRONT
    groups = rows // PLANES
    row_lo, row_hi, col_lo, col_hi = meta[0], meta[1], meta[2], meta[3]
    gather_pair(raw1, w1)
    spread_pair(raw2, w2, 4)
    side = taps_of(raw3, 16, 24, 8)
    side = [side[t] for t in (0, 1, 3, 4, 6, 7, 2, 5, 8)] + [jnp.zeros((8, 128), f32)]
    w3[...] = jnp.concatenate(taps_of(raw3, 0, 16, 16) + side, 0).T.astype(bf16)

    def enlist(q, n):
        live = tabs[0, q] < FAR

        @pl.when(live)
        def _():
            order[n] = q

        return n + live.astype(jnp.int32)

    entries = ring_out.shape[0]
    number = lax.fori_loop(0, entries, enlist, jnp.int32(0))
    order[entries] = number
    for ref in (sums, cond_a, cond_b):
        ref[:, :PAD] = jnp.zeros((ref.shape[0], PAD), ref.dtype)
        ref[:, PAD + size :] = jnp.zeros((ref.shape[0], PAD), ref.dtype)
    cond_c[:FRONT, :] = jnp.zeros((FRONT, 128), f32)
    cond_c[FRONT + size : 2 * FRONT + size, :] = jnp.zeros((FRONT, 128), f32)
    cond_c[cells : cells + FRONT, :] = jnp.zeros((FRONT, 128), f32)
    cond_c[cells + FRONT + size :, :] = jnp.zeros((cond_c.shape[0] - cells - FRONT - size, 128), f32)

    def stage1(k):
        base = pl.multiple_of(k * STEP, 128)
        x = shifted(coarse, base, STEP, 16)
        group = base // STRIDE
        lane = lax.broadcasted_iota(jnp.int32, (PLANES, STEP), 1)
        later = (lane >= (group + 1) * STRIDE - base).astype(jnp.int32)
        col = lane + base - (group + later) * STRIDE
        row = (group + later) * PLANES + lax.broadcasted_iota(jnp.int32, (PLANES, STEP), 0)
        inside = (row >= row_lo) & (row < row_hi) & (col >= col_lo) & (col < col_hi)
        keep = jnp.where(inside, 1.0, 0.0)
        parts = []
        for pair in range(PLANES // 2):
            stack = jnp.concatenate(
                [x[b][2 * pair + r] for r in range(4) for b in range(3)], 0
            )
            h = silu_half(jnp.dot(w1[...], stack, preferred_element_type=f32))
            h = jnp.concatenate(
                [
                    h[:128] * keep[2 * pair : 2 * pair + 1],
                    h[128:] * keep[2 * pair + 1 : 2 * pair + 2],
                ],
                0,
            ).astype(bf16)
            parts.append(jnp.dot(w2[...], h, preferred_element_type=f32))
        sums[:, pl.ds(base + PAD, STEP)] = jnp.concatenate(overlapped(parts), 0)

    def stage2(k):
        base = pl.multiple_of(k * STEP, 128)
        means = combined(sums, base, STEP)
        lat = latent[:, pl.ds(base + PAD, STEP)].astype(f32)
        zero = jnp.zeros((8, STEP), f32)
        main, side, full = [], [], []
        for i, mean in enumerate(means):
            head = lat[16 * i : 16 * i + 8]
            mid = lat[16 * i + 8 : 16 * i + 16] + mean[:8]
            main += [head, mid]
            side.append(mean[8:])
            full += [head, mid, mean[8:], zero]
        mean_out[:, pl.ds(base, STEP)] = jnp.concatenate(means, 0)
        cond_a[:, pl.ds(base + PAD, STEP)] = jnp.concatenate(main, 0).astype(bf16)
        cond_b[:, pl.ds(base + PAD, STEP)] = jnp.concatenate(side, 0)
        for h in range(2):
            block = jnp.concatenate(full[16 * h : 16 * h + 16], 0)
            for j in range(STEP // 128):
                cond_c[pl.ds(base + h * cells + FRONT + 128 * j, 128), :] = block[
                    :, 128 * j : 128 * j + 128
                ].T

    def stage3(k):
        base = pl.multiple_of(k * STEP, 128)
        xa = shifted(cond_a, base, STEP, 16)
        xb = shifted(cond_b, base, STEP, 8)
        left = [
            jnp.concatenate([xb[0][i], xb[1][i]], 0).astype(bf16) for i in range(PLANES + 2)
        ]
        right = [
            jnp.concatenate([xb[2][i], xb[2][min(i + 1, PLANES + 1)]], 0).astype(bf16)
            for i in range(PLANES + 2)
        ]
        group = base // STRIDE
        lane = lax.broadcasted_iota(jnp.int32, (STEP, 128), 0)
        split = (group + 1) * STRIDE - base
        later = lane >= split
        col = lane + base - group * STRIDE - jnp.where(later, STRIDE, 0)
        r0b, c0b = tabs_v[:1], tabs_v[1:2]
        wanted = (
            (col > c0b) & (col < c0b + (patch - 1)) & (col >= HALO) & (col < HALO + tile_c)
        )
        now = jnp.where(wanted & (lane < split), 1.0, 0.0).astype(bf16)
        late = jnp.where(wanted & later, 1.0, 0.0).astype(bf16)

        def row_keep(row):
            keep = (
                (r0b < row) & (row < r0b + (patch - 1)) & (row >= TOP) & (row < TOP + tile_r)
            )
            return jnp.where(keep, 1.0, 0.0).astype(bf16)

        masks, firsts = [], []
        for i in range(PLANES):
            stack = jnp.concatenate(
                [xa[b][i + a] for a in range(3) for b in range(3)]
                + [left[i], left[i + 1], left[i + 2], right[i], right[i + 2]],
                0,
            )
            first = silu_half(jnp.dot(w3[...], stack, preferred_element_type=f32)).astype(bf16)
            first_out[128 * i : 128 * i + 128, pl.ds(base, STEP)] = first
            firsts.append(first)
            row = group * PLANES + i
            masks.append(now * row_keep(row) + late * row_keep(row + PLANES))
        part_out[...] += jnp.dot(
            jnp.concatenate(firsts, 1), jnp.concatenate(masks, 0), preferred_element_type=f32
        )

    part_out[...] = jnp.zeros_like(part_out)

    @pl.loop(0, LAG, unroll=LAG)
    def _(k):
        stage1(k)

    @pl.loop(LAG, 2 * LAG, unroll=LAG)
    def _(k):
        stage2(k - LAG)
        stage1(k)

    @pl.loop(2 * LAG, steps)
    def _(k):
        stage3(k - 2 * LAG)
        stage2(k - LAG)
        stage1(k)

    @pl.loop(steps - LAG, steps, unroll=LAG)
    def _(k):
        stage3(k - LAG)
        stage2(k)

    @pl.loop(steps - LAG, steps, unroll=LAG)
    def _(k):
        stage3(k)

    ring_out[...] = jnp.zeros_like(ring_out)
    j = lax.broadcasted_iota(jnp.int32, (STRIDE, 128), 0)
    g = lax.broadcasted_iota(jnp.int32, (COLUMN, 128), 0)
    i = jnp.concatenate([g * PLANES + p for p in range(PLANES)], 0)
    live = jnp.concatenate([g < groups for p in range(PLANES)], 0)

    def put(n):
        return pltpu.make_async_copy(sbuf.at[n % 2], strips_out.at[n], sem.at[n % 2])

    @pl.loop(0, number)
    def _(n):
        q = order[n]
        r0, c0 = tabs[0, q], tabs[1, q]
        r1, c1 = r0 + patch - 1, c0 + patch - 1

        slot = n % 2

        @pl.when(n >= 2)
        def _():
            put(n - 2).wait()

        def add(value, weight):
            got = jnp.sum(jnp.where(weight, value.astype(f32), 0.0), 0, keepdims=True)
            ring_out[pl.ds(q, 1), :] += got

        for s, (r, height) in enumerate(((r0, (1, 2)), (r1, (0, 1)))):

            @pl.when((r >= TOP - 1) & (r <= TOP + tile_r))
            def _(s=s, r=r, height=height):
                total = None
                for a in height:
                    at = r + a - 1
                    plane = at % PLANES
                    start = plane // 4 * cells + FRONT + at // PLANES * STRIDE
                    for b in range(3):
                        x = cond_c[pl.ds(start + b - 1, STRIDE), :]
                        x = jnp.where((j + (b - 1) >= c0) & (j + (b - 1) <= c1), x, 0.0)
                        x = pltpu.roll(x, (128 - plane % 4 * 32) % 128, 1)[:, :24].astype(bf16)
                        term = jnp.dot(x, raw3[3 * a + b], preferred_element_type=f32)
                        total = term if total is None else total + term
                value = silu_half(0.5 * total)
                tail = jnp.zeros((STRIP - STRIDE, 128), f32)
                sbuf[slot, STRIP * s : STRIP * s + STRIP, :] = jnp.concatenate(
                    [value, tail], 0
                ).astype(bf16)
                value = value.astype(bf16)
                own = (r >= TOP) & (r < TOP + tile_r)
                add(value, own & (j >= c0) & (j <= c1) & (j >= HALO) & (j < HALO + tile_c))

        for s, (c, breadth) in enumerate(((c0, (1, 2)), (c1, (0, 1)))):

            @pl.when((c >= HALO - 1) & (c <= HALO + tile_c))
            def _(s=s, c=c, breadth=breadth):
                total = None
                for b in breadth:

                    def at(h, g_move, b=b):
                        start = h * cells + FRONT + c + b - 1 + g_move * STRIDE
                        return cond_c[pl.ds(start, COLUMN, stride=STRIDE), :]

                    halves = [at(0, 0), at(1, 0)]
                    planes = [at(1, -1)[:, 96:]]
                    planes += [
                        halves[p // 4][:, p % 4 * 32 : p % 4 * 32 + 32] for p in range(PLANES)
                    ]
                    planes += [at(0, 1)[:, :32]]
                    for a in range(3):
                        x = jnp.concatenate(planes[a : a + PLANES], 0)
                        inside = (i + (a - 1) >= r0) & (i + (a - 1) <= r1)
                        x = jnp.where(inside[:, :32], x, 0.0)[:, :24].astype(bf16)
                        term = jnp.dot(x, raw3[3 * a + b], preferred_element_type=f32)
                        total = term if total is None else total + term
                value = silu_half(0.5 * total).astype(bf16)
                lo = 2 * STRIP + PLANES * COLUMN * s
                sbuf[slot, lo : lo + PLANES * COLUMN, :] = value
                own = (c >= HALO) & (c < HALO + tile_c) & live
                add(value, own & (i > r0) & (i < r1) & (i >= TOP) & (i < TOP + tile_r))

        put(n).start()

    for back in (2, 1):

        @pl.when(number >= back)
        def _(back=back):
            put(number - back).wait()


def patch_kernel(
    rows, patch, tile_r, tile_c,
    order, tabs, noise, first, strips, lift, weight, mean, latent, middle, raw5,
    next_out, est_out,
    w5, m, acc, sbuf, keep_row, keep_col, wbuf, sem,
):
    size = lanes_of(rows)
    steps = size // STEP
    groups = rows // PLANES
    number = order[lift.shape[0]]
    spread_pair(raw5, w5, 0)

    def mixed(x, dim):
        return 0.5 * lax.dot_general(
            x, middle[...], (((dim,), (1,)), ((), ())), preferred_element_type=f32
        )
    high = 2 * STRIP
    tall = PLANES * COLUMN

    def fetch(n):
        return pltpu.make_async_copy(strips.at[n], sbuf.at[n % 2], sem.at[n % 2])

    @pl.when(number > 0)
    def _():
        fetch(0).start()

    @pl.loop(0, steps, unroll=2)
    def _(k):
        base = pl.multiple_of(k * STEP, 128)
        for i in range(PLANES):
            x = first[128 * i : 128 * i + 128, pl.ds(base, STEP)]
            m[pl.ds(base + i * size, STEP), :] = mixed(x, 0)

    acc[...] = jnp.zeros_like(acc)
    m[PLANES * size :, :] = jnp.zeros((TILE, 128), f32)
    j = lax.broadcasted_iota(jnp.int32, (STRIDE, 128), 0)
    g = lax.broadcasted_iota(jnp.int32, (COLUMN, 128), 0)
    lane = lax.broadcasted_iota(jnp.int32, (8, TILE), 1)
    ones = jnp.where(lax.broadcasted_iota(jnp.int32, (16, TILE), 0) >= 12, 1.0, 0.0)

    @pl.loop(0, number)
    def _(n):
        q = order[n]
        r0, c0 = tabs[0, q], tabs[1, q]
        r1, c1 = r0 + patch - 1, c0 + patch - 1
        slot = n % 2
        fetch(n).wait()

        @pl.when(n + 1 < number)
        def _():
            fetch(n + 1).start()

        half_lift = lift[pl.ds(q, 1), :]

        def row_ok(r):
            return (r >= TOP - 1) & (r <= TOP + tile_r)

        def col_ok(c):
            return (c >= HALO - 1) & (c <= HALO + tile_c)

        def row_at(r):
            return pl.ds(pl.multiple_of(r % PLANES * size + r // PLANES * STRIDE, 8), STRIDE)

        def col_at(c, i):
            return pl.ds(c + i * size, groups, stride=STRIDE)

        cols = ((0, c0 - 1, None), (1, c0, 0), (2, c1, 1), (3, c1 + 1, None))
        rws = ((0, r0 - 1, None), (1, r0, 0), (2, r1, 1), (3, r1 + 1, None))
        for s, c, source in cols:

            @pl.when(col_ok(c))
            def _(s=s, c=c, source=source):
                if source is not None:
                    strip = sbuf[slot, high + tall * source : high + tall * source + tall, :]
                    got = mixed(strip, 1)
                for i in range(PLANES):
                    keep_col[s, i, :groups, :] = m[col_at(c, i), :]
                    if source is None:
                        new = jnp.full((groups, 128), NEG, f32)
                    else:
                        row = g * PLANES + i
                        new = got[COLUMN * i : COLUMN * i + COLUMN]
                        new = jnp.where((row >= r0) & (row <= r1), new, NEG)[:groups]
                    m[col_at(c, i), :] = new

        for s, r, source in rws:

            @pl.when(row_ok(r))
            def _(s=s, r=r, source=source):
                keep_row[s, :, :] = m[row_at(r), :]
                if source is None:
                    m[row_at(r), :] = jnp.full((STRIDE, 128), NEG, f32)
                else:
                    strip = sbuf[slot, STRIP * source : STRIP * source + STRIP, :]
                    got = mixed(strip, 1)[:STRIDE]
                    m[row_at(r), :] = jnp.where((j >= c0) & (j <= c1), got, NEG)

        top = r0 // PLANES
        phase = r0 - top * PLANES
        move = top * STRIDE + c0
        shifts = (move, move + STRIDE, jnp.where(phase == 0, move - STRIDE, move))
        clo, chi = jnp.maximum(c0, HALO - 1), jnp.minimum(c1, HALO + tile_c)
        glo = jnp.maximum(r0, TOP - 1) // PLANES
        ghi = jnp.minimum(r1, TOP + tile_r) // PLANES

        @pl.loop((glo * STRIDE + clo) // TILE, (ghi * STRIDE + chi) // TILE + 1)
        def _(k):
            base = pl.multiple_of(k * TILE, 128)
            col_start = base % STRIDE
            col = lane + col_start
            for _ in range((TILE + STRIDE - 2) // STRIDE):
                col = jnp.where(col >= STRIDE, col - STRIDE, col)
            for b in range(3):
                inside = (col - (b - 1) >= c0) & (col - (b - 1) <= c1)
                for v, shift in enumerate(shifts):
                    source = base - shift - (b - 1) + WFRONT
                    rem = source % 128
                    count = TILE // 128
                    blocks = weight[pl.ds(source // 128, count + 1), :, :]
                    blocks = blocks.reshape(8 * count + 8, 128)
                    rolled = pltpu.roll(blocks, (128 - rem) % 128, 1)
                    here = lane[:, :128] < 128 - rem
                    got = jnp.concatenate(
                        [
                            jnp.where(here, rolled[8 * x : 8 * x + 8], rolled[8 * x + 8 : 8 * x + 16])
                            for x in range(count)
                        ],
                        1,
                    )
                    wbuf[8 * (3 * v + b) : 8 * (3 * v + b) + 8, :] = jnp.where(inside, got, 0.0)
            pairs = []
            for pair in range(PLANES // 2):
                halves = []
                for i in (2 * pair, 2 * pair + 1):
                    t = m[pl.ds(base + i * size, TILE), :] + half_lift
                    halves.append(silu_half(t).astype(bf16))
                pairs.append(jnp.concatenate(halves, 1))
            y = lax.dot_general(
                w5[...], jnp.concatenate(pairs, 0), (((1,), (1,)), ((), ())),
                preferred_element_type=f32,
            )
            parts = overlapped([y[:, TILE * x : TILE * x + TILE] for x in range(PLANES // 2)])
            for i in range(-1, PLANES + 1):
                block = parts[(i + 1) // 2][(i + 1) % 2 * 48 : (i + 1) % 2 * 48 + 48]
                if i < 0:
                    version = 1
                elif i == PLANES:
                    version = 2
                else:
                    version = jnp.where(phase <= i, 0, 1)
                line = (i - phase) % PLANES
                for b in range(3):
                    term = block[16 * b : 16 * b + 16]
                    if b == 1 and 0 <= i < PLANES:
                        term = term + ones
                    w = wbuf[pl.ds(8 * (3 * version + b) + line, 1), :]
                    row = 48 * (i + 1) + 16 * b
                    acc[row : row + 16, pl.ds(base + PAD, TILE)] += term * w

        for s, r, source in rws[::-1]:

            @pl.when(row_ok(r))
            def _(s=s, r=r):
                m[row_at(r), :] = keep_row[s, :, :]

        for s, c, source in cols[::-1]:

            @pl.when(col_ok(c))
            def _(s=s, c=c):
                for i in range(PLANES):
                    m[col_at(c, i), :] = keep_col[s, i, :groups, :]

    for k in range(tile_r // PLANES):
        start = (k + TOP // PLANES) * STRIDE + HALO
        whole = start // 128 * 128
        off = start - whole
        span = -(-(off + tile_c) // 128) * 128
        planes = combined(acc, whole, span)
        got = jnp.stack([p / (1.0 + p[12:13]) for p in planes], 0)[:, :, off : off + tile_c]
        got = jnp.swapaxes(got, 0, 1)[:12]
        base = mean[:, whole : whole + span].reshape(PLANES, 16, span)[:, :, off : off + tile_c]
        base = jnp.swapaxes(base, 0, 1)[4:]
        rows_at = slice(PLANES * k, PLANES * k + PLANES)
        scale_in, skip, scale_out = precondition(noise)
        lat = latent[:, rows_at, :]
        denoised = skip * lat + scale_out * got
        next_out[:, rows_at, :] = lat + (step_ratio - 1.0) * (lat - denoised)
        est_out[:, rows_at, :] = base + denoised


FAR = 1 << 20
WFRONT = 2048


def precondition(noise):
    level = jnp.full((1, 1, 1), noise[0], f32)
    spread = level * level + sigma_data * sigma_data
    root = jnp.sqrt(spread)
    return 1.0 / root, sigma_data * sigma_data / spread, level * sigma_data / root


def specs():
    return (
        pl.BlockSpec(memory_space=pltpu.SMEM),
        pl.BlockSpec(memory_space=pltpu.VMEM),
        pl.BlockSpec(memory_space=pl.ANY),
    )


def run_regress(fixed, entries, *args):
    size = lanes_of(fixed[0])
    smem, vmem, anyw = specs()
    cells = size + 2 * FRONT
    return pl.pallas_call(
        functools.partial(regress_kernel, *fixed),
        in_specs=[smem] * 2 + [vmem] * 6,
        out_specs=[vmem, vmem, vmem, vmem, anyw, smem],
        out_shape=[
            jax.ShapeDtypeStruct((PLANES * 128, size), bf16),
            jax.ShapeDtypeStruct((PLANES * 16, size), f32),
            jax.ShapeDtypeStruct((128, 128), f32),
            jax.ShapeDtypeStruct((entries, 128), f32),
            jax.ShapeDtypeStruct((entries, 2 * (STRIP + PLANES * COLUMN), 128), bf16),
            jax.ShapeDtypeStruct((entries + 1,), jnp.int32),
        ],
        scratch_shapes=[
            pltpu.VMEM((256, 192), bf16),
            pltpu.VMEM((192, 256), bf16),
            pltpu.VMEM((128, 224), bf16),
            pltpu.VMEM((48 * (PLANES + 2), size + 2 * PAD), f32),
            pltpu.VMEM((16 * PLANES, size + 2 * PAD), bf16),
            pltpu.VMEM((8 * PLANES, size + 2 * PAD), f32),
            pltpu.VMEM((2 * cells + COLUMN * STRIDE - size + STRIDE, 128), f32),
            pltpu.VMEM((2, 2 * (STRIP + PLANES * COLUMN), 128), bf16),
            pltpu.SemaphoreType.DMA((2,)),
        ],
        compiler_params=pltpu.CompilerParams(vmem_limit_bytes=VMEM),
        name="regress",
    )(*args)


def run_patches(fixed, *args):
    rows = fixed[0]
    size = lanes_of(rows)
    smem, vmem, anyw = specs()
    return pl.pallas_call(
        functools.partial(patch_kernel, *fixed),
        in_specs=[smem] * 3 + [vmem, anyw] + [vmem] * 6,
        out_specs=[vmem] * 2,
        out_shape=[jax.ShapeDtypeStruct((12, fixed[2], fixed[3]), f32)] * 2,
        scratch_shapes=[
            pltpu.VMEM((192, 256), bf16),
            pltpu.VMEM((PLANES * size + TILE, 128), f32),
            pltpu.VMEM((48 * (PLANES + 2), size + 2 * PAD), f32),
            pltpu.VMEM((2, 2 * (STRIP + PLANES * COLUMN), 128), bf16),
            pltpu.VMEM((4, STRIDE, 128), f32),
            pltpu.VMEM((4, PLANES, COLUMN, 128), f32),
            pltpu.VMEM((72, TILE), f32),
            pltpu.SemaphoreType.DMA((2,)),
        ],
        compiler_params=pltpu.CompilerParams(vmem_limit_bytes=VMEM),
        name="patches",
    )(*args)


NEAR = [(di, dj) for di in range(-2, 3) for dj in range(-1, 2) if (di, dj) != (0, 0)]
MESH = pl.DeviceIdType.MESH


def neighbours(near, shape):
    me = (lax.axis_index("slab"), lax.axis_index("patch"))
    out = []
    for offset in near:
        at = tuple(a + d for a, d in zip(me, offset))
        there = (at[0] >= 0) & (at[0] < shape[0]) & (at[1] >= 0) & (at[1] < shape[1])
        out.append((there, at))
    return out


def greet(around):
    barrier = pltpu.get_barrier_semaphore()
    for there, at in around:

        @pl.when(there)
        def _(at=at):
            pl.semaphore_signal(barrier, inc=1, device_id=at, device_id_type=MESH)

    peers = jnp.int32(0)
    for there, at in around:
        peers = peers + there.astype(jnp.int32)
    pl.semaphore_wait(barrier, peers)


def pool_kernel(shape, per_slab, cells, part, ring, pool, lift, mine, got, send, recv):
    around = neighbours(NEAR, shape)
    greet(around)
    mine[...] = ring[...] + part[...].T[: 3 * per_slab]
    copies = []
    for x, (there, at) in enumerate(around):
        copy = pltpu.make_async_remote_copy(
            src_ref=mine, dst_ref=got.at[len(NEAR) - 1 - x],
            send_sem=send.at[x], recv_sem=recv.at[len(NEAR) - 1 - x],
            device_id=at, device_id_type=MESH,
        )
        copies.append(copy)

        @pl.when(there)
        def _(copy=copy):
            copy.start()

    lift[...] = mine[...]
    for x, (there, at) in enumerate(around):
        di = NEAR[x][0]

        @pl.when(there)
        def _(x=x, di=di):
            copies[len(NEAR) - 1 - x].wait_recv()
            for d in range(3):
                e = d - di
                if 0 <= e < 3:
                    lift[per_slab * d : per_slab * d + per_slab, :] += got[
                        x, per_slab * e : per_slab * e + per_slab, :
                    ]

    for x, (there, at) in enumerate(around):

        @pl.when(there)
        def _(x=x):
            copies[x].wait_send()

    lift[...] = 0.5 * lax.dot_general(
        lift[...] / cells, pool[...].astype(f32), (((1,), (1,)), ((), ())),
        precision=lax.Precision.HIGHEST, preferred_element_type=f32,
    )


SIDES = [(-1, 0), (1, 0), (0, -1), (0, 1), (-1, -1), (-1, 1), (1, -1), (1, 1)]


def frame_kernel(
    shape, per_slab, patch,
    noise, coarse, latent, table, move, ends, back,
    coarse_out, latent_out, tabs_out,
    both, framed, edge_rows, edge_cols, corners, strip, tables, send, recv,
):
    channels, tile_r, tile_c = latent.shape
    around = neighbours(SIDES, shape)
    there = [a[0] for a in around]
    scale_in = precondition(noise)[0]
    both[:channels, :, :] = coarse[...]
    both[channels:, :, :] = (scale_in * latent[...]).astype(bf16)
    greet(around)

    def last(d):
        return slice(0, 16) if d < 0 else slice(tile_r - 16, tile_r)

    def side(d):
        return slice(0, 128) if d < 0 else slice(tile_c - 128, tile_c)

    opposite = [SIDES.index((-a, -b)) for a, b in SIDES]
    copies = []

    def copy(x, source, target, slot):
        here = opposite[x]
        return pltpu.make_async_remote_copy(
            src_ref=source, dst_ref=target, send_sem=send.at[slot, x], recv_sem=recv.at[slot, here],
            device_id=around[x][1], device_id_type=MESH,
        )

    def begin(x, one):
        copies.append((x, one))

        @pl.when(there[x])
        def _():
            one.start()

    for x in (0, 1):
        begin(x, copy(x, both.at[:, last(SIDES[x][0]), :], edge_rows.at[opposite[x]], 0))
        begin(x, copy(x, table, tables.at[opposite[x]], 1))
    for x in range(4, 8):
        di, dj = SIDES[x]
        begin(x, copy(x, both.at[:, last(di), side(dj)], corners.at[opposite[x] - 4], 0))
    flat = both[...].reshape(2 * channels * tile_r, tile_c)
    strip[...] = lax.dot_general(
        ends[...], flat, (((1,), (1,)), ((), ())), preferred_element_type=f32
    )
    for x in (2, 3):
        begin(x, copy(x, strip, edge_cols.at[opposite[x] - 2], 0))

    @pl.loop(0, 2 * channels)
    def _(c):
        x = jnp.dot(both[c], move[...], preferred_element_type=f32)
        framed[c + c // channels * (16 - channels), TOP : TOP + tile_r, :] = x

    for x in range(8):

        @pl.when(jnp.logical_not(there[x]))
        def _(x=x):
            if x < 2:
                edge_rows[x] = jnp.zeros(edge_rows.shape[1:], bf16)
                tables[x] = jnp.zeros(tables.shape[1:], jnp.int32)
            elif x < 4:
                edge_cols[x - 2] = jnp.zeros(edge_cols.shape[1:], f32)
            else:
                corners[x - 4] = jnp.zeros(corners.shape[1:], bf16)

    for x, one in copies:

        @pl.when(there[x])
        def _(one=one):
            one.wait_send()

    for x, one in copies:

        @pl.when(there[opposite[x]])
        def _(one=one):
            one.wait_recv()

    for c in range(2 * channels):
        at = c + c // channels * (16 - channels)
        cols = jnp.concatenate(
            [edge_cols[x][:, tile_r * c : tile_r * c + tile_r] for x in range(2)], 0
        ).astype(bf16)
        framed[at, TOP : TOP + tile_r, :] += lax.dot_general(
            cols, back[256:272, :], (((0,), (0,)), ((), ())), preferred_element_type=f32
        )
        for x, rows_at in ((0, slice(0, TOP)), (1, slice(TOP + tile_r, 2 * TOP + tile_r))):
            x4 = 4 + 2 * x
            got = jnp.dot(edge_rows[x, c], move[...], preferred_element_type=f32)
            got += jnp.dot(corners[x4 - 4, c], back[:128, :], preferred_element_type=f32)
            got += jnp.dot(corners[x4 - 3, c], back[128:256, :], preferred_element_type=f32)
            framed[at, rows_at, :] = got[16 - TOP :] if x == 0 else got[:TOP]
    zero = jnp.zeros((16 - channels, tile_r + 2 * TOP, STRIDE), f32)
    framed[channels:16] = zero
    framed[16 + channels :] = zero
    groups = (tile_r + 2 * TOP) // PLANES
    parts = []
    for g in range(groups):
        block = framed[:, PLANES * g : PLANES * g + PLANES, :]
        parts.append(jnp.swapaxes(block, 0, 1))
    rest = coarse_out.shape[1] - PAD - groups * STRIDE
    for i in range(PLANES):
        row = jnp.concatenate(
            [jnp.zeros((32, PAD), f32)] + [p[i] for p in parts] + [jnp.zeros((32, rest), f32)], 1
        ).astype(bf16)
        coarse_out[16 * i : 16 * i + 16, :] = row[:16]
        latent_out[16 * i : 16 * i + 16, :] = row[16:]

    lane = lax.broadcasted_iota(jnp.int32, (8, 128), 1)
    got = jnp.where(lane < per_slab, tables[0], jnp.where(lane < 2 * per_slab, table[...], tables[1]))
    row0 = got[:1] - (lax.axis_index("slab") * tile_r - TOP)
    col0 = got[1:2] - (lax.axis_index("patch") * tile_c - HALO)
    live = (got[3:4] < got[2:3]) & (lane[:1] < 3 * per_slab)
    live = live & (row0 < TOP + tile_r) & (row0 + patch > TOP)
    live = live & (col0 < HALO + tile_c) & (col0 + patch > HALO)
    tabs_out[...] = jnp.concatenate(
        [jnp.where(live, row0, FAR), jnp.where(live, col0, FAR), lane[:6]], 0
    )


def run_frame(shape, per_slab, patch, tile, *args):
    channels, tile_r, tile_c = tile
    smem, vmem, anyw = specs()
    lanes = lanes_of(tile_r + 2 * TOP) + 2 * PAD
    return pl.pallas_call(
        functools.partial(frame_kernel, shape, per_slab, patch),
        in_specs=[smem] + [vmem] * 6,
        out_specs=[vmem] * 3,
        out_shape=[
            jax.ShapeDtypeStruct((PLANES * 16, lanes), bf16),
            jax.ShapeDtypeStruct((PLANES * 16, lanes), bf16),
            jax.ShapeDtypeStruct((8, 128), jnp.int32),
        ],
        scratch_shapes=[
            pltpu.VMEM((2 * channels, tile_r, tile_c), bf16),
            pltpu.VMEM((32, tile_r + 2 * TOP, STRIDE), f32),
            pltpu.VMEM((2, 2 * channels, 16, tile_c), bf16),
            pltpu.VMEM((2, 8, 2 * channels * tile_r), f32),
            pltpu.VMEM((4, 2 * channels, 16, 128), bf16),
            pltpu.VMEM((8, 2 * channels * tile_r), f32),
            pltpu.VMEM((2, 8, 128), jnp.int32),
            pltpu.SemaphoreType.DMA((2, 8)),
            pltpu.SemaphoreType.DMA((2, 8)),
        ],
        compiler_params=pltpu.CompilerParams(
            collective_id=2, has_side_effects=True, vmem_limit_bytes=VMEM
        ),
        name="frame",
    )(*args)


def run_pool(shape, per_slab, cells, *args):
    vmem = specs()[1]
    entries = 3 * per_slab
    return pl.pallas_call(
        functools.partial(pool_kernel, shape, per_slab, cells),
        in_specs=[vmem] * 3,
        out_specs=vmem,
        out_shape=jax.ShapeDtypeStruct((entries, 128), f32),
        scratch_shapes=[
            pltpu.VMEM((entries, 128), f32),
            pltpu.VMEM((len(NEAR), entries, 128), f32),
            pltpu.SemaphoreType.DMA((len(NEAR),)),
            pltpu.SemaphoreType.DMA((len(NEAR),)),
        ],
        compiler_params=pltpu.CompilerParams(collective_id=1, has_side_effects=True),
        name="pool",
    )(*args)


def frame_constants(tile_c):
    move = np.zeros((tile_c, STRIDE), np.float32)
    move[np.arange(tile_c), HALO + np.arange(tile_c)] = 1
    ends = np.zeros((8, tile_c), np.float32)
    back = np.zeros((272, STRIDE), np.float32)
    for x in range(HALO):
        ends[x, x] = 1
        ends[HALO + x, tile_c - HALO + x] = 1
        back[128 - HALO + x, x] = 1
        back[128 + x, HALO + tile_c + x] = 1
        back[256 + HALO + x, x] = 1
        back[264 + x, HALO + tile_c + x] = 1
    return tuple(jnp.asarray(a, bf16) for a in (move, ends, back))


def body(
    coarse, latent, noise_level, reg_first, reg_second, den_first, den_middle, den_pool, den_last,
    anchors, patch_count, patch_weight,
):
    tile_r, tile_c = latent.shape[1:]
    patch = patch_weight.shape[0]
    rows = tile_r + 2 * TOP
    slab = lax.axis_index("slab")
    column = lax.axis_index("patch")
    shape = (lax.axis_size("slab"), lax.axis_size("patch"))
    per_slab = anchors.shape[1]

    labels = np.arange(per_slab, dtype=np.int32)
    table = jnp.stack(
        [anchors[0, :, 0], anchors[0, :, 1], jnp.broadcast_to(patch_count, (per_slab,)), labels], 0
    )
    table = jnp.pad(jnp.tile(table, (1, 3)), ((0, 4), (0, 128 - 3 * per_slab)))
    coarse_flat, latent_flat, tabs = run_frame(
        shape, per_slab, patch, latent.shape,
        noise_level, coarse, latent, table, *frame_constants(tile_c),
    )

    top = TOP - slab * tile_r
    left = HALO - column * tile_c
    meta = jnp.stack([top, top + shape[0] * tile_r, left, left + shape[1] * tile_c])
    fixed = (rows, patch, tile_r, tile_c)
    first, mean, part, ring, strips, order = run_regress(
        fixed, 3 * per_slab,
        meta.astype(jnp.int32), tabs, coarse_flat, latent_flat, tabs,
        jnp.transpose(reg_first, (0, 2, 1)), reg_second, jnp.transpose(den_first, (0, 2, 1)),
    )

    lift = run_pool(shape, per_slab, patch * patch, part, ring, den_pool)

    weight = jnp.pad(patch_weight.astype(f32), ((0, 0), (0, STRIDE - patch)))
    weight = weight.reshape(patch // PLANES, PLANES, STRIDE).transpose(1, 0, 2)
    weight = weight.reshape(PLANES, patch // PLANES * STRIDE)
    end = -weight.shape[1] % 128
    weight = jnp.pad(weight, ((0, 0), (WFRONT, end + WFRONT)))
    weight = weight.reshape(PLANES, -1, 128).transpose(1, 0, 2)
    next_state, estimate = run_patches(
        fixed,
        order, tabs, noise_level, first, strips, lift, weight, mean, latent, den_middle, den_last,
    )
    return (next_state, estimate)


def solution(mesh):
    return jax.shard_map(
        body,
        mesh=mesh,
        in_specs=(
            P(None, "slab", "patch"), P(None, "slab", "patch"),
            P(), P(), P(), P(), P(), P(), P(),
            P("slab", None, None), P("slab"), P(),
        ),
        out_specs=(P(None, "slab", "patch"), P(None, "slab", "patch")),
        check_vma=False,
    )
```

```python
import functools

import jax
import jax.numpy as jnp
import numpy as np
from jax import lax
from jax.experimental import pallas as pl
from jax.experimental.pallas import tpu as pltpu
from jax.sharding import PartitionSpec as P

sigma_data = 0.5
step_ratio = 0.6

HALO = 4
TOP = 8
STRIDE = 264
STRIP = 272
PLANES = 8
PAD = 384
FRONT = 528
LAG = 3
STEP = 256
TILE = 512
COLUMN = 24
NEG = -1e30
VMEM = 60 * 1024 * 1024
f32, bf16 = jnp.float32, jnp.bfloat16


def lanes_of(rows):
    return -(-(rows // PLANES * STRIDE) // STEP) * STEP


def silu_half(t):
    return t + t * jnp.tanh(t)


def shifted(ref, base, step, depth):
    at = base + PAD
    edge = STRIDE // 128 * 128
    rest = STRIDE - edge
    mid = ref[:, pl.ds(at - 128, step + 256)]
    low = ref[(PLANES - 1) * depth :, pl.ds(at - edge - 128, step + 256)]
    high = ref[:depth, pl.ds(at + edge - 128, step + 256)]
    out = []
    for b in range(3):
        m = mid[:, 127 + b : 127 + b + step]
        rows = [low[:, 127 + b - rest : 127 + b - rest + step]]
        rows += [m[depth * i : depth * i + depth] for i in range(PLANES)]
        rows += [high[:, 127 + b + rest : 127 + b + rest + step]]
        out.append(rows)
    return out


def overlapped(parts):
    got = [parts[0][:96]]
    for a, b in zip(parts, parts[1:]):
        got.append(a[96:] + b[:96])
    return got + [parts[-1][96:]]


def combined(ref, base, step):
    at = base + PAD
    edge = STRIDE // 128 * 128
    rest = STRIDE - edge

    def columns(plane, start, move):
        total = None
        for b in range(3):
            row = (plane + 1) * 48 + b * 16
            block = ref[row : row + 16, pl.ds(start - 128, step + 256)]
            term = block[:, 127 + b + move : 127 + b + move + step]
            total = term if total is None else total + term
        return total

    planes = [columns(i, at, 0) for i in range(PLANES)]
    planes[-1] += columns(-1, at + edge, rest)
    planes[0] += columns(PLANES, at - edge, -rest)
    return planes


def taps_of(raw, lo, hi, count):
    parts = []
    for t in range(9):
        parts.append(0.5 * raw[t].astype(f32)[lo:hi])
        if hi - lo < count:
            parts.append(jnp.zeros((count - hi + lo, 128), f32))
    return parts


def gather_pair(raw, out):
    gap = [jnp.zeros((48, 128), f32)]
    parts = taps_of(raw, 0, raw.shape[1], 16)
    out[:128, :] = jnp.concatenate(parts + gap, 0).T.astype(bf16)
    out[128:, :] = jnp.concatenate(gap + parts, 0).T.astype(bf16)


def spread_pair(raw, out, front):
    zeros = [jnp.zeros((n, 128), f32) for n in (front, 16 - front - raw.shape[1]) if n]
    parts = []
    for a in (2, 1, 0):
        for b in range(3):
            taps = raw[3 * a + b].astype(f32)
            parts += [zeros[0], taps] if front else [taps, zeros[0]]
    gap = jnp.zeros((48, 128), f32)
    out[:, :128] = jnp.concatenate(parts + [gap], 0).astype(bf16)
    out[:, 128:] = jnp.concatenate([gap] + parts, 0).astype(bf16)


def regress_kernel(
    rows, patch, tile_r, tile_c,
    meta, tabs, coarse, latent, tabs_v, raw1, raw2, raw3,
    first_out, mean_out, part_out, ring_out, strips_out, order,
    w1, w2, w3, sums, cond_a, cond_b, cond_c, fbuf, sbuf, sem, fsem,
):
    size = lanes_of(rows)
    steps = size // STEP
    cells = size + 2 * FRONT
    groups = rows // PLANES
    row_lo, row_hi, col_lo, col_hi = meta[0], meta[1], meta[2], meta[3]
    gather_pair(raw1, w1)
    spread_pair(raw2, w2, 4)
    side = taps_of(raw3, 16, 24, 8)
    side = [side[t] for t in (0, 1, 3, 4, 6, 7, 2, 5, 8)] + [jnp.zeros((8, 128), f32)]
    w3[...] = jnp.concatenate(taps_of(raw3, 0, 16, 16) + side, 0).T.astype(bf16)

    def enlist(q, n):
        live = tabs[0, q] < FAR

        @pl.when(live)
        def _():
            order[n] = q

        return n + live.astype(jnp.int32)

    entries = ring_out.shape[0]
    number = lax.fori_loop(0, entries, enlist, jnp.int32(0))
    order[entries] = number
    for ref in (sums, cond_a, cond_b):
        ref[:, :PAD] = jnp.zeros((ref.shape[0], PAD), ref.dtype)
        ref[:, PAD + size :] = jnp.zeros((ref.shape[0], PAD), ref.dtype)
    cond_c[:FRONT, :] = jnp.zeros((FRONT, 128), f32)
    cond_c[FRONT + size : 2 * FRONT + size, :] = jnp.zeros((FRONT, 128), f32)
    cond_c[cells : cells + FRONT, :] = jnp.zeros((FRONT, 128), f32)
    cond_c[cells + FRONT + size :, :] = jnp.zeros((cond_c.shape[0] - cells - FRONT - size, 128), f32)

    def stage1(k):
        base = pl.multiple_of(k * STEP, 128)
        x = shifted(coarse, base, STEP, 16)
        group = base // STRIDE
        lane = lax.broadcasted_iota(jnp.int32, (PLANES, STEP), 1)
        later = (lane >= (group + 1) * STRIDE - base).astype(jnp.int32)
        col = lane + base - (group + later) * STRIDE
        row = (group + later) * PLANES + lax.broadcasted_iota(jnp.int32, (PLANES, STEP), 0)
        inside = (row >= row_lo) & (row < row_hi) & (col >= col_lo) & (col < col_hi)
        keep = jnp.where(inside, 1.0, 0.0)
        parts = []
        for pair in range(PLANES // 2):
            stack = jnp.concatenate(
                [x[b][2 * pair + r] for r in range(4) for b in range(3)], 0
            )
            h = silu_half(jnp.dot(w1[...], stack, preferred_element_type=f32))
            h = jnp.concatenate(
                [
                    h[:128] * keep[2 * pair : 2 * pair + 1],
                    h[128:] * keep[2 * pair + 1 : 2 * pair + 2],
                ],
                0,
            ).astype(bf16)
            parts.append(jnp.dot(w2[...], h, preferred_element_type=f32))
        sums[:, pl.ds(base + PAD, STEP)] = jnp.concatenate(overlapped(parts), 0)

    def stage2(k):
        base = pl.multiple_of(k * STEP, 128)
        means = combined(sums, base, STEP)
        lat = latent[:, pl.ds(base + PAD, STEP)].astype(f32)
        zero = jnp.zeros((8, STEP), f32)
        main, side, full = [], [], []
        for i, mean in enumerate(means):
            head = lat[16 * i : 16 * i + 8]
            mid = lat[16 * i + 8 : 16 * i + 16] + mean[:8]
            main += [head, mid]
            side.append(mean[8:])
            full += [head, mid, mean[8:], zero]
        mean_out[:, pl.ds(base, STEP)] = jnp.concatenate(means, 0)
        cond_a[:, pl.ds(base + PAD, STEP)] = jnp.concatenate(main, 0).astype(bf16)
        cond_b[:, pl.ds(base + PAD, STEP)] = jnp.concatenate(side, 0)
        for h in range(2):
            block = jnp.concatenate(full[16 * h : 16 * h + 16], 0)
            for j in range(STEP // 128):
                cond_c[pl.ds(base + h * cells + FRONT + 128 * j, 128), :] = block[
                    :, 128 * j : 128 * j + 128
                ].T

    def put_first(k):
        at = pl.ds(pl.multiple_of(k * STEP, 128), STEP)
        return pltpu.make_async_copy(fbuf.at[k % 2], first_out.at[:, at], fsem.at[k % 2])

    def stage3(k):
        slot = k % 2
        base = pl.multiple_of(k * STEP, 128)
        xa = shifted(cond_a, base, STEP, 16)
        xb = shifted(cond_b, base, STEP, 8)
        left = [
            jnp.concatenate([xb[0][i], xb[1][i]], 0).astype(bf16) for i in range(PLANES + 2)
        ]
        right = [
            jnp.concatenate([xb[2][i], xb[2][min(i + 1, PLANES + 1)]], 0).astype(bf16)
            for i in range(PLANES + 2)
        ]
        group = base // STRIDE
        lane = lax.broadcasted_iota(jnp.int32, (STEP, 128), 0)
        split = (group + 1) * STRIDE - base
        later = lane >= split
        col = lane + base - group * STRIDE - jnp.where(later, STRIDE, 0)
        r0b, c0b = tabs_v[:1], tabs_v[1:2]
        wanted = (
            (col > c0b) & (col < c0b + (patch - 1)) & (col >= HALO) & (col < HALO + tile_c)
        )
        now = jnp.where(wanted & (lane < split), 1.0, 0.0).astype(bf16)
        late = jnp.where(wanted & later, 1.0, 0.0).astype(bf16)

        def row_keep(row):
            keep = (
                (r0b < row) & (row < r0b + (patch - 1)) & (row >= TOP) & (row < TOP + tile_r)
            )
            return jnp.where(keep, 1.0, 0.0).astype(bf16)

        masks, firsts = [], []
        for i in range(PLANES):
            stack = jnp.concatenate(
                [xa[b][i + a] for a in range(3) for b in range(3)]
                + [left[i], left[i + 1], left[i + 2], right[i], right[i + 2]],
                0,
            )
            first = silu_half(jnp.dot(w3[...], stack, preferred_element_type=f32)).astype(bf16)
            fbuf[slot, 128 * i : 128 * i + 128, :] = first
            firsts.append(first)
            row = group * PLANES + i
            masks.append(now * row_keep(row) + late * row_keep(row + PLANES))
        part_out[...] += jnp.dot(
            jnp.concatenate(firsts, 1), jnp.concatenate(masks, 0), preferred_element_type=f32
        )

    part_out[...] = jnp.zeros_like(part_out)

    @pl.loop(0, LAG, unroll=LAG)
    def _(k):
        stage1(k)

    @pl.loop(LAG, 2 * LAG, unroll=LAG)
    def _(k):
        stage2(k - LAG)
        stage1(k)

    for k in range(2):
        stage3(k)
        stage2(k + LAG)
        stage1(k + 2 * LAG)
        put_first(k).start()

    @pl.loop(2 * LAG + 2, steps)
    def _(k):
        put_first(k - 2 * LAG - 2).wait()
        stage3(k - 2 * LAG)
        stage2(k - LAG)
        stage1(k)
        put_first(k - 2 * LAG).start()

    @pl.loop(steps - LAG, steps)
    def _(k):
        put_first(k - LAG - 2).wait()
        stage3(k - LAG)
        stage2(k)
        put_first(k - LAG).start()

    @pl.loop(steps - LAG, steps)
    def _(k):
        put_first(k - 2).wait()
        stage3(k)
        put_first(k).start()

    ring_out[...] = jnp.zeros_like(ring_out)
    j = lax.broadcasted_iota(jnp.int32, (STRIDE, 128), 0)
    g = lax.broadcasted_iota(jnp.int32, (COLUMN, 128), 0)
    i = jnp.concatenate([g * PLANES + p for p in range(PLANES)], 0)
    live = jnp.concatenate([g < groups for p in range(PLANES)], 0)

    def put(n):
        return pltpu.make_async_copy(sbuf.at[n % 2], strips_out.at[n], sem.at[n % 2])

    @pl.loop(0, number)
    def _(n):
        q = order[n]
        r0, c0 = tabs[0, q], tabs[1, q]
        r1, c1 = r0 + patch - 1, c0 + patch - 1

        slot = n % 2

        @pl.when(n >= 2)
        def _():
            put(n - 2).wait()

        def add(value, weight):
            got = jnp.sum(jnp.where(weight, value.astype(f32), 0.0), 0, keepdims=True)
            ring_out[pl.ds(q, 1), :] += got

        for s, (r, height) in enumerate(((r0, (1, 2)), (r1, (0, 1)))):

            @pl.when((r >= TOP - 1) & (r <= TOP + tile_r))
            def _(s=s, r=r, height=height):
                total = None
                for a in height:
                    at = r + a - 1
                    plane = at % PLANES
                    start = plane // 4 * cells + FRONT + at // PLANES * STRIDE
                    for b in range(3):
                        x = cond_c[pl.ds(start + b - 1, STRIDE), :]
                        x = jnp.where((j + (b - 1) >= c0) & (j + (b - 1) <= c1), x, 0.0)
                        x = pltpu.roll(x, (128 - plane % 4 * 32) % 128, 1)[:, :24].astype(bf16)
                        term = jnp.dot(x, raw3[3 * a + b], preferred_element_type=f32)
                        total = term if total is None else total + term
                value = silu_half(0.5 * total)
                tail = jnp.zeros((STRIP - STRIDE, 128), f32)
                sbuf[slot, STRIP * s : STRIP * s + STRIP, :] = jnp.concatenate(
                    [value, tail], 0
                ).astype(bf16)
                value = value.astype(bf16)
                own = (r >= TOP) & (r < TOP + tile_r)
                add(value, own & (j >= c0) & (j <= c1) & (j >= HALO) & (j < HALO + tile_c))

        for s, (c, breadth) in enumerate(((c0, (1, 2)), (c1, (0, 1)))):

            @pl.when((c >= HALO - 1) & (c <= HALO + tile_c))
            def _(s=s, c=c, breadth=breadth):
                total = None
                for b in breadth:

                    def at(h, g_move, b=b):
                        start = h * cells + FRONT + c + b - 1 + g_move * STRIDE
                        return cond_c[pl.ds(start, COLUMN, stride=STRIDE), :]

                    halves = [at(0, 0), at(1, 0)]
                    planes = [at(1, -1)[:, 96:]]
                    planes += [
                        halves[p // 4][:, p % 4 * 32 : p % 4 * 32 + 32] for p in range(PLANES)
                    ]
                    planes += [at(0, 1)[:, :32]]
                    for a in range(3):
                        x = jnp.concatenate(planes[a : a + PLANES], 0)
                        inside = (i + (a - 1) >= r0) & (i + (a - 1) <= r1)
                        x = jnp.where(inside[:, :32], x, 0.0)[:, :24].astype(bf16)
                        term = jnp.dot(x, raw3[3 * a + b], preferred_element_type=f32)
                        total = term if total is None else total + term
                value = silu_half(0.5 * total).astype(bf16)
                lo = 2 * STRIP + PLANES * COLUMN * s
                sbuf[slot, lo : lo + PLANES * COLUMN, :] = value
                own = (c >= HALO) & (c < HALO + tile_c) & live
                add(value, own & (i > r0) & (i < r1) & (i >= TOP) & (i < TOP + tile_r))

        put(n).start()

    put_first(steps - 2).wait()
    put_first(steps - 1).wait()
    for back in (2, 1):

        @pl.when(number >= back)
        def _(back=back):
            put(number - back).wait()


def patch_kernel(
    rows, patch, tile_r, tile_c,
    order, tabs, noise, first, strips, lift, weight, mean, latent, middle, raw5,
    next_out, est_out,
    w5, m, acc, sbuf, keep_row, keep_col, wbuf, sem,
):
    size = lanes_of(rows)
    steps = size // STEP
    groups = rows // PLANES
    number = order[lift.shape[0]]
    spread_pair(raw5, w5, 0)

    def mixed(x, dim):
        return 0.5 * lax.dot_general(
            x, middle[...], (((dim,), (1,)), ((), ())), preferred_element_type=f32
        )
    high = 2 * STRIP
    tall = PLANES * COLUMN

    def fetch(n):
        return pltpu.make_async_copy(strips.at[n], sbuf.at[n % 2], sem.at[n % 2])

    @pl.when(number > 0)
    def _():
        fetch(0).start()

    @pl.loop(0, steps, unroll=2)
    def _(k):
        base = pl.multiple_of(k * STEP, 128)
        for i in range(PLANES):
            x = first[128 * i : 128 * i + 128, pl.ds(base, STEP)]
            m[pl.ds(base + i * size, STEP), :] = mixed(x, 0)

    acc[...] = jnp.zeros_like(acc)
    m[PLANES * size :, :] = jnp.zeros((TILE, 128), f32)
    j = lax.broadcasted_iota(jnp.int32, (STRIDE, 128), 0)
    g = lax.broadcasted_iota(jnp.int32, (COLUMN, 128), 0)
    lane = lax.broadcasted_iota(jnp.int32, (8, TILE), 1)
    ones = jnp.where(lax.broadcasted_iota(jnp.int32, (16, TILE), 0) >= 12, 1.0, 0.0)

    @pl.loop(0, number)
    def _(n):
        q = order[n]
        r0, c0 = tabs[0, q], tabs[1, q]
        r1, c1 = r0 + patch - 1, c0 + patch - 1
        slot = n % 2
        fetch(n).wait()

        @pl.when(n + 1 < number)
        def _():
            fetch(n + 1).start()

        half_lift = lift[pl.ds(q, 1), :]

        def row_ok(r):
            return (r >= TOP - 1) & (r <= TOP + tile_r)

        def col_ok(c):
            return (c >= HALO - 1) & (c <= HALO + tile_c)

        def row_at(r):
            return pl.ds(pl.multiple_of(r % PLANES * size + r // PLANES * STRIDE, 8), STRIDE)

        def col_at(c, i):
            return pl.ds(c + i * size, groups, stride=STRIDE)

        cols = ((0, c0 - 1, None), (1, c0, 0), (2, c1, 1), (3, c1 + 1, None))
        rws = ((0, r0 - 1, None), (1, r0, 0), (2, r1, 1), (3, r1 + 1, None))
        for s, c, source in cols:

            @pl.when(col_ok(c))
            def _(s=s, c=c, source=source):
                if source is not None:
                    strip = sbuf[slot, high + tall * source : high + tall * source + tall, :]
                    got = mixed(strip, 1)
                for i in range(PLANES):
                    keep_col[s, i, :groups, :] = m[col_at(c, i), :]
                    if source is None:
                        new = jnp.full((groups, 128), NEG, f32)
                    else:
                        row = g * PLANES + i
                        new = got[COLUMN * i : COLUMN * i + COLUMN]
                        new = jnp.where((row >= r0) & (row <= r1), new, NEG)[:groups]
                    m[col_at(c, i), :] = new

        for s, r, source in rws:

            @pl.when(row_ok(r))
            def _(s=s, r=r, source=source):
                keep_row[s, :, :] = m[row_at(r), :]
                if source is None:
                    m[row_at(r), :] = jnp.full((STRIDE, 128), NEG, f32)
                else:
                    strip = sbuf[slot, STRIP * source : STRIP * source + STRIP, :]
                    got = mixed(strip, 1)[:STRIDE]
                    m[row_at(r), :] = jnp.where((j >= c0) & (j <= c1), got, NEG)

        top = r0 // PLANES
        phase = r0 - top * PLANES
        move = top * STRIDE + c0
        shifts = (move, move + STRIDE, jnp.where(phase == 0, move - STRIDE, move))
        clo, chi = jnp.maximum(c0, HALO - 1), jnp.minimum(c1, HALO + tile_c)
        glo = jnp.maximum(r0, TOP - 1) // PLANES
        ghi = jnp.minimum(r1, TOP + tile_r) // PLANES

        @pl.loop((glo * STRIDE + clo) // TILE, (ghi * STRIDE + chi) // TILE + 1)
        def _(k):
            base = pl.multiple_of(k * TILE, 128)
            col_start = base % STRIDE
            col = lane + col_start
            for _ in range((TILE + STRIDE - 2) // STRIDE):
                col = jnp.where(col >= STRIDE, col - STRIDE, col)
            for b in range(3):
                inside = (col - (b - 1) >= c0) & (col - (b - 1) <= c1)
                for v, shift in enumerate(shifts):
                    source = base - shift - (b - 1) + WFRONT
                    rem = source % 128
                    count = TILE // 128
                    blocks = weight[pl.ds(source // 128, count + 1), :, :]
                    blocks = blocks.reshape(8 * count + 8, 128)
                    rolled = pltpu.roll(blocks, (128 - rem) % 128, 1)
                    here = lane[:, :128] < 128 - rem
                    got = jnp.concatenate(
                        [
                            jnp.where(here, rolled[8 * x : 8 * x + 8], rolled[8 * x + 8 : 8 * x + 16])
                            for x in range(count)
                        ],
                        1,
                    )
                    wbuf[8 * (3 * v + b) : 8 * (3 * v + b) + 8, :] = jnp.where(inside, got, 0.0)
            pairs = []
            for pair in range(PLANES // 2):
                halves = []
                for i in (2 * pair, 2 * pair + 1):
                    t = m[pl.ds(base + i * size, TILE), :] + half_lift
                    halves.append(silu_half(t).astype(bf16))
                pairs.append(jnp.concatenate(halves, 1))
            y = lax.dot_general(
                w5[...], jnp.concatenate(pairs, 0), (((1,), (1,)), ((), ())),
                preferred_element_type=f32,
            )
            parts = overlapped([y[:, TILE * x : TILE * x + TILE] for x in range(PLANES // 2)])
            for i in range(-1, PLANES + 1):
                block = parts[(i + 1) // 2][(i + 1) % 2 * 48 : (i + 1) % 2 * 48 + 48]
                if i < 0:
                    version = 1
                elif i == PLANES:
                    version = 2
                else:
                    version = jnp.where(phase <= i, 0, 1)
                line = (i - phase) % PLANES
                for b in range(3):
                    term = block[16 * b : 16 * b + 16]
                    if b == 1 and 0 <= i < PLANES:
                        term = term + ones
                    w = wbuf[pl.ds(8 * (3 * version + b) + line, 1), :]
                    row = 48 * (i + 1) + 16 * b
                    acc[row : row + 16, pl.ds(base + PAD, TILE)] += term * w

        for s, r, source in rws[::-1]:

            @pl.when(row_ok(r))
            def _(s=s, r=r):
                m[row_at(r), :] = keep_row[s, :, :]

        for s, c, source in cols[::-1]:

            @pl.when(col_ok(c))
            def _(s=s, c=c):
                for i in range(PLANES):
                    m[col_at(c, i), :] = keep_col[s, i, :groups, :]

    for k in range(tile_r // PLANES):
        start = (k + TOP // PLANES) * STRIDE + HALO
        whole = start // 128 * 128
        off = start - whole
        span = -(-(off + tile_c) // 128) * 128
        planes = combined(acc, whole, span)
        got = jnp.stack([p / (1.0 + p[12:13]) for p in planes], 0)[:, :, off : off + tile_c]
        got = jnp.swapaxes(got, 0, 1)[:12]
        base = mean[:, whole : whole + span].reshape(PLANES, 16, span)[:, :, off : off + tile_c]
        base = jnp.swapaxes(base, 0, 1)[4:]
        rows_at = slice(PLANES * k, PLANES * k + PLANES)
        scale_in, skip, scale_out = precondition(noise)
        lat = latent[:, rows_at, :]
        denoised = skip * lat + scale_out * got
        next_out[:, rows_at, :] = lat + (step_ratio - 1.0) * (lat - denoised)
        est_out[:, rows_at, :] = base + denoised


FAR = 1 << 20
WFRONT = 2048


def precondition(noise):
    level = jnp.full((1, 1, 1), noise[0], f32)
    spread = level * level + sigma_data * sigma_data
    root = jnp.sqrt(spread)
    return 1.0 / root, sigma_data * sigma_data / spread, level * sigma_data / root


def specs():
    return (
        pl.BlockSpec(memory_space=pltpu.SMEM),
        pl.BlockSpec(memory_space=pltpu.VMEM),
        pl.BlockSpec(memory_space=pl.ANY),
    )


def run_regress(fixed, entries, *args):
    size = lanes_of(fixed[0])
    smem, vmem, anyw = specs()
    cells = size + 2 * FRONT
    return pl.pallas_call(
        functools.partial(regress_kernel, *fixed),
        in_specs=[smem] * 2 + [vmem] * 6,
        out_specs=[anyw, vmem, vmem, vmem, anyw, smem],
        out_shape=[
            jax.ShapeDtypeStruct((PLANES * 128, size), bf16),
            jax.ShapeDtypeStruct((PLANES * 16, size), f32),
            jax.ShapeDtypeStruct((128, 128), f32),
            jax.ShapeDtypeStruct((entries, 128), f32),
            jax.ShapeDtypeStruct((entries, 2 * (STRIP + PLANES * COLUMN), 128), bf16),
            jax.ShapeDtypeStruct((entries + 1,), jnp.int32),
        ],
        scratch_shapes=[
            pltpu.VMEM((256, 192), bf16),
            pltpu.VMEM((192, 256), bf16),
            pltpu.VMEM((128, 224), bf16),
            pltpu.VMEM((48 * (PLANES + 2), size + 2 * PAD), f32),
            pltpu.VMEM((16 * PLANES, size + 2 * PAD), bf16),
            pltpu.VMEM((8 * PLANES, size + 2 * PAD), f32),
            pltpu.VMEM((2 * cells + COLUMN * STRIDE - size + STRIDE, 128), f32),
            pltpu.VMEM((2, PLANES * 128, STEP), bf16),
            pltpu.VMEM((2, 2 * (STRIP + PLANES * COLUMN), 128), bf16),
            pltpu.SemaphoreType.DMA((2,)),
            pltpu.SemaphoreType.DMA((2,)),
        ],
        compiler_params=pltpu.CompilerParams(vmem_limit_bytes=VMEM),
        name="regress",
    )(*args)


def run_patches(fixed, *args):
    rows = fixed[0]
    size = lanes_of(rows)
    smem, vmem, anyw = specs()
    return pl.pallas_call(
        functools.partial(patch_kernel, *fixed),
        in_specs=[smem] * 3 + [vmem, anyw] + [vmem] * 6,
        out_specs=[vmem] * 2,
        out_shape=[jax.ShapeDtypeStruct((12, fixed[2], fixed[3]), f32)] * 2,
        scratch_shapes=[
            pltpu.VMEM((192, 256), bf16),
            pltpu.VMEM((PLANES * size + TILE, 128), f32),
            pltpu.VMEM((48 * (PLANES + 2), size + 2 * PAD), f32),
            pltpu.VMEM((2, 2 * (STRIP + PLANES * COLUMN), 128), bf16),
            pltpu.VMEM((4, STRIDE, 128), f32),
            pltpu.VMEM((4, PLANES, COLUMN, 128), f32),
            pltpu.VMEM((72, TILE), f32),
            pltpu.SemaphoreType.DMA((2,)),
        ],
        compiler_params=pltpu.CompilerParams(vmem_limit_bytes=VMEM),
        name="patches",
    )(*args)


NEAR = [(di, dj) for di in range(-2, 3) for dj in range(-1, 2) if (di, dj) != (0, 0)]
MESH = pl.DeviceIdType.MESH


def neighbours(near, shape):
    me = (lax.axis_index("slab"), lax.axis_index("patch"))
    out = []
    for offset in near:
        at = tuple(a + d for a, d in zip(me, offset))
        there = (at[0] >= 0) & (at[0] < shape[0]) & (at[1] >= 0) & (at[1] < shape[1])
        out.append((there, at))
    return out


def greet(around):
    barrier = pltpu.get_barrier_semaphore()
    for there, at in around:

        @pl.when(there)
        def _(at=at):
            pl.semaphore_signal(barrier, inc=1, device_id=at, device_id_type=MESH)

    peers = jnp.int32(0)
    for there, at in around:
        peers = peers + there.astype(jnp.int32)
    pl.semaphore_wait(barrier, peers)


def pool_kernel(shape, per_slab, cells, part, ring, pool, lift, mine, got, send, recv):
    around = neighbours(NEAR, shape)
    greet(around)
    mine[...] = ring[...] + part[...].T[: 3 * per_slab]
    copies = []
    for x, (there, at) in enumerate(around):
        copy = pltpu.make_async_remote_copy(
            src_ref=mine, dst_ref=got.at[len(NEAR) - 1 - x],
            send_sem=send.at[x], recv_sem=recv.at[len(NEAR) - 1 - x],
            device_id=at, device_id_type=MESH,
        )
        copies.append(copy)

        @pl.when(there)
        def _(copy=copy):
            copy.start()

    lift[...] = mine[...]
    for x, (there, at) in enumerate(around):
        di = NEAR[x][0]

        @pl.when(there)
        def _(x=x, di=di):
            copies[len(NEAR) - 1 - x].wait_recv()
            for d in range(3):
                e = d - di
                if 0 <= e < 3:
                    lift[per_slab * d : per_slab * d + per_slab, :] += got[
                        x, per_slab * e : per_slab * e + per_slab, :
                    ]

    for x, (there, at) in enumerate(around):

        @pl.when(there)
        def _(x=x):
            copies[x].wait_send()

    lift[...] = 0.5 * lax.dot_general(
        lift[...] / cells, pool[...].astype(f32), (((1,), (1,)), ((), ())),
        precision=lax.Precision.HIGHEST, preferred_element_type=f32,
    )


SIDES = [(-1, 0), (1, 0), (0, -1), (0, 1), (-1, -1), (-1, 1), (1, -1), (1, 1)]


def frame_kernel(
    shape, per_slab, patch,
    noise, coarse, latent, table, move, ends, back,
    coarse_out, latent_out, tabs_out,
    both, framed, edge_rows, edge_cols, corners, strip, tables, send, recv,
):
    channels, tile_r, tile_c = latent.shape
    around = neighbours(SIDES, shape)
    there = [a[0] for a in around]
    scale_in = precondition(noise)[0]
    both[:channels, :, :] = coarse[...]
    both[channels:, :, :] = (scale_in * latent[...]).astype(bf16)
    greet(around)

    def last(d):
        return slice(0, 16) if d < 0 else slice(tile_r - 16, tile_r)

    def side(d):
        return slice(0, 128) if d < 0 else slice(tile_c - 128, tile_c)

    opposite = [SIDES.index((-a, -b)) for a, b in SIDES]
    copies = []

    def copy(x, source, target, slot):
        here = opposite[x]
        return pltpu.make_async_remote_copy(
            src_ref=source, dst_ref=target, send_sem=send.at[slot, x], recv_sem=recv.at[slot, here],
            device_id=around[x][1], device_id_type=MESH,
        )

    def begin(x, one):
        copies.append((x, one))

        @pl.when(there[x])
        def _():
            one.start()

    for x in (0, 1):
        begin(x, copy(x, both.at[:, last(SIDES[x][0]), :], edge_rows.at[opposite[x]], 0))
        begin(x, copy(x, table, tables.at[opposite[x]], 1))
    for x in range(4, 8):
        di, dj = SIDES[x]
        begin(x, copy(x, both.at[:, last(di), side(dj)], corners.at[opposite[x] - 4], 0))
    flat = both[...].reshape(2 * channels * tile_r, tile_c)
    strip[...] = lax.dot_general(
        ends[...], flat, (((1,), (1,)), ((), ())), preferred_element_type=f32
    )
    for x in (2, 3):
        begin(x, copy(x, strip, edge_cols.at[opposite[x] - 2], 0))

    @pl.loop(0, 2 * channels)
    def _(c):
        x = jnp.dot(both[c], move[...], preferred_element_type=f32)
        framed[c + c // channels * (16 - channels), TOP : TOP + tile_r, :] = x

    for x in range(8):

        @pl.when(jnp.logical_not(there[x]))
        def _(x=x):
            if x < 2:
                edge_rows[x] = jnp.zeros(edge_rows.shape[1:], bf16)
                tables[x] = jnp.zeros(tables.shape[1:], jnp.int32)
            elif x < 4:
                edge_cols[x - 2] = jnp.zeros(edge_cols.shape[1:], f32)
            else:
                corners[x - 4] = jnp.zeros(corners.shape[1:], bf16)

    for x, one in copies:

        @pl.when(there[x])
        def _(one=one):
            one.wait_send()

    for x, one in copies:

        @pl.when(there[opposite[x]])
        def _(one=one):
            one.wait_recv()

    for c in range(2 * channels):
        at = c + c // channels * (16 - channels)
        cols = jnp.concatenate(
            [edge_cols[x][:, tile_r * c : tile_r * c + tile_r] for x in range(2)], 0
        ).astype(bf16)
        framed[at, TOP : TOP + tile_r, :] += lax.dot_general(
            cols, back[256:272, :], (((0,), (0,)), ((), ())), preferred_element_type=f32
        )
        for x, rows_at in ((0, slice(0, TOP)), (1, slice(TOP + tile_r, 2 * TOP + tile_r))):
            x4 = 4 + 2 * x
            got = jnp.dot(edge_rows[x, c], move[...], preferred_element_type=f32)
            got += jnp.dot(corners[x4 - 4, c], back[:128, :], preferred_element_type=f32)
            got += jnp.dot(corners[x4 - 3, c], back[128:256, :], preferred_element_type=f32)
            framed[at, rows_at, :] = got[16 - TOP :] if x == 0 else got[:TOP]
    zero = jnp.zeros((16 - channels, tile_r + 2 * TOP, STRIDE), f32)
    framed[channels:16] = zero
    framed[16 + channels :] = zero
    groups = (tile_r + 2 * TOP) // PLANES
    parts = []
    for g in range(groups):
        block = framed[:, PLANES * g : PLANES * g + PLANES, :]
        parts.append(jnp.swapaxes(block, 0, 1))
    rest = coarse_out.shape[1] - PAD - groups * STRIDE
    for i in range(PLANES):
        row = jnp.concatenate(
            [jnp.zeros((32, PAD), f32)] + [p[i] for p in parts] + [jnp.zeros((32, rest), f32)], 1
        ).astype(bf16)
        coarse_out[16 * i : 16 * i + 16, :] = row[:16]
        latent_out[16 * i : 16 * i + 16, :] = row[16:]

    lane = lax.broadcasted_iota(jnp.int32, (8, 128), 1)
    got = jnp.where(lane < per_slab, tables[0], jnp.where(lane < 2 * per_slab, table[...], tables[1]))
    row0 = got[:1] - (lax.axis_index("slab") * tile_r - TOP)
    col0 = got[1:2] - (lax.axis_index("patch") * tile_c - HALO)
    live = (got[3:4] < got[2:3]) & (lane[:1] < 3 * per_slab)
    live = live & (row0 < TOP + tile_r) & (row0 + patch > TOP)
    live = live & (col0 < HALO + tile_c) & (col0 + patch > HALO)
    tabs_out[...] = jnp.concatenate(
        [jnp.where(live, row0, FAR), jnp.where(live, col0, FAR), lane[:6]], 0
    )


def run_frame(shape, per_slab, patch, tile, *args):
    channels, tile_r, tile_c = tile
    smem, vmem, anyw = specs()
    lanes = lanes_of(tile_r + 2 * TOP) + 2 * PAD
    return pl.pallas_call(
        functools.partial(frame_kernel, shape, per_slab, patch),
        in_specs=[smem] + [vmem] * 6,
        out_specs=[vmem] * 3,
        out_shape=[
            jax.ShapeDtypeStruct((PLANES * 16, lanes), bf16),
            jax.ShapeDtypeStruct((PLANES * 16, lanes), bf16),
            jax.ShapeDtypeStruct((8, 128), jnp.int32),
        ],
        scratch_shapes=[
            pltpu.VMEM((2 * channels, tile_r, tile_c), bf16),
            pltpu.VMEM((32, tile_r + 2 * TOP, STRIDE), f32),
            pltpu.VMEM((2, 2 * channels, 16, tile_c), bf16),
            pltpu.VMEM((2, 8, 2 * channels * tile_r), f32),
            pltpu.VMEM((4, 2 * channels, 16, 128), bf16),
            pltpu.VMEM((8, 2 * channels * tile_r), f32),
            pltpu.VMEM((2, 8, 128), jnp.int32),
            pltpu.SemaphoreType.DMA((2, 8)),
            pltpu.SemaphoreType.DMA((2, 8)),
        ],
        compiler_params=pltpu.CompilerParams(
            collective_id=2, has_side_effects=True, vmem_limit_bytes=VMEM
        ),
        name="frame",
    )(*args)


def run_pool(shape, per_slab, cells, *args):
    vmem = specs()[1]
    entries = 3 * per_slab
    return pl.pallas_call(
        functools.partial(pool_kernel, shape, per_slab, cells),
        in_specs=[vmem] * 3,
        out_specs=vmem,
        out_shape=jax.ShapeDtypeStruct((entries, 128), f32),
        scratch_shapes=[
            pltpu.VMEM((entries, 128), f32),
            pltpu.VMEM((len(NEAR), entries, 128), f32),
            pltpu.SemaphoreType.DMA((len(NEAR),)),
            pltpu.SemaphoreType.DMA((len(NEAR),)),
        ],
        compiler_params=pltpu.CompilerParams(collective_id=1, has_side_effects=True),
        name="pool",
    )(*args)


def frame_constants(tile_c):
    move = np.zeros((tile_c, STRIDE), np.float32)
    move[np.arange(tile_c), HALO + np.arange(tile_c)] = 1
    ends = np.zeros((8, tile_c), np.float32)
    back = np.zeros((272, STRIDE), np.float32)
    for x in range(HALO):
        ends[x, x] = 1
        ends[HALO + x, tile_c - HALO + x] = 1
        back[128 - HALO + x, x] = 1
        back[128 + x, HALO + tile_c + x] = 1
        back[256 + HALO + x, x] = 1
        back[264 + x, HALO + tile_c + x] = 1
    return tuple(jnp.asarray(a, bf16) for a in (move, ends, back))


def body(
    coarse, latent, noise_level, reg_first, reg_second, den_first, den_middle, den_pool, den_last,
    anchors, patch_count, patch_weight,
):
    tile_r, tile_c = latent.shape[1:]
    patch = patch_weight.shape[0]
    rows = tile_r + 2 * TOP
    slab = lax.axis_index("slab")
    column = lax.axis_index("patch")
    shape = (lax.axis_size("slab"), lax.axis_size("patch"))
    per_slab = anchors.shape[1]

    labels = np.arange(per_slab, dtype=np.int32)
    table = jnp.stack(
        [anchors[0, :, 0], anchors[0, :, 1], jnp.broadcast_to(patch_count, (per_slab,)), labels], 0
    )
    table = jnp.pad(jnp.tile(table, (1, 3)), ((0, 4), (0, 128 - 3 * per_slab)))
    coarse_flat, latent_flat, tabs = run_frame(
        shape, per_slab, patch, latent.shape,
        noise_level, coarse, latent, table, *frame_constants(tile_c),
    )

    top = TOP - slab * tile_r
    left = HALO - column * tile_c
    meta = jnp.stack([top, top + shape[0] * tile_r, left, left + shape[1] * tile_c])
    fixed = (rows, patch, tile_r, tile_c)
    first, mean, part, ring, strips, order = run_regress(
        fixed, 3 * per_slab,
        meta.astype(jnp.int32), tabs, coarse_flat, latent_flat, tabs,
        jnp.transpose(reg_first, (0, 2, 1)), reg_second, jnp.transpose(den_first, (0, 2, 1)),
    )

    lift = run_pool(shape, per_slab, patch * patch, part, ring, den_pool)

    weight = jnp.pad(patch_weight.astype(f32), ((0, 0), (0, STRIDE - patch)))
    weight = weight.reshape(patch // PLANES, PLANES, STRIDE).transpose(1, 0, 2)
    weight = weight.reshape(PLANES, patch // PLANES * STRIDE)
    end = -weight.shape[1] % 128
    weight = jnp.pad(weight, ((0, 0), (WFRONT, end + WFRONT)))
    weight = weight.reshape(PLANES, -1, 128).transpose(1, 0, 2)
    next_state, estimate = run_patches(
        fixed,
        order, tabs, noise_level, first, strips, lift, weight, mean, latent, den_middle, den_last,
    )
    return (next_state, estimate)


def solution(mesh):
    return jax.shard_map(
        body,
        mesh=mesh,
        in_specs=(
            P(None, "slab", "patch"), P(None, "slab", "patch"),
            P(), P(), P(), P(), P(), P(), P(),
            P("slab", None, None), P("slab"), P(),
        ),
        out_specs=(P(None, "slab", "patch"), P(None, "slab", "patch")),
        check_vma=False,
    )
```

```python
import functools

import jax
import jax.numpy as jnp
import numpy as np
from jax import lax
from jax.experimental import pallas as pl
from jax.experimental.pallas import tpu as pltpu
from jax.sharding import PartitionSpec as P

sigma_data = 0.5
step_ratio = 0.6

HALO = 4
TOP = 8
STRIDE = 264
STRIP = 272
PLANES = 8
PAD = 384
FRONT = 528
LAG = 3
STEP = 256
TILE = 512
COLUMN = 24
NEG = -1e30
VMEM = 60 * 1024 * 1024
f32, bf16 = jnp.float32, jnp.bfloat16


def lanes_of(rows):
    return -(-(rows // PLANES * STRIDE) // STEP) * STEP


def silu_half(t):
    return t + t * jnp.tanh(t)


def shifted(ref, base, step, depth):
    at = base + PAD
    edge = STRIDE // 128 * 128
    rest = STRIDE - edge
    mid = ref[:, pl.ds(at - 128, step + 256)]
    low = ref[(PLANES - 1) * depth :, pl.ds(at - edge - 128, step + 256)]
    high = ref[:depth, pl.ds(at + edge - 128, step + 256)]
    out = []
    for b in range(3):
        m = mid[:, 127 + b : 127 + b + step]
        rows = [low[:, 127 + b - rest : 127 + b - rest + step]]
        rows += [m[depth * i : depth * i + depth] for i in range(PLANES)]
        rows += [high[:, 127 + b + rest : 127 + b + rest + step]]
        out.append(rows)
    return out


def overlapped(parts):
    got = [parts[0][:96]]
    for a, b in zip(parts, parts[1:]):
        got.append(a[96:] + b[:96])
    return got + [parts[-1][96:]]


def combined(ref, base, step):
    at = base + PAD
    edge = STRIDE // 128 * 128
    rest = STRIDE - edge

    def columns(plane, start, move):
        total = None
        for b in range(3):
            row = (plane + 1) * 48 + b * 16
            block = ref[row : row + 16, pl.ds(start - 128, step + 256)]
            term = block[:, 127 + b + move : 127 + b + move + step]
            total = term if total is None else total + term
        return total

    planes = [columns(i, at, 0) for i in range(PLANES)]
    planes[-1] += columns(-1, at + edge, rest)
    planes[0] += columns(PLANES, at - edge, -rest)
    return planes


def taps_of(raw, lo, hi, count):
    parts = []
    for t in range(9):
        parts.append(0.5 * raw[t].astype(f32)[lo:hi])
        if hi - lo < count:
            parts.append(jnp.zeros((count - hi + lo, 128), f32))
    return parts


def gather_pair(raw, out):
    gap = [jnp.zeros((48, 128), f32)]
    parts = taps_of(raw, 0, raw.shape[1], 16)
    out[:128, :] = jnp.concatenate(parts + gap, 0).T.astype(bf16)
    out[128:, :] = jnp.concatenate(gap + parts, 0).T.astype(bf16)


def spread_pair(raw, out, front):
    zeros = [jnp.zeros((n, 128), f32) for n in (front, 16 - front - raw.shape[1]) if n]
    parts = []
    for a in (2, 1, 0):
        for b in range(3):
            taps = raw[3 * a + b].astype(f32)
            parts += [zeros[0], taps] if front else [taps, zeros[0]]
    gap = jnp.zeros((48, 128), f32)
    out[:, :128] = jnp.concatenate(parts + [gap], 0).astype(bf16)
    out[:, 128:] = jnp.concatenate([gap] + parts, 0).astype(bf16)


def regress_kernel(
    rows, patch, tile_r, tile_c,
    meta, tabs, coarse, latent, tabs_v, raw1, raw2, raw3,
    first_out, mean_out, part_out, ring_out, strips_out, order,
    w1, w2, w3, sums, cond_a, cond_b, cond_c, fbuf, sbuf, sem, fsem,
):
    size = lanes_of(rows)
    steps = size // STEP
    cells = size + 2 * FRONT
    groups = rows // PLANES
    row_lo, row_hi, col_lo, col_hi = meta[0], meta[1], meta[2], meta[3]
    gather_pair(raw1, w1)
    spread_pair(raw2, w2, 4)
    side = taps_of(raw3, 16, 24, 8)
    side = [side[t] for t in (0, 1, 3, 4, 6, 7, 2, 5, 8)] + [jnp.zeros((8, 128), f32)]
    w3[...] = jnp.concatenate(taps_of(raw3, 0, 16, 16) + side, 0).T.astype(bf16)

    def enlist(q, n):
        live = tabs[0, q] < FAR

        @pl.when(live)
        def _():
            order[n] = q

        return n + live.astype(jnp.int32)

    entries = ring_out.shape[0]
    number = lax.fori_loop(0, entries, enlist, jnp.int32(0))
    order[entries] = number
    for ref in (sums, cond_a, cond_b):
        ref[:, :PAD] = jnp.zeros((ref.shape[0], PAD), ref.dtype)
        ref[:, PAD + size :] = jnp.zeros((ref.shape[0], PAD), ref.dtype)
    cond_c[:FRONT, :] = jnp.zeros((FRONT, 128), f32)
    cond_c[FRONT + size : 2 * FRONT + size, :] = jnp.zeros((FRONT, 128), f32)
    cond_c[cells : cells + FRONT, :] = jnp.zeros((FRONT, 128), f32)
    cond_c[cells + FRONT + size :, :] = jnp.zeros((cond_c.shape[0] - cells - FRONT - size, 128), f32)

    def stage1(k):
        base = pl.multiple_of(k * STEP, 128)
        x = shifted(coarse, base, STEP, 16)
        group = base // STRIDE
        lane = lax.broadcasted_iota(jnp.int32, (PLANES, STEP), 1)
        later = (lane >= (group + 1) * STRIDE - base).astype(jnp.int32)
        col = lane + base - (group + later) * STRIDE
        row = (group + later) * PLANES + lax.broadcasted_iota(jnp.int32, (PLANES, STEP), 0)
        inside = (row >= row_lo) & (row < row_hi) & (col >= col_lo) & (col < col_hi)
        keep = jnp.where(inside, 1.0, 0.0)
        parts = []
        for pair in range(PLANES // 2):
            stack = jnp.concatenate(
                [x[b][2 * pair + r] for r in range(4) for b in range(3)], 0
            )
            h = silu_half(jnp.dot(w1[...], stack, preferred_element_type=f32))
            h = jnp.concatenate(
                [
                    h[:128] * keep[2 * pair : 2 * pair + 1],
                    h[128:] * keep[2 * pair + 1 : 2 * pair + 2],
                ],
                0,
            ).astype(bf16)
            parts.append(jnp.dot(w2[...], h, preferred_element_type=f32))
        sums[:, pl.ds(base + PAD, STEP)] = jnp.concatenate(overlapped(parts), 0)

    def stage2(k):
        base = pl.multiple_of(k * STEP, 128)
        means = combined(sums, base, STEP)
        lat = latent[:, pl.ds(base + PAD, STEP)].astype(f32)
        zero = jnp.zeros((8, STEP), f32)
        main, side, full = [], [], []
        for i, mean in enumerate(means):
            head = lat[16 * i : 16 * i + 8]
            mid = lat[16 * i + 8 : 16 * i + 16] + mean[:8]
            main += [head, mid]
            side.append(mean[8:])
            full += [head, mid, mean[8:], zero]
        mean_out[:, pl.ds(base, STEP)] = jnp.concatenate(means, 0)
        cond_a[:, pl.ds(base + PAD, STEP)] = jnp.concatenate(main, 0).astype(bf16)
        cond_b[:, pl.ds(base + PAD, STEP)] = jnp.concatenate(side, 0)
        for h in range(2):
            block = jnp.concatenate(full[16 * h : 16 * h + 16], 0)
            for j in range(STEP // 128):
                cond_c[pl.ds(base + h * cells + FRONT + 128 * j, 128), :] = block[
                    :, 128 * j : 128 * j + 128
                ].T

    def put_first(k):
        at = pl.ds(pl.multiple_of(k * STEP, 128), STEP)
        return pltpu.make_async_copy(fbuf.at[k % 2], first_out.at[:, at], fsem.at[k % 2])

    def stage3(k):
        slot = k % 2
        base = pl.multiple_of(k * STEP, 128)
        xa = shifted(cond_a, base, STEP, 16)
        xb = shifted(cond_b, base, STEP, 8)
        left = [
            jnp.concatenate([xb[0][i], xb[1][i]], 0).astype(bf16) for i in range(PLANES + 2)
        ]
        right = [
            jnp.concatenate([xb[2][i], xb[2][min(i + 1, PLANES + 1)]], 0).astype(bf16)
            for i in range(PLANES + 2)
        ]
        group = base // STRIDE
        lane = lax.broadcasted_iota(jnp.int32, (STEP, 128), 0)
        split = (group + 1) * STRIDE - base
        later = lane >= split
        col = lane + base - group * STRIDE - jnp.where(later, STRIDE, 0)
        r0b, c0b = tabs_v[:1], tabs_v[1:2]
        wanted = (
            (col > c0b) & (col < c0b + (patch - 1)) & (col >= HALO) & (col < HALO + tile_c)
        )
        now = jnp.where(wanted & (lane < split), 1.0, 0.0).astype(bf16)
        late = jnp.where(wanted & later, 1.0, 0.0).astype(bf16)

        def row_keep(row):
            keep = (
                (r0b < row) & (row < r0b + (patch - 1)) & (row >= TOP) & (row < TOP + tile_r)
            )
            return jnp.where(keep, 1.0, 0.0).astype(bf16)

        masks, firsts = [], []
        for i in range(PLANES):
            stack = jnp.concatenate(
                [xa[b][i + a] for a in range(3) for b in range(3)]
                + [left[i], left[i + 1], left[i + 2], right[i], right[i + 2]],
                0,
            )
            first = silu_half(jnp.dot(w3[...], stack, preferred_element_type=f32)).astype(bf16)
            fbuf[slot, 128 * i : 128 * i + 128, :] = first
            firsts.append(first)
            row = group * PLANES + i
            masks.append(now * row_keep(row) + late * row_keep(row + PLANES))
        part_out[...] += jnp.dot(
            jnp.concatenate(firsts, 1), jnp.concatenate(masks, 0), preferred_element_type=f32
        )

    part_out[...] = jnp.zeros_like(part_out)

    @pl.loop(0, LAG, unroll=LAG)
    def _(k):
        stage1(k)

    @pl.loop(LAG, 2 * LAG, unroll=LAG)
    def _(k):
        stage2(k - LAG)
        stage1(k)

    for k in range(2):
        stage3(k)
        stage2(k + LAG)
        stage1(k + 2 * LAG)
        put_first(k).start()

    @pl.loop(2 * LAG + 2, steps)
    def _(k):
        put_first(k - 2 * LAG - 2).wait()
        stage3(k - 2 * LAG)
        stage2(k - LAG)
        stage1(k)
        put_first(k - 2 * LAG).start()

    @pl.loop(steps - LAG, steps)
    def _(k):
        put_first(k - LAG - 2).wait()
        stage3(k - LAG)
        stage2(k)
        put_first(k - LAG).start()

    @pl.loop(steps - LAG, steps)
    def _(k):
        put_first(k - 2).wait()
        stage3(k)
        put_first(k).start()

    ring_out[...] = jnp.zeros_like(ring_out)
    j = lax.broadcasted_iota(jnp.int32, (STRIDE, 128), 0)
    g = lax.broadcasted_iota(jnp.int32, (COLUMN, 128), 0)
    i = jnp.concatenate([g * PLANES + p for p in range(PLANES)], 0)
    live = jnp.concatenate([g < groups for p in range(PLANES)], 0)

    def put(n):
        return pltpu.make_async_copy(sbuf.at[n % 2], strips_out.at[n], sem.at[n % 2])

    @pl.loop(0, number)
    def _(n):
        q = order[n]
        r0, c0 = tabs[0, q], tabs[1, q]
        r1, c1 = r0 + patch - 1, c0 + patch - 1

        slot = n % 2

        @pl.when(n >= 2)
        def _():
            put(n - 2).wait()

        def add(value, weight):
            got = jnp.sum(jnp.where(weight, value.astype(f32), 0.0), 0, keepdims=True)
            ring_out[pl.ds(q, 1), :] += got

        for s, (r, height) in enumerate(((r0, (1, 2)), (r1, (0, 1)))):

            @pl.when((r >= TOP - 1) & (r <= TOP + tile_r))
            def _(s=s, r=r, height=height):
                total = None
                for a in height:
                    at = r + a - 1
                    plane = at % PLANES
                    start = plane // 4 * cells + FRONT + at // PLANES * STRIDE
                    for b in range(3):
                        x = cond_c[pl.ds(start + b - 1, STRIDE), :]
                        x = jnp.where((j + (b - 1) >= c0) & (j + (b - 1) <= c1), x, 0.0)
                        x = pltpu.roll(x, (128 - plane % 4 * 32) % 128, 1)[:, :24].astype(bf16)
                        term = jnp.dot(x, raw3[3 * a + b], preferred_element_type=f32)
                        total = term if total is None else total + term
                value = silu_half(0.5 * total)
                tail = jnp.zeros((STRIP - STRIDE, 128), f32)
                sbuf[slot, STRIP * s : STRIP * s + STRIP, :] = jnp.concatenate(
                    [value, tail], 0
                ).astype(bf16)
                value = value.astype(bf16)
                own = (r >= TOP) & (r < TOP + tile_r)
                add(value, own & (j >= c0) & (j <= c1) & (j >= HALO) & (j < HALO + tile_c))

        for s, (c, breadth) in enumerate(((c0, (1, 2)), (c1, (0, 1)))):

            @pl.when((c >= HALO - 1) & (c <= HALO + tile_c))
            def _(s=s, c=c, breadth=breadth):
                total = None
                for b in breadth:

                    def at(h, g_move, b=b):
                        start = h * cells + FRONT + c + b - 1 + g_move * STRIDE
                        return cond_c[pl.ds(start, COLUMN, stride=STRIDE), :]

                    halves = [at(0, 0), at(1, 0)]
                    planes = [at(1, -1)[:, 96:]]
                    planes += [
                        halves[p // 4][:, p % 4 * 32 : p % 4 * 32 + 32] for p in range(PLANES)
                    ]
                    planes += [at(0, 1)[:, :32]]
                    for a in range(3):
                        x = jnp.concatenate(planes[a : a + PLANES], 0)
                        inside = (i + (a - 1) >= r0) & (i + (a - 1) <= r1)
                        x = jnp.where(inside[:, :32], x, 0.0)[:, :24].astype(bf16)
                        term = jnp.dot(x, raw3[3 * a + b], preferred_element_type=f32)
                        total = term if total is None else total + term
                value = silu_half(0.5 * total).astype(bf16)
                lo = 2 * STRIP + PLANES * COLUMN * s
                sbuf[slot, lo : lo + PLANES * COLUMN, :] = value
                own = (c >= HALO) & (c < HALO + tile_c) & live
                add(value, own & (i > r0) & (i < r1) & (i >= TOP) & (i < TOP + tile_r))

        put(n).start()

    put_first(steps - 2).wait()
    put_first(steps - 1).wait()
    for back in (2, 1):

        @pl.when(number >= back)
        def _(back=back):
            put(number - back).wait()


def patch_kernel(
    rows, patch, tile_r, tile_c,
    order, tabs, noise, first, strips, lift, weight, mean, latent, middle, raw5,
    next_out, est_out,
    w5, m, acc, sbuf, keep_row, keep_col, wbuf, sem,
):
    size = lanes_of(rows)
    steps = size // STEP
    groups = rows // PLANES
    number = order[lift.shape[0]]
    spread_pair(raw5, w5, 0)

    def mixed(x, dim):
        return 0.5 * lax.dot_general(
            x, middle[...], (((dim,), (1,)), ((), ())), preferred_element_type=f32
        )
    high = 2 * STRIP
    tall = PLANES * COLUMN

    def fetch(n):
        return pltpu.make_async_copy(strips.at[n], sbuf.at[n % 2], sem.at[n % 2])

    @pl.when(number > 0)
    def _():
        fetch(0).start()

    @pl.loop(0, steps, unroll=4)
    def _(k):
        base = pl.multiple_of(k * STEP, 128)
        for i in range(PLANES):
            x = first[128 * i : 128 * i + 128, pl.ds(base, STEP)]
            m[pl.ds(base + i * size, STEP), :] = mixed(x, 0)

    acc[...] = jnp.zeros_like(acc)
    m[PLANES * size :, :] = jnp.zeros((TILE, 128), f32)
    j = lax.broadcasted_iota(jnp.int32, (STRIDE, 128), 0)
    g = lax.broadcasted_iota(jnp.int32, (COLUMN, 128), 0)
    lane = lax.broadcasted_iota(jnp.int32, (8, TILE), 1)
    ones = jnp.where(lax.broadcasted_iota(jnp.int32, (16, TILE), 0) >= 12, 1.0, 0.0)

    @pl.loop(0, number)
    def _(n):
        q = order[n]
        r0, c0 = tabs[0, q], tabs[1, q]
        r1, c1 = r0 + patch - 1, c0 + patch - 1
        slot = n % 2
        fetch(n).wait()

        @pl.when(n + 1 < number)
        def _():
            fetch(n + 1).start()

        half_lift = lift[pl.ds(q, 1), :]

        def row_ok(r):
            return (r >= TOP - 1) & (r <= TOP + tile_r)

        def col_ok(c):
            return (c >= HALO - 1) & (c <= HALO + tile_c)

        def row_at(r):
            return pl.ds(pl.multiple_of(r % PLANES * size + r // PLANES * STRIDE, 8), STRIDE)

        def col_at(c, i):
            return pl.ds(c + i * size, groups, stride=STRIDE)

        cols = ((0, c0 - 1, None), (1, c0, 0), (2, c1, 1), (3, c1 + 1, None))
        rws = ((0, r0 - 1, None), (1, r0, 0), (2, r1, 1), (3, r1 + 1, None))
        for s, c, source in cols:

            @pl.when(col_ok(c))
            def _(s=s, c=c, source=source):
                if source is not None:
                    strip = sbuf[slot, high + tall * source : high + tall * source + tall, :]
                    got = mixed(strip, 1)
                for i in range(PLANES):
                    keep_col[s, i, :groups, :] = m[col_at(c, i), :]
                    if source is None:
                        new = jnp.full((groups, 128), NEG, f32)
                    else:
                        row = g * PLANES + i
                        new = got[COLUMN * i : COLUMN * i + COLUMN]
                        new = jnp.where((row >= r0) & (row <= r1), new, NEG)[:groups]
                    m[col_at(c, i), :] = new

        for s, r, source in rws:

            @pl.when(row_ok(r))
            def _(s=s, r=r, source=source):
                keep_row[s, :, :] = m[row_at(r), :]
                if source is None:
                    m[row_at(r), :] = jnp.full((STRIDE, 128), NEG, f32)
                else:
                    strip = sbuf[slot, STRIP * source : STRIP * source + STRIP, :]
                    got = mixed(strip, 1)[:STRIDE]
                    m[row_at(r), :] = jnp.where((j >= c0) & (j <= c1), got, NEG)

        top = r0 // PLANES
        phase = r0 - top * PLANES
        move = top * STRIDE + c0
        shifts = (move, move + STRIDE, jnp.where(phase == 0, move - STRIDE, move))
        clo, chi = jnp.maximum(c0, HALO - 1), jnp.minimum(c1, HALO + tile_c)
        glo = jnp.maximum(r0, TOP - 1) // PLANES
        ghi = jnp.minimum(r1, TOP + tile_r) // PLANES

        @pl.loop((glo * STRIDE + clo) // TILE, (ghi * STRIDE + chi) // TILE + 1)
        def _(k):
            base = pl.multiple_of(k * TILE, 128)
            col_start = base % STRIDE
            col = lane + col_start
            for _ in range((TILE + STRIDE - 2) // STRIDE):
                col = jnp.where(col >= STRIDE, col - STRIDE, col)
            for b in range(3):
                inside = (col - (b - 1) >= c0) & (col - (b - 1) <= c1)
                for v, shift in enumerate(shifts):
                    source = base - shift - (b - 1) + WFRONT
                    rem = source % 128
                    count = TILE // 128
                    blocks = weight[pl.ds(source // 128, count + 1), :, :]
                    blocks = blocks.reshape(8 * count + 8, 128)
                    rolled = pltpu.roll(blocks, (128 - rem) % 128, 1)
                    here = lane[:, :128] < 128 - rem
                    got = jnp.concatenate(
                        [
                            jnp.where(here, rolled[8 * x : 8 * x + 8], rolled[8 * x + 8 : 8 * x + 16])
                            for x in range(count)
                        ],
                        1,
                    )
                    got = jnp.where(inside, got, 0).astype(f32)
                    wbuf[8 * (3 * v + b) : 8 * (3 * v + b) + 8, :] = got
            pairs = []
            for pair in range(PLANES // 2):
                halves = []
                for i in (2 * pair, 2 * pair + 1):
                    t = m[pl.ds(base + i * size, TILE), :] + half_lift
                    halves.append(silu_half(t).astype(bf16))
                pairs.append(jnp.concatenate(halves, 1))
            y = lax.dot_general(
                w5[...], jnp.concatenate(pairs, 0), (((1,), (1,)), ((), ())),
                preferred_element_type=f32,
            )
            parts = overlapped([y[:, TILE * x : TILE * x + TILE] for x in range(PLANES // 2)])
            for i in range(-1, PLANES + 1):
                block = parts[(i + 1) // 2][(i + 1) % 2 * 48 : (i + 1) % 2 * 48 + 48]
                if i < 0:
                    version = 1
                elif i == PLANES:
                    version = 2
                else:
                    version = jnp.where(phase <= i, 0, 1)
                line = (i - phase) % PLANES
                for b in range(3):
                    term = block[16 * b : 16 * b + 16]
                    if b == 1 and 0 <= i < PLANES:
                        term = term + ones
                    w = wbuf[pl.ds(8 * (3 * version + b) + line, 1), :]
                    row = 48 * (i + 1) + 16 * b
                    acc[row : row + 16, pl.ds(base + PAD, TILE)] += term * w

        for s, r, source in rws[::-1]:

            @pl.when(row_ok(r))
            def _(s=s, r=r):
                m[row_at(r), :] = keep_row[s, :, :]

        for s, c, source in cols[::-1]:

            @pl.when(col_ok(c))
            def _(s=s, c=c):
                for i in range(PLANES):
                    m[col_at(c, i), :] = keep_col[s, i, :groups, :]

    for k in range(tile_r // PLANES):
        start = (k + TOP // PLANES) * STRIDE + HALO
        whole = start // 128 * 128
        off = start - whole
        span = -(-(off + tile_c) // 128) * 128
        planes = combined(acc, whole, span)
        got = jnp.stack([p / (1.0 + p[12:13]) for p in planes], 0)[:, :, off : off + tile_c]
        got = jnp.swapaxes(got, 0, 1)[:12]
        base = mean[:, whole : whole + span].reshape(PLANES, 16, span)[:, :, off : off + tile_c]
        base = jnp.swapaxes(base, 0, 1)[4:]
        rows_at = slice(PLANES * k, PLANES * k + PLANES)
        scale_in, skip, scale_out = precondition(noise)
        lat = latent[:, rows_at, :]
        denoised = skip * lat + scale_out * got
        next_out[:, rows_at, :] = lat + (step_ratio - 1.0) * (lat - denoised)
        est_out[:, rows_at, :] = base + denoised


FAR = 1 << 20
WFRONT = 2048


def precondition(noise):
    level = jnp.full((1, 1, 1), noise[0], f32)
    spread = level * level + sigma_data * sigma_data
    root = jnp.sqrt(spread)
    return 1.0 / root, sigma_data * sigma_data / spread, level * sigma_data / root


def specs():
    return (
        pl.BlockSpec(memory_space=pltpu.SMEM),
        pl.BlockSpec(memory_space=pltpu.VMEM),
        pl.BlockSpec(memory_space=pl.ANY),
    )


def run_regress(fixed, entries, *args):
    size = lanes_of(fixed[0])
    smem, vmem, anyw = specs()
    cells = size + 2 * FRONT
    return pl.pallas_call(
        functools.partial(regress_kernel, *fixed),
        in_specs=[smem] * 2 + [vmem] * 6,
        out_specs=[anyw, vmem, vmem, vmem, anyw, smem],
        out_shape=[
            jax.ShapeDtypeStruct((PLANES * 128, size), bf16),
            jax.ShapeDtypeStruct((PLANES * 16, size), f32),
            jax.ShapeDtypeStruct((128, 128), f32),
            jax.ShapeDtypeStruct((entries, 128), f32),
            jax.ShapeDtypeStruct((entries, 2 * (STRIP + PLANES * COLUMN), 128), bf16),
            jax.ShapeDtypeStruct((entries + 1,), jnp.int32),
        ],
        scratch_shapes=[
            pltpu.VMEM((256, 192), bf16),
            pltpu.VMEM((192, 256), bf16),
            pltpu.VMEM((128, 224), bf16),
            pltpu.VMEM((48 * (PLANES + 2), size + 2 * PAD), f32),
            pltpu.VMEM((16 * PLANES, size + 2 * PAD), bf16),
            pltpu.VMEM((8 * PLANES, size + 2 * PAD), f32),
            pltpu.VMEM((2 * cells + COLUMN * STRIDE - size + STRIDE, 128), f32),
            pltpu.VMEM((2, PLANES * 128, STEP), bf16),
            pltpu.VMEM((2, 2 * (STRIP + PLANES * COLUMN), 128), bf16),
            pltpu.SemaphoreType.DMA((2,)),
            pltpu.SemaphoreType.DMA((2,)),
        ],
        compiler_params=pltpu.CompilerParams(vmem_limit_bytes=VMEM),
        name="regress",
    )(*args)


def run_patches(fixed, *args):
    rows = fixed[0]
    size = lanes_of(rows)
    smem, vmem, anyw = specs()
    return pl.pallas_call(
        functools.partial(patch_kernel, *fixed),
        in_specs=[smem] * 3 + [vmem, anyw] + [vmem] * 6,
        out_specs=[vmem] * 2,
        out_shape=[jax.ShapeDtypeStruct((12, fixed[2], fixed[3]), f32)] * 2,
        scratch_shapes=[
            pltpu.VMEM((192, 256), bf16),
            pltpu.VMEM((PLANES * size + TILE, 128), f32),
            pltpu.VMEM((48 * (PLANES + 2), size + 2 * PAD), f32),
            pltpu.VMEM((2, 2 * (STRIP + PLANES * COLUMN), 128), bf16),
            pltpu.VMEM((4, STRIDE, 128), f32),
            pltpu.VMEM((4, PLANES, COLUMN, 128), f32),
            pltpu.VMEM((72, TILE), f32),
            pltpu.SemaphoreType.DMA((2,)),
        ],
        compiler_params=pltpu.CompilerParams(vmem_limit_bytes=VMEM),
        name="patches",
    )(*args)


NEAR = [(di, dj) for di in range(-2, 3) for dj in range(-1, 2) if (di, dj) != (0, 0)]
MESH = pl.DeviceIdType.MESH


def neighbours(near, shape):
    me = (lax.axis_index("slab"), lax.axis_index("patch"))
    out = []
    for offset in near:
        at = tuple(a + d for a, d in zip(me, offset))
        there = (at[0] >= 0) & (at[0] < shape[0]) & (at[1] >= 0) & (at[1] < shape[1])
        out.append((there, at))
    return out


def greet(around):
    barrier = pltpu.get_barrier_semaphore()
    for there, at in around:

        @pl.when(there)
        def _(at=at):
            pl.semaphore_signal(barrier, inc=1, device_id=at, device_id_type=MESH)

    peers = jnp.int32(0)
    for there, at in around:
        peers = peers + there.astype(jnp.int32)
    pl.semaphore_wait(barrier, peers)


def pool_kernel(shape, per_slab, cells, part, ring, pool, lift, mine, got, send, recv):
    around = neighbours(NEAR, shape)
    greet(around)
    mine[...] = ring[...] + part[...].T[: 3 * per_slab]
    copies = []
    for x, (there, at) in enumerate(around):
        copy = pltpu.make_async_remote_copy(
            src_ref=mine, dst_ref=got.at[len(NEAR) - 1 - x],
            send_sem=send.at[x], recv_sem=recv.at[len(NEAR) - 1 - x],
            device_id=at, device_id_type=MESH,
        )
        copies.append(copy)

        @pl.when(there)
        def _(copy=copy):
            copy.start()

    lift[...] = mine[...]
    for x, (there, at) in enumerate(around):
        di = NEAR[x][0]

        @pl.when(there)
        def _(x=x, di=di):
            copies[len(NEAR) - 1 - x].wait_recv()
            for d in range(3):
                e = d - di
                if 0 <= e < 3:
                    lift[per_slab * d : per_slab * d + per_slab, :] += got[
                        x, per_slab * e : per_slab * e + per_slab, :
                    ]

    for x, (there, at) in enumerate(around):

        @pl.when(there)
        def _(x=x):
            copies[x].wait_send()

    lift[...] = 0.5 * lax.dot_general(
        lift[...] / cells, pool[...].astype(f32), (((1,), (1,)), ((), ())),
        precision=lax.Precision.HIGHEST, preferred_element_type=f32,
    )


SIDES = [(-1, 0), (1, 0), (0, -1), (0, 1), (-1, -1), (-1, 1), (1, -1), (1, 1)]


def frame_kernel(
    shape, per_slab, patch,
    noise, coarse, latent, table, move, ends, back,
    coarse_out, latent_out, tabs_out,
    both, framed, edge_rows, edge_cols, corners, strip, tables, send, recv,
):
    channels, tile_r, tile_c = latent.shape
    around = neighbours(SIDES, shape)
    there = [a[0] for a in around]
    scale_in = precondition(noise)[0]
    both[:channels, :, :] = coarse[...]
    both[channels:, :, :] = (scale_in * latent[...]).astype(bf16)
    greet(around)

    def last(d):
        return slice(0, 16) if d < 0 else slice(tile_r - 16, tile_r)

    def side(d):
        return slice(0, 128) if d < 0 else slice(tile_c - 128, tile_c)

    opposite = [SIDES.index((-a, -b)) for a, b in SIDES]
    copies = []

    def copy(x, source, target, slot):
        here = opposite[x]
        return pltpu.make_async_remote_copy(
            src_ref=source, dst_ref=target, send_sem=send.at[slot, x], recv_sem=recv.at[slot, here],
            device_id=around[x][1], device_id_type=MESH,
        )

    def begin(x, one):
        copies.append((x, one))

        @pl.when(there[x])
        def _():
            one.start()

    for x in (0, 1):
        begin(x, copy(x, both.at[:, last(SIDES[x][0]), :], edge_rows.at[opposite[x]], 0))
        begin(x, copy(x, table, tables.at[opposite[x]], 1))
    for x in range(4, 8):
        di, dj = SIDES[x]
        begin(x, copy(x, both.at[:, last(di), side(dj)], corners.at[opposite[x] - 4], 0))
    flat = both[...].reshape(2 * channels * tile_r, tile_c)
    strip[...] = lax.dot_general(
        ends[...], flat, (((1,), (1,)), ((), ())), preferred_element_type=f32
    )
    for x in (2, 3):
        begin(x, copy(x, strip, edge_cols.at[opposite[x] - 2], 0))

    @pl.loop(0, 2 * channels)
    def _(c):
        x = jnp.dot(both[c], move[...], preferred_element_type=f32)
        framed[c + c // channels * (16 - channels), TOP : TOP + tile_r, :] = x

    for x in range(8):

        @pl.when(jnp.logical_not(there[x]))
        def _(x=x):
            if x < 2:
                edge_rows[x] = jnp.zeros(edge_rows.shape[1:], bf16)
                tables[x] = jnp.zeros(tables.shape[1:], jnp.int32)
            elif x < 4:
                edge_cols[x - 2] = jnp.zeros(edge_cols.shape[1:], f32)
            else:
                corners[x - 4] = jnp.zeros(corners.shape[1:], bf16)

    for x, one in copies:

        @pl.when(there[x])
        def _(one=one):
            one.wait_send()

    for x, one in copies:

        @pl.when(there[opposite[x]])
        def _(one=one):
            one.wait_recv()

    for c in range(2 * channels):
        at = c + c // channels * (16 - channels)
        cols = jnp.concatenate(
            [edge_cols[x][:, tile_r * c : tile_r * c + tile_r] for x in range(2)], 0
        ).astype(bf16)
        framed[at, TOP : TOP + tile_r, :] += lax.dot_general(
            cols, back[256:272, :], (((0,), (0,)), ((), ())), preferred_element_type=f32
        )
        for x, rows_at in ((0, slice(0, TOP)), (1, slice(TOP + tile_r, 2 * TOP + tile_r))):
            x4 = 4 + 2 * x
            got = jnp.dot(edge_rows[x, c], move[...], preferred_element_type=f32)
            got += jnp.dot(corners[x4 - 4, c], back[:128, :], preferred_element_type=f32)
            got += jnp.dot(corners[x4 - 3, c], back[128:256, :], preferred_element_type=f32)
            framed[at, rows_at, :] = got[16 - TOP :] if x == 0 else got[:TOP]
    zero = jnp.zeros((16 - channels, tile_r + 2 * TOP, STRIDE), f32)
    framed[channels:16] = zero
    framed[16 + channels :] = zero
    groups = (tile_r + 2 * TOP) // PLANES
    parts = []
    for g in range(groups):
        block = framed[:, PLANES * g : PLANES * g + PLANES, :]
        parts.append(jnp.swapaxes(block, 0, 1))
    rest = coarse_out.shape[1] - PAD - groups * STRIDE
    for i in range(PLANES):
        row = jnp.concatenate(
            [jnp.zeros((32, PAD), f32)] + [p[i] for p in parts] + [jnp.zeros((32, rest), f32)], 1
        ).astype(bf16)
        coarse_out[16 * i : 16 * i + 16, :] = row[:16]
        latent_out[16 * i : 16 * i + 16, :] = row[16:]

    lane = lax.broadcasted_iota(jnp.int32, (8, 128), 1)
    got = jnp.where(lane < per_slab, tables[0], jnp.where(lane < 2 * per_slab, table[...], tables[1]))
    row0 = got[:1] - (lax.axis_index("slab") * tile_r - TOP)
    col0 = got[1:2] - (lax.axis_index("patch") * tile_c - HALO)
    live = (got[3:4] < got[2:3]) & (lane[:1] < 3 * per_slab)
    live = live & (row0 < TOP + tile_r) & (row0 + patch > TOP)
    live = live & (col0 < HALO + tile_c) & (col0 + patch > HALO)
    tabs_out[...] = jnp.concatenate(
        [jnp.where(live, row0, FAR), jnp.where(live, col0, FAR), lane[:6]], 0
    )


def run_frame(shape, per_slab, patch, tile, *args):
    channels, tile_r, tile_c = tile
    smem, vmem, anyw = specs()
    lanes = lanes_of(tile_r + 2 * TOP) + 2 * PAD
    return pl.pallas_call(
        functools.partial(frame_kernel, shape, per_slab, patch),
        in_specs=[smem] + [vmem] * 6,
        out_specs=[vmem] * 3,
        out_shape=[
            jax.ShapeDtypeStruct((PLANES * 16, lanes), bf16),
            jax.ShapeDtypeStruct((PLANES * 16, lanes), bf16),
            jax.ShapeDtypeStruct((8, 128), jnp.int32),
        ],
        scratch_shapes=[
            pltpu.VMEM((2 * channels, tile_r, tile_c), bf16),
            pltpu.VMEM((32, tile_r + 2 * TOP, STRIDE), f32),
            pltpu.VMEM((2, 2 * channels, 16, tile_c), bf16),
            pltpu.VMEM((2, 8, 2 * channels * tile_r), f32),
            pltpu.VMEM((4, 2 * channels, 16, 128), bf16),
            pltpu.VMEM((8, 2 * channels * tile_r), f32),
            pltpu.VMEM((2, 8, 128), jnp.int32),
            pltpu.SemaphoreType.DMA((2, 8)),
            pltpu.SemaphoreType.DMA((2, 8)),
        ],
        compiler_params=pltpu.CompilerParams(
            collective_id=2, has_side_effects=True, vmem_limit_bytes=VMEM
        ),
        name="frame",
    )(*args)


def run_pool(shape, per_slab, cells, *args):
    vmem = specs()[1]
    entries = 3 * per_slab
    return pl.pallas_call(
        functools.partial(pool_kernel, shape, per_slab, cells),
        in_specs=[vmem] * 3,
        out_specs=vmem,
        out_shape=jax.ShapeDtypeStruct((entries, 128), f32),
        scratch_shapes=[
            pltpu.VMEM((entries, 128), f32),
            pltpu.VMEM((len(NEAR), entries, 128), f32),
            pltpu.SemaphoreType.DMA((len(NEAR),)),
            pltpu.SemaphoreType.DMA((len(NEAR),)),
        ],
        compiler_params=pltpu.CompilerParams(collective_id=1, has_side_effects=True),
        name="pool",
    )(*args)


def frame_constants(tile_c):
    move = np.zeros((tile_c, STRIDE), np.float32)
    move[np.arange(tile_c), HALO + np.arange(tile_c)] = 1
    ends = np.zeros((8, tile_c), np.float32)
    back = np.zeros((272, STRIDE), np.float32)
    for x in range(HALO):
        ends[x, x] = 1
        ends[HALO + x, tile_c - HALO + x] = 1
        back[128 - HALO + x, x] = 1
        back[128 + x, HALO + tile_c + x] = 1
        back[256 + HALO + x, x] = 1
        back[264 + x, HALO + tile_c + x] = 1
    return tuple(jnp.asarray(a, bf16) for a in (move, ends, back))


def body(
    coarse, latent, noise_level, reg_first, reg_second, den_first, den_middle, den_pool, den_last,
    anchors, patch_count, patch_weight,
):
    tile_r, tile_c = latent.shape[1:]
    patch = patch_weight.shape[0]
    rows = tile_r + 2 * TOP
    slab = lax.axis_index("slab")
    column = lax.axis_index("patch")
    shape = (lax.axis_size("slab"), lax.axis_size("patch"))
    per_slab = anchors.shape[1]

    labels = np.arange(per_slab, dtype=np.int32)
    table = jnp.stack(
        [anchors[0, :, 0], anchors[0, :, 1], jnp.broadcast_to(patch_count, (per_slab,)), labels], 0
    )
    table = jnp.pad(jnp.tile(table, (1, 3)), ((0, 4), (0, 128 - 3 * per_slab)))
    coarse_flat, latent_flat, tabs = run_frame(
        shape, per_slab, patch, latent.shape,
        noise_level, coarse, latent, table, *frame_constants(tile_c),
    )

    top = TOP - slab * tile_r
    left = HALO - column * tile_c
    meta = jnp.stack([top, top + shape[0] * tile_r, left, left + shape[1] * tile_c])
    fixed = (rows, patch, tile_r, tile_c)
    first, mean, part, ring, strips, order = run_regress(
        fixed, 3 * per_slab,
        meta.astype(jnp.int32), tabs, coarse_flat, latent_flat, tabs,
        jnp.transpose(reg_first, (0, 2, 1)), reg_second, jnp.transpose(den_first, (0, 2, 1)),
    )

    lift = run_pool(shape, per_slab, patch * patch, part, ring, den_pool)

    weight = jnp.pad(patch_weight, ((0, 0), (0, STRIDE - patch)))
    weight = weight.reshape(patch // PLANES, PLANES, STRIDE).transpose(1, 0, 2)
    weight = weight.reshape(PLANES, patch // PLANES * STRIDE)
    end = -weight.shape[1] % 128
    weight = jnp.pad(weight, ((0, 0), (WFRONT, end + WFRONT)))
    weight = weight.reshape(PLANES, -1, 128).transpose(1, 0, 2)
    next_state, estimate = run_patches(
        fixed,
        order, tabs, noise_level, first, strips, lift, weight, mean, latent, den_middle, den_last,
    )
    return (next_state, estimate)


def solution(mesh):
    return jax.shard_map(
        body,
        mesh=mesh,
        in_specs=(
            P(None, "slab", "patch"), P(None, "slab", "patch"),
            P(), P(), P(), P(), P(), P(), P(),
            P("slab", None, None), P("slab"), P(),
        ),
        out_specs=(P(None, "slab", "patch"), P(None, "slab", "patch")),
        check_vma=False,
    )
```

```python
import functools

import jax
import jax.numpy as jnp
import numpy as np
from jax import lax
from jax.experimental import pallas as pl
from jax.experimental.pallas import tpu as pltpu
from jax.sharding import PartitionSpec as P

sigma_data = 0.5
step_ratio = 0.6

HALO = 4
TOP = 8
STRIDE = 264
STRIP = 272
PLANES = 8
PAD = 384
FRONT = 528
LAG = 3
STEP = 256
TILE = 512
COLUMN = 24
NEG = -1e30
VMEM = 60 * 1024 * 1024
f32, bf16 = jnp.float32, jnp.bfloat16


def lanes_of(rows):
    return -(-(rows // PLANES * STRIDE) // STEP) * STEP


def silu_half(t):
    return t + t * jnp.tanh(t)


def shifted(ref, base, step, depth):
    at = base + PAD
    edge = STRIDE // 128 * 128
    rest = STRIDE - edge
    mid = ref[:, pl.ds(at - 128, step + 256)]
    low = ref[(PLANES - 1) * depth :, pl.ds(at - edge - 128, step + 256)]
    high = ref[:depth, pl.ds(at + edge - 128, step + 256)]
    out = []
    for b in range(3):
        m = mid[:, 127 + b : 127 + b + step]
        rows = [low[:, 127 + b - rest : 127 + b - rest + step]]
        rows += [m[depth * i : depth * i + depth] for i in range(PLANES)]
        rows += [high[:, 127 + b + rest : 127 + b + rest + step]]
        out.append(rows)
    return out


def overlapped(parts):
    got = [parts[0][:96]]
    for a, b in zip(parts, parts[1:]):
        got.append(a[96:] + b[:96])
    return got + [parts[-1][96:]]


def combined(ref, base, step):
    at = base + PAD
    edge = STRIDE // 128 * 128
    rest = STRIDE - edge

    def columns(plane, start, move):
        total = None
        for b in range(3):
            row = (plane + 1) * 48 + b * 16
            block = ref[row : row + 16, pl.ds(start - 128, step + 256)]
            term = block[:, 127 + b + move : 127 + b + move + step]
            total = term if total is None else total + term
        return total

    planes = [columns(i, at, 0) for i in range(PLANES)]
    planes[-1] += columns(-1, at + edge, rest)
    planes[0] += columns(PLANES, at - edge, -rest)
    return planes


def taps_of(raw, lo, hi, count):
    parts = []
    for t in range(9):
        parts.append(0.5 * raw[t].astype(f32)[lo:hi])
        if hi - lo < count:
            parts.append(jnp.zeros((count - hi + lo, 128), f32))
    return parts


def gather_pair(raw, out):
    gap = [jnp.zeros((48, 128), f32)]
    parts = taps_of(raw, 0, raw.shape[1], 16)
    out[:128, :] = jnp.concatenate(parts + gap, 0).T.astype(bf16)
    out[128:, :] = jnp.concatenate(gap + parts, 0).T.astype(bf16)


def spread_pair(raw, out, front):
    zeros = [jnp.zeros((n, 128), f32) for n in (front, 16 - front - raw.shape[1]) if n]
    parts = []
    for a in (2, 1, 0):
        for b in range(3):
            taps = raw[3 * a + b].astype(f32)
            parts += [zeros[0], taps] if front else [taps, zeros[0]]
    gap = jnp.zeros((48, 128), f32)
    out[:, :128] = jnp.concatenate(parts + [gap], 0).astype(bf16)
    out[:, 128:] = jnp.concatenate([gap] + parts, 0).astype(bf16)


def regress_kernel(
    rows, patch, tile_r, tile_c,
    meta, tabs, coarse, latent, tabs_v, raw1, raw2, raw3,
    first_out, mean_out, part_out, ring_out, strips_out, order,
    w1, w2, w3, sums, cond_a, cond_b, cond_c, fbuf, sbuf, sem, fsem,
):
    size = lanes_of(rows)
    steps = size // STEP
    cells = size + 2 * FRONT
    groups = rows // PLANES
    row_lo, row_hi, col_lo, col_hi = meta[0], meta[1], meta[2], meta[3]
    gather_pair(raw1, w1)
    spread_pair(raw2, w2, 4)
    side = taps_of(raw3, 16, 24, 8)
    side = [side[t] for t in (0, 1, 3, 4, 6, 7, 2, 5, 8)] + [jnp.zeros((8, 128), f32)]
    w3[...] = jnp.concatenate(taps_of(raw3, 0, 16, 16) + side, 0).T.astype(bf16)

    def enlist(q, n):
        live = tabs[0, q] < FAR

        @pl.when(live)
        def _():
            order[n] = q

        return n + live.astype(jnp.int32)

    entries = ring_out.shape[0]
    number = lax.fori_loop(0, entries, enlist, jnp.int32(0))
    order[entries] = number
    for ref in (sums, cond_a, cond_b):
        ref[:, :PAD] = jnp.zeros((ref.shape[0], PAD), ref.dtype)
        ref[:, PAD + size :] = jnp.zeros((ref.shape[0], PAD), ref.dtype)
    cond_c[:FRONT, :] = jnp.zeros((FRONT, 128), f32)
    cond_c[FRONT + size : 2 * FRONT + size, :] = jnp.zeros((FRONT, 128), f32)
    cond_c[cells : cells + FRONT, :] = jnp.zeros((FRONT, 128), f32)
    cond_c[cells + FRONT + size :, :] = jnp.zeros((cond_c.shape[0] - cells - FRONT - size, 128), f32)

    def stage1(k):
        base = pl.multiple_of(k * STEP, 128)
        x = shifted(coarse, base, STEP, 16)
        group = base // STRIDE
        lane = lax.broadcasted_iota(jnp.int32, (PLANES, STEP), 1)
        later = (lane >= (group + 1) * STRIDE - base).astype(jnp.int32)
        col = lane + base - (group + later) * STRIDE
        row = (group + later) * PLANES + lax.broadcasted_iota(jnp.int32, (PLANES, STEP), 0)
        inside = (row >= row_lo) & (row < row_hi) & (col >= col_lo) & (col < col_hi)
        keep = jnp.where(inside, 1.0, 0.0)
        parts = []
        for pair in range(PLANES // 2):
            stack = jnp.concatenate(
                [x[b][2 * pair + r] for r in range(4) for b in range(3)], 0
            )
            h = silu_half(jnp.dot(w1[...], stack, preferred_element_type=f32))
            h = jnp.concatenate(
                [
                    h[:128] * keep[2 * pair : 2 * pair + 1],
                    h[128:] * keep[2 * pair + 1 : 2 * pair + 2],
                ],
                0,
            ).astype(bf16)
            parts.append(jnp.dot(w2[...], h, preferred_element_type=f32))
        sums[:, pl.ds(base + PAD, STEP)] = jnp.concatenate(overlapped(parts), 0)

    def stage2(k):
        base = pl.multiple_of(k * STEP, 128)
        means = combined(sums, base, STEP)
        lat = latent[:, pl.ds(base + PAD, STEP)].astype(f32)
        zero = jnp.zeros((8, STEP), f32)
        main, side, full = [], [], []
        for i, mean in enumerate(means):
            head = lat[16 * i : 16 * i + 8]
            mid = lat[16 * i + 8 : 16 * i + 16] + mean[:8]
            main += [head, mid]
            side.append(mean[8:])
            full += [head, mid, mean[8:], zero]
        mean_out[:, pl.ds(base, STEP)] = jnp.concatenate(means, 0)
        cond_a[:, pl.ds(base + PAD, STEP)] = jnp.concatenate(main, 0).astype(bf16)
        cond_b[:, pl.ds(base + PAD, STEP)] = jnp.concatenate(side, 0)
        for h in range(2):
            block = jnp.concatenate(full[16 * h : 16 * h + 16], 0)
            for j in range(STEP // 128):
                cond_c[pl.ds(base + h * cells + FRONT + 128 * j, 128), :] = block[
                    :, 128 * j : 128 * j + 128
                ].T

    def put_first(k):
        at = pl.ds(pl.multiple_of(k * STEP, 128), STEP)
        return pltpu.make_async_copy(fbuf.at[k % 2], first_out.at[:, at], fsem.at[k % 2])

    def stage3(k):
        slot = k % 2
        base = pl.multiple_of(k * STEP, 128)
        xa = shifted(cond_a, base, STEP, 16)
        xb = shifted(cond_b, base, STEP, 8)
        left = [
            jnp.concatenate([xb[0][i], xb[1][i]], 0).astype(bf16) for i in range(PLANES + 2)
        ]
        right = [
            jnp.concatenate([xb[2][i], xb[2][min(i + 1, PLANES + 1)]], 0).astype(bf16)
            for i in range(PLANES + 2)
        ]
        group = base // STRIDE
        lane = lax.broadcasted_iota(jnp.int32, (STEP, 128), 0)
        split = (group + 1) * STRIDE - base
        later = lane >= split
        col = lane + base - group * STRIDE - jnp.where(later, STRIDE, 0)
        r0b, c0b = tabs_v[:1], tabs_v[1:2]
        wanted = (
            (col > c0b) & (col < c0b + (patch - 1)) & (col >= HALO) & (col < HALO + tile_c)
        )
        now = jnp.where(wanted & (lane < split), 1.0, 0.0).astype(bf16)
        late = jnp.where(wanted & later, 1.0, 0.0).astype(bf16)

        def row_keep(row):
            keep = (
                (r0b < row) & (row < r0b + (patch - 1)) & (row >= TOP) & (row < TOP + tile_r)
            )
            return jnp.where(keep, 1.0, 0.0).astype(bf16)

        masks, firsts = [], []
        for i in range(PLANES):
            stack = jnp.concatenate(
                [xa[b][i + a] for a in range(3) for b in range(3)]
                + [left[i], left[i + 1], left[i + 2], right[i], right[i + 2]],
                0,
            )
            first = silu_half(jnp.dot(w3[...], stack, preferred_element_type=f32)).astype(bf16)
            fbuf[slot, 128 * i : 128 * i + 128, :] = first
            firsts.append(first)
            row = group * PLANES + i
            masks.append(now * row_keep(row) + late * row_keep(row + PLANES))
        part_out[...] += jnp.dot(
            jnp.concatenate(firsts, 1), jnp.concatenate(masks, 0), preferred_element_type=f32
        )

    part_out[...] = jnp.zeros_like(part_out)

    @pl.loop(0, LAG, unroll=LAG)
    def _(k):
        stage1(k)

    @pl.loop(LAG, 2 * LAG, unroll=LAG)
    def _(k):
        stage2(k - LAG)
        stage1(k)

    for k in range(2):
        stage3(k)
        stage2(k + LAG)
        stage1(k + 2 * LAG)
        put_first(k).start()

    @pl.loop(2 * LAG + 2, steps)
    def _(k):
        put_first(k - 2 * LAG - 2).wait()
        stage3(k - 2 * LAG)
        stage2(k - LAG)
        stage1(k)
        put_first(k - 2 * LAG).start()

    @pl.loop(steps - LAG, steps, unroll=LAG)
    def _(k):
        put_first(k - LAG - 2).wait()
        stage3(k - LAG)
        stage2(k)
        put_first(k - LAG).start()

    @pl.loop(steps - LAG, steps, unroll=LAG)
    def _(k):
        put_first(k - 2).wait()
        stage3(k)
        put_first(k).start()

    ring_out[...] = jnp.zeros_like(ring_out)
    j = lax.broadcasted_iota(jnp.int32, (STRIDE, 128), 0)
    g = lax.broadcasted_iota(jnp.int32, (COLUMN, 128), 0)
    i = jnp.concatenate([g * PLANES + p for p in range(PLANES)], 0)
    live = jnp.concatenate([g < groups for p in range(PLANES)], 0)

    def put(n):
        return pltpu.make_async_copy(sbuf.at[n % 2], strips_out.at[n], sem.at[n % 2])

    @pl.loop(0, number)
    def _(n):
        q = order[n]
        r0, c0 = tabs[0, q], tabs[1, q]
        r1, c1 = r0 + patch - 1, c0 + patch - 1

        slot = n % 2

        @pl.when(n >= 2)
        def _():
            put(n - 2).wait()

        def add(value, weight):
            got = jnp.sum(jnp.where(weight, value.astype(f32), 0.0), 0, keepdims=True)
            ring_out[pl.ds(q, 1), :] += got

        for s, (r, height) in enumerate(((r0, (1, 2)), (r1, (0, 1)))):

            @pl.when((r >= TOP - 1) & (r <= TOP + tile_r))
            def _(s=s, r=r, height=height):
                total = None
                for a in height:
                    at = r + a - 1
                    plane = at % PLANES
                    start = plane // 4 * cells + FRONT + at // PLANES * STRIDE
                    for b in range(3):
                        x = cond_c[pl.ds(start + b - 1, STRIDE), :]
                        x = jnp.where((j + (b - 1) >= c0) & (j + (b - 1) <= c1), x, 0.0)
                        x = pltpu.roll(x, (128 - plane % 4 * 32) % 128, 1)[:, :24].astype(bf16)
                        term = jnp.dot(x, raw3[3 * a + b], preferred_element_type=f32)
                        total = term if total is None else total + term
                value = silu_half(0.5 * total)
                tail = jnp.zeros((STRIP - STRIDE, 128), f32)
                sbuf[slot, STRIP * s : STRIP * s + STRIP, :] = jnp.concatenate(
                    [value, tail], 0
                ).astype(bf16)
                value = value.astype(bf16)
                own = (r >= TOP) & (r < TOP + tile_r)
                add(value, own & (j >= c0) & (j <= c1) & (j >= HALO) & (j < HALO + tile_c))

        for s, (c, breadth) in enumerate(((c0, (1, 2)), (c1, (0, 1)))):

            @pl.when((c >= HALO - 1) & (c <= HALO + tile_c))
            def _(s=s, c=c, breadth=breadth):
                total = None
                for b in breadth:

                    def at(h, g_move, b=b):
                        start = h * cells + FRONT + c + b - 1 + g_move * STRIDE
                        return cond_c[pl.ds(start, COLUMN, stride=STRIDE), :]

                    halves = [at(0, 0), at(1, 0)]
                    planes = [at(1, -1)[:, 96:]]
                    planes += [
                        halves[p // 4][:, p % 4 * 32 : p % 4 * 32 + 32] for p in range(PLANES)
                    ]
                    planes += [at(0, 1)[:, :32]]
                    for a in range(3):
                        x = jnp.concatenate(planes[a : a + PLANES], 0)
                        inside = (i + (a - 1) >= r0) & (i + (a - 1) <= r1)
                        x = jnp.where(inside[:, :32], x, 0.0)[:, :24].astype(bf16)
                        term = jnp.dot(x, raw3[3 * a + b], preferred_element_type=f32)
                        total = term if total is None else total + term
                value = silu_half(0.5 * total).astype(bf16)
                lo = 2 * STRIP + PLANES * COLUMN * s
                sbuf[slot, lo : lo + PLANES * COLUMN, :] = value
                own = (c >= HALO) & (c < HALO + tile_c) & live
                add(value, own & (i > r0) & (i < r1) & (i >= TOP) & (i < TOP + tile_r))

        put(n).start()

    put_first(steps - 2).wait()
    put_first(steps - 1).wait()
    for back in (2, 1):

        @pl.when(number >= back)
        def _(back=back):
            put(number - back).wait()


def patch_kernel(
    rows, patch, tile_r, tile_c,
    order, tabs, noise, first, strips, lift, weight, mean, latent, middle, raw5,
    next_out, est_out,
    w5, m, acc, sbuf, keep_row, keep_col, wbuf, sem,
):
    size = lanes_of(rows)
    steps = size // STEP
    groups = rows // PLANES
    number = order[lift.shape[0]]
    spread_pair(raw5, w5, 0)

    def mixed(x, dim):
        return 0.5 * lax.dot_general(
            x, middle[...], (((dim,), (1,)), ((), ())), preferred_element_type=f32
        )
    high = 2 * STRIP
    tall = PLANES * COLUMN

    def fetch(n):
        return pltpu.make_async_copy(strips.at[n], sbuf.at[n % 2], sem.at[n % 2])

    @pl.when(number > 0)
    def _():
        fetch(0).start()

    @pl.loop(0, steps, unroll=4)
    def _(k):
        base = pl.multiple_of(k * STEP, 128)
        for i in range(PLANES):
            x = first[128 * i : 128 * i + 128, pl.ds(base, STEP)]
            m[pl.ds(base + i * size, STEP), :] = mixed(x, 0)

    acc[...] = jnp.zeros_like(acc)
    m[PLANES * size :, :] = jnp.zeros((TILE, 128), f32)
    j = lax.broadcasted_iota(jnp.int32, (STRIDE, 128), 0)
    g = lax.broadcasted_iota(jnp.int32, (COLUMN, 128), 0)
    lane = lax.broadcasted_iota(jnp.int32, (8, TILE), 1)
    ones = jnp.where(lax.broadcasted_iota(jnp.int32, (16, TILE), 0) >= 12, 1.0, 0.0)

    @pl.loop(0, number)
    def _(n):
        q = order[n]
        r0, c0 = tabs[0, q], tabs[1, q]
        r1, c1 = r0 + patch - 1, c0 + patch - 1
        slot = n % 2
        fetch(n).wait()

        @pl.when(n + 1 < number)
        def _():
            fetch(n + 1).start()

        half_lift = lift[pl.ds(q, 1), :]

        def row_ok(r):
            return (r >= TOP - 1) & (r <= TOP + tile_r)

        def col_ok(c):
            return (c >= HALO - 1) & (c <= HALO + tile_c)

        def row_at(r):
            return pl.ds(pl.multiple_of(r % PLANES * size + r // PLANES * STRIDE, 8), STRIDE)

        def col_at(c, i):
            return pl.ds(c + i * size, groups, stride=STRIDE)

        cols = ((0, c0 - 1, None), (1, c0, 0), (2, c1, 1), (3, c1 + 1, None))
        rws = ((0, r0 - 1, None), (1, r0, 0), (2, r1, 1), (3, r1 + 1, None))
        for s, c, source in cols:

            @pl.when(col_ok(c))
            def _(s=s, c=c, source=source):
                if source is not None:
                    strip = sbuf[slot, high + tall * source : high + tall * source + tall, :]
                    got = mixed(strip, 1)
                for i in range(PLANES):
                    keep_col[s, i, :groups, :] = m[col_at(c, i), :]
                    if source is None:
                        new = jnp.full((groups, 128), NEG, f32)
                    else:
                        row = g * PLANES + i
                        new = got[COLUMN * i : COLUMN * i + COLUMN]
                        new = jnp.where((row >= r0) & (row <= r1), new, NEG)[:groups]
                    m[col_at(c, i), :] = new

        for s, r, source in rws:

            @pl.when(row_ok(r))
            def _(s=s, r=r, source=source):
                keep_row[s, :, :] = m[row_at(r), :]
                if source is None:
                    m[row_at(r), :] = jnp.full((STRIDE, 128), NEG, f32)
                else:
                    strip = sbuf[slot, STRIP * source : STRIP * source + STRIP, :]
                    got = mixed(strip, 1)[:STRIDE]
                    m[row_at(r), :] = jnp.where((j >= c0) & (j <= c1), got, NEG)

        top = r0 // PLANES
        phase = r0 - top * PLANES
        move = top * STRIDE + c0
        shifts = (move, move + STRIDE, jnp.where(phase == 0, move - STRIDE, move))
        clo, chi = jnp.maximum(c0, HALO - 1), jnp.minimum(c1, HALO + tile_c)
        glo = jnp.maximum(r0, TOP - 1) // PLANES
        ghi = jnp.minimum(r1, TOP + tile_r) // PLANES

        @pl.loop((glo * STRIDE + clo) // TILE, (ghi * STRIDE + chi) // TILE + 1)
        def _(k):
            base = pl.multiple_of(k * TILE, 128)
            col_start = base % STRIDE
            col = lane + col_start
            for _ in range((TILE + STRIDE - 2) // STRIDE):
                col = jnp.where(col >= STRIDE, col - STRIDE, col)
            for b in range(3):
                inside = (col - (b - 1) >= c0) & (col - (b - 1) <= c1)
                for v, shift in enumerate(shifts):
                    source = base - shift - (b - 1) + WFRONT
                    rem = source % 128
                    count = TILE // 128
                    blocks = weight[pl.ds(source // 128, count + 1), :, :]
                    blocks = blocks.reshape(8 * count + 8, 128)
                    rolled = pltpu.roll(blocks, (128 - rem) % 128, 1)
                    here = lane[:, :128] < 128 - rem
                    got = jnp.concatenate(
                        [
                            jnp.where(here, rolled[8 * x : 8 * x + 8], rolled[8 * x + 8 : 8 * x + 16])
                            for x in range(count)
                        ],
                        1,
                    )
                    got = jnp.where(inside, got, 0).astype(f32)
                    wbuf[8 * (3 * v + b) : 8 * (3 * v + b) + 8, :] = got
            pairs = []
            for pair in range(PLANES // 2):
                halves = []
                for i in (2 * pair, 2 * pair + 1):
                    t = m[pl.ds(base + i * size, TILE), :] + half_lift
                    halves.append(silu_half(t).astype(bf16))
                pairs.append(jnp.concatenate(halves, 1))
            y = lax.dot_general(
                w5[...], jnp.concatenate(pairs, 0), (((1,), (1,)), ((), ())),
                preferred_element_type=f32,
            )
            parts = overlapped([y[:, TILE * x : TILE * x + TILE] for x in range(PLANES // 2)])
            for i in range(-1, PLANES + 1):
                block = parts[(i + 1) // 2][(i + 1) % 2 * 48 : (i + 1) % 2 * 48 + 48]
                if i < 0:
                    version = 1
                elif i == PLANES:
                    version = 2
                else:
                    version = jnp.where(phase <= i, 0, 1)
                line = (i - phase) % PLANES
                for b in range(3):
                    term = block[16 * b : 16 * b + 16]
                    if b == 1 and 0 <= i < PLANES:
                        term = term + ones
                    w = wbuf[pl.ds(8 * (3 * version + b) + line, 1), :]
                    row = 48 * (i + 1) + 16 * b
                    acc[row : row + 16, pl.ds(base + PAD, TILE)] += term * w

        for s, r, source in rws[::-1]:

            @pl.when(row_ok(r))
            def _(s=s, r=r):
                m[row_at(r), :] = keep_row[s, :, :]

        for s, c, source in cols[::-1]:

            @pl.when(col_ok(c))
            def _(s=s, c=c):
                for i in range(PLANES):
                    m[col_at(c, i), :] = keep_col[s, i, :groups, :]

    for k in range(tile_r // PLANES):
        start = (k + TOP // PLANES) * STRIDE + HALO
        whole = start // 128 * 128
        off = start - whole
        span = -(-(off + tile_c) // 128) * 128
        planes = combined(acc, whole, span)
        got = jnp.stack([p / (1.0 + p[12:13]) for p in planes], 0)[:, :, off : off + tile_c]
        got = jnp.swapaxes(got, 0, 1)[:12]
        base = mean[:, whole : whole + span].reshape(PLANES, 16, span)[:, :, off : off + tile_c]
        base = jnp.swapaxes(base, 0, 1)[4:]
        rows_at = slice(PLANES * k, PLANES * k + PLANES)
        scale_in, skip, scale_out = precondition(noise)
        lat = latent[:, rows_at, :]
        denoised = skip * lat + scale_out * got
        next_out[:, rows_at, :] = lat + (step_ratio - 1.0) * (lat - denoised)
        est_out[:, rows_at, :] = base + denoised


FAR = 1 << 20
WFRONT = 2048


def precondition(noise):
    level = jnp.full((1, 1, 1), noise[0], f32)
    spread = level * level + sigma_data * sigma_data
    root = jnp.sqrt(spread)
    return 1.0 / root, sigma_data * sigma_data / spread, level * sigma_data / root


def specs():
    return (
        pl.BlockSpec(memory_space=pltpu.SMEM),
        pl.BlockSpec(memory_space=pltpu.VMEM),
        pl.BlockSpec(memory_space=pl.ANY),
    )


def run_regress(fixed, entries, *args):
    size = lanes_of(fixed[0])
    smem, vmem, anyw = specs()
    cells = size + 2 * FRONT
    return pl.pallas_call(
        functools.partial(regress_kernel, *fixed),
        in_specs=[smem] * 2 + [vmem] * 6,
        out_specs=[anyw, vmem, vmem, vmem, anyw, smem],
        out_shape=[
            jax.ShapeDtypeStruct((PLANES * 128, size), bf16),
            jax.ShapeDtypeStruct((PLANES * 16, size), f32),
            jax.ShapeDtypeStruct((128, 128), f32),
            jax.ShapeDtypeStruct((entries, 128), f32),
            jax.ShapeDtypeStruct((entries, 2 * (STRIP + PLANES * COLUMN), 128), bf16),
            jax.ShapeDtypeStruct((entries + 1,), jnp.int32),
        ],
        scratch_shapes=[
            pltpu.VMEM((256, 192), bf16),
            pltpu.VMEM((192, 256), bf16),
            pltpu.VMEM((128, 224), bf16),
            pltpu.VMEM((48 * (PLANES + 2), size + 2 * PAD), f32),
            pltpu.VMEM((16 * PLANES, size + 2 * PAD), bf16),
            pltpu.VMEM((8 * PLANES, size + 2 * PAD), f32),
            pltpu.VMEM((2 * cells + COLUMN * STRIDE - size + STRIDE, 128), f32),
            pltpu.VMEM((2, PLANES * 128, STEP), bf16),
            pltpu.VMEM((2, 2 * (STRIP + PLANES * COLUMN), 128), bf16),
            pltpu.SemaphoreType.DMA((2,)),
            pltpu.SemaphoreType.DMA((2,)),
        ],
        compiler_params=pltpu.CompilerParams(vmem_limit_bytes=VMEM),
        name="regress",
    )(*args)


def run_patches(fixed, *args):
    rows = fixed[0]
    size = lanes_of(rows)
    smem, vmem, anyw = specs()
    return pl.pallas_call(
        functools.partial(patch_kernel, *fixed),
        in_specs=[smem] * 3 + [vmem, anyw] + [vmem] * 6,
        out_specs=[vmem] * 2,
        out_shape=[jax.ShapeDtypeStruct((12, fixed[2], fixed[3]), f32)] * 2,
        scratch_shapes=[
            pltpu.VMEM((192, 256), bf16),
            pltpu.VMEM((PLANES * size + TILE, 128), f32),
            pltpu.VMEM((48 * (PLANES + 2), size + 2 * PAD), f32),
            pltpu.VMEM((2, 2 * (STRIP + PLANES * COLUMN), 128), bf16),
            pltpu.VMEM((4, STRIDE, 128), f32),
            pltpu.VMEM((4, PLANES, COLUMN, 128), f32),
            pltpu.VMEM((72, TILE), f32),
            pltpu.SemaphoreType.DMA((2,)),
        ],
        compiler_params=pltpu.CompilerParams(vmem_limit_bytes=VMEM),
        name="patches",
    )(*args)


NEAR = [(di, dj) for di in range(-2, 3) for dj in range(-1, 2) if (di, dj) != (0, 0)]
MESH = pl.DeviceIdType.MESH


def neighbours(near, shape):
    me = (lax.axis_index("slab"), lax.axis_index("patch"))
    out = []
    for offset in near:
        at = tuple(a + d for a, d in zip(me, offset))
        there = (at[0] >= 0) & (at[0] < shape[0]) & (at[1] >= 0) & (at[1] < shape[1])
        out.append((there, at))
    return out


def greet(around):
    barrier = pltpu.get_barrier_semaphore()
    for there, at in around:

        @pl.when(there)
        def _(at=at):
            pl.semaphore_signal(barrier, inc=1, device_id=at, device_id_type=MESH)

    peers = jnp.int32(0)
    for there, at in around:
        peers = peers + there.astype(jnp.int32)
    pl.semaphore_wait(barrier, peers)


def pool_kernel(shape, per_slab, cells, part, ring, pool, lift, mine, got, send, recv):
    around = neighbours(NEAR, shape)
    greet(around)
    mine[...] = ring[...] + part[...].T[: 3 * per_slab]
    copies = []
    for x, (there, at) in enumerate(around):
        copy = pltpu.make_async_remote_copy(
            src_ref=mine, dst_ref=got.at[len(NEAR) - 1 - x],
            send_sem=send.at[x], recv_sem=recv.at[len(NEAR) - 1 - x],
            device_id=at, device_id_type=MESH,
        )
        copies.append(copy)

        @pl.when(there)
        def _(copy=copy):
            copy.start()

    lift[...] = mine[...]
    for x, (there, at) in enumerate(around):
        di = NEAR[x][0]

        @pl.when(there)
        def _(x=x, di=di):
            copies[len(NEAR) - 1 - x].wait_recv()
            for d in range(3):
                e = d - di
                if 0 <= e < 3:
                    lift[per_slab * d : per_slab * d + per_slab, :] += got[
                        x, per_slab * e : per_slab * e + per_slab, :
                    ]

    for x, (there, at) in enumerate(around):

        @pl.when(there)
        def _(x=x):
            copies[x].wait_send()

    lift[...] = 0.5 * lax.dot_general(
        lift[...] / cells, pool[...].astype(f32), (((1,), (1,)), ((), ())),
        precision=lax.Precision.HIGHEST, preferred_element_type=f32,
    )


SIDES = [(-1, 0), (1, 0), (0, -1), (0, 1), (-1, -1), (-1, 1), (1, -1), (1, 1)]


def frame_kernel(
    shape, per_slab, patch,
    noise, coarse, latent, table, move, ends, back,
    coarse_out, latent_out, tabs_out,
    both, framed, edge_rows, edge_cols, corners, strip, tables, send, recv,
):
    channels, tile_r, tile_c = latent.shape
    around = neighbours(SIDES, shape)
    there = [a[0] for a in around]
    scale_in = precondition(noise)[0]
    both[:channels, :, :] = coarse[...]
    both[channels:, :, :] = (scale_in * latent[...]).astype(bf16)
    greet(around)

    def last(d):
        return slice(0, 16) if d < 0 else slice(tile_r - 16, tile_r)

    def side(d):
        return slice(0, 128) if d < 0 else slice(tile_c - 128, tile_c)

    opposite = [SIDES.index((-a, -b)) for a, b in SIDES]
    copies = []

    def copy(x, source, target, slot):
        here = opposite[x]
        return pltpu.make_async_remote_copy(
            src_ref=source, dst_ref=target, send_sem=send.at[slot, x], recv_sem=recv.at[slot, here],
            device_id=around[x][1], device_id_type=MESH,
        )

    def begin(x, one):
        copies.append((x, one))

        @pl.when(there[x])
        def _():
            one.start()

    for x in (0, 1):
        begin(x, copy(x, both.at[:, last(SIDES[x][0]), :], edge_rows.at[opposite[x]], 0))
        begin(x, copy(x, table, tables.at[opposite[x]], 1))
    for x in range(4, 8):
        di, dj = SIDES[x]
        begin(x, copy(x, both.at[:, last(di), side(dj)], corners.at[opposite[x] - 4], 0))
    flat = both[...].reshape(2 * channels * tile_r, tile_c)
    strip[...] = lax.dot_general(
        ends[...], flat, (((1,), (1,)), ((), ())), preferred_element_type=f32
    )
    for x in (2, 3):
        begin(x, copy(x, strip, edge_cols.at[opposite[x] - 2], 0))

    @pl.loop(0, 2 * channels)
    def _(c):
        x = jnp.dot(both[c], move[...], preferred_element_type=f32)
        framed[c + c // channels * (16 - channels), TOP : TOP + tile_r, :] = x

    for x in range(8):

        @pl.when(jnp.logical_not(there[x]))
        def _(x=x):
            if x < 2:
                edge_rows[x] = jnp.zeros(edge_rows.shape[1:], bf16)
                tables[x] = jnp.zeros(tables.shape[1:], jnp.int32)
            elif x < 4:
                edge_cols[x - 2] = jnp.zeros(edge_cols.shape[1:], f32)
            else:
                corners[x - 4] = jnp.zeros(corners.shape[1:], bf16)

    for x, one in copies:

        @pl.when(there[x])
        def _(one=one):
            one.wait_send()

    for x, one in copies:

        @pl.when(there[opposite[x]])
        def _(one=one):
            one.wait_recv()

    for c in range(2 * channels):
        at = c + c // channels * (16 - channels)
        cols = jnp.concatenate(
            [edge_cols[x][:, tile_r * c : tile_r * c + tile_r] for x in range(2)], 0
        ).astype(bf16)
        framed[at, TOP : TOP + tile_r, :] += lax.dot_general(
            cols, back[256:272, :], (((0,), (0,)), ((), ())), preferred_element_type=f32
        )
        for x, rows_at in ((0, slice(0, TOP)), (1, slice(TOP + tile_r, 2 * TOP + tile_r))):
            x4 = 4 + 2 * x
            got = jnp.dot(edge_rows[x, c], move[...], preferred_element_type=f32)
            got += jnp.dot(corners[x4 - 4, c], back[:128, :], preferred_element_type=f32)
            got += jnp.dot(corners[x4 - 3, c], back[128:256, :], preferred_element_type=f32)
            framed[at, rows_at, :] = got[16 - TOP :] if x == 0 else got[:TOP]
    zero = jnp.zeros((16 - channels, tile_r + 2 * TOP, STRIDE), f32)
    framed[channels:16] = zero
    framed[16 + channels :] = zero
    groups = (tile_r + 2 * TOP) // PLANES
    parts = []
    for g in range(groups):
        block = framed[:, PLANES * g : PLANES * g + PLANES, :]
        parts.append(jnp.swapaxes(block, 0, 1))
    rest = coarse_out.shape[1] - PAD - groups * STRIDE
    for i in range(PLANES):
        row = jnp.concatenate(
            [jnp.zeros((32, PAD), f32)] + [p[i] for p in parts] + [jnp.zeros((32, rest), f32)], 1
        ).astype(bf16)
        coarse_out[16 * i : 16 * i + 16, :] = row[:16]
        latent_out[16 * i : 16 * i + 16, :] = row[16:]

    lane = lax.broadcasted_iota(jnp.int32, (8, 128), 1)
    got = jnp.where(lane < per_slab, tables[0], jnp.where(lane < 2 * per_slab, table[...], tables[1]))
    row0 = got[:1] - (lax.axis_index("slab") * tile_r - TOP)
    col0 = got[1:2] - (lax.axis_index("patch") * tile_c - HALO)
    live = (got[3:4] < got[2:3]) & (lane[:1] < 3 * per_slab)
    live = live & (row0 < TOP + tile_r) & (row0 + patch > TOP)
    live = live & (col0 < HALO + tile_c) & (col0 + patch > HALO)
    tabs_out[...] = jnp.concatenate(
        [jnp.where(live, row0, FAR), jnp.where(live, col0, FAR), lane[:6]], 0
    )


def run_frame(shape, per_slab, patch, tile, *args):
    channels, tile_r, tile_c = tile
    smem, vmem, anyw = specs()
    lanes = lanes_of(tile_r + 2 * TOP) + 2 * PAD
    return pl.pallas_call(
        functools.partial(frame_kernel, shape, per_slab, patch),
        in_specs=[smem] + [vmem] * 6,
        out_specs=[vmem] * 3,
        out_shape=[
            jax.ShapeDtypeStruct((PLANES * 16, lanes), bf16),
            jax.ShapeDtypeStruct((PLANES * 16, lanes), bf16),
            jax.ShapeDtypeStruct((8, 128), jnp.int32),
        ],
        scratch_shapes=[
            pltpu.VMEM((2 * channels, tile_r, tile_c), bf16),
            pltpu.VMEM((32, tile_r + 2 * TOP, STRIDE), f32),
            pltpu.VMEM((2, 2 * channels, 16, tile_c), bf16),
            pltpu.VMEM((2, 8, 2 * channels * tile_r), f32),
            pltpu.VMEM((4, 2 * channels, 16, 128), bf16),
            pltpu.VMEM((8, 2 * channels * tile_r), f32),
            pltpu.VMEM((2, 8, 128), jnp.int32),
            pltpu.SemaphoreType.DMA((2, 8)),
            pltpu.SemaphoreType.DMA((2, 8)),
        ],
        compiler_params=pltpu.CompilerParams(
            collective_id=2, has_side_effects=True, vmem_limit_bytes=VMEM
        ),
        name="frame",
    )(*args)


def run_pool(shape, per_slab, cells, *args):
    vmem = specs()[1]
    entries = 3 * per_slab
    return pl.pallas_call(
        functools.partial(pool_kernel, shape, per_slab, cells),
        in_specs=[vmem] * 3,
        out_specs=vmem,
        out_shape=jax.ShapeDtypeStruct((entries, 128), f32),
        scratch_shapes=[
            pltpu.VMEM((entries, 128), f32),
            pltpu.VMEM((len(NEAR), entries, 128), f32),
            pltpu.SemaphoreType.DMA((len(NEAR),)),
            pltpu.SemaphoreType.DMA((len(NEAR),)),
        ],
        compiler_params=pltpu.CompilerParams(collective_id=1, has_side_effects=True),
        name="pool",
    )(*args)


def frame_constants(tile_c):
    move = np.zeros((tile_c, STRIDE), np.float32)
    move[np.arange(tile_c), HALO + np.arange(tile_c)] = 1
    ends = np.zeros((8, tile_c), np.float32)
    back = np.zeros((272, STRIDE), np.float32)
    for x in range(HALO):
        ends[x, x] = 1
        ends[HALO + x, tile_c - HALO + x] = 1
        back[128 - HALO + x, x] = 1
        back[128 + x, HALO + tile_c + x] = 1
        back[256 + HALO + x, x] = 1
        back[264 + x, HALO + tile_c + x] = 1
    return tuple(jnp.asarray(a, bf16) for a in (move, ends, back))


def body(
    coarse, latent, noise_level, reg_first, reg_second, den_first, den_middle, den_pool, den_last,
    anchors, patch_count, patch_weight,
):
    tile_r, tile_c = latent.shape[1:]
    patch = patch_weight.shape[0]
    rows = tile_r + 2 * TOP
    slab = lax.axis_index("slab")
    column = lax.axis_index("patch")
    shape = (lax.axis_size("slab"), lax.axis_size("patch"))
    per_slab = anchors.shape[1]

    labels = np.arange(per_slab, dtype=np.int32)
    table = jnp.stack(
        [anchors[0, :, 0], anchors[0, :, 1], jnp.broadcast_to(patch_count, (per_slab,)), labels], 0
    )
    table = jnp.pad(jnp.tile(table, (1, 3)), ((0, 4), (0, 128 - 3 * per_slab)))
    coarse_flat, latent_flat, tabs = run_frame(
        shape, per_slab, patch, latent.shape,
        noise_level, coarse, latent, table, *frame_constants(tile_c),
    )

    top = TOP - slab * tile_r
    left = HALO - column * tile_c
    meta = jnp.stack([top, top + shape[0] * tile_r, left, left + shape[1] * tile_c])
    fixed = (rows, patch, tile_r, tile_c)
    first, mean, part, ring, strips, order = run_regress(
        fixed, 3 * per_slab,
        meta.astype(jnp.int32), tabs, coarse_flat, latent_flat, tabs,
        jnp.transpose(reg_first, (0, 2, 1)), reg_second, jnp.transpose(den_first, (0, 2, 1)),
    )

    lift = run_pool(shape, per_slab, patch * patch, part, ring, den_pool)

    weight = jnp.pad(patch_weight, ((0, 0), (0, STRIDE - patch)))
    weight = weight.reshape(patch // PLANES, PLANES, STRIDE).transpose(1, 0, 2)
    weight = weight.reshape(PLANES, patch // PLANES * STRIDE)
    end = -weight.shape[1] % 128
    weight = jnp.pad(weight, ((0, 0), (WFRONT, end + WFRONT)))
    weight = weight.reshape(PLANES, -1, 128).transpose(1, 0, 2)
    next_state, estimate = run_patches(
        fixed,
        order, tabs, noise_level, first, strips, lift, weight, mean, latent, den_middle, den_last,
    )
    return (next_state, estimate)


def solution(mesh):
    return jax.shard_map(
        body,
        mesh=mesh,
        in_specs=(
            P(None, "slab", "patch"), P(None, "slab", "patch"),
            P(), P(), P(), P(), P(), P(), P(),
            P("slab", None, None), P("slab"), P(),
        ),
        out_specs=(P(None, "slab", "patch"), P(None, "slab", "patch")),
        check_vma=False,
    )
```
